32 devices in a mesh: band: 8 (over y, x, core), row: 4 (over z).
Axes of the slice: x: 2, y: 2, z: 4, core: 2. Of those that a mesh axis runs over, the one named last changes fastest.
Arguments:
- grid_input: float32 [7680, 227], P('band'), may hold values from -6 to 6
- grid_target: float32 [7680, 227], P('band'), may hold values from -6 to 6
- edge_input: float32 [10240, 4], P('band'), may hold values from -6 to 6
- senders: int32 [10240], P('band'), may hold values from 0 to 831
- receivers: int32 [10240], P('band'), may hold values from 0 to 319
- border_nodes: int32 [512], P('band'), may hold values from 0 to 319
- grid_to_mesh: int32 [7680], P('band'), may hold values from 0 to 319, as said below
- mesh_to_grid: int32 [23040], P('band'), may hold values from 0 to 831
- loss_mask: int32 [7680], P('band'), may hold values from 0 to 1
- encoder_weights: float32 [231, 512], replicated, may hold values from -0.375 to 0.375
- encoder_first: float32 [231, 512], replicated, may hold values from -0.0546875 to 0.0546875
- encoder_second: float32 [231, 512], replicated, may hold values from 5.859375e-05 to 0.000234375
- processor_weights: float32 [3, 7, 512, 512], P(None, None, 'row'), may hold values from -0.25 to 0.25
- processor_momentum: float32 [3, 7, 512, 512], P(None, None, 'row'), may hold values from -0.4107919 to 0.4107919
- processor_average: float32 [3, 7, 512, 512], P(None, None, 'row'), may hold values from -0.25 to 0.25
- norm_params: float32 [3, 8, 512], replicated, may hold values from -4 to 4
- norm_first: float32 [3, 8, 512], replicated, may hold values from -0.0546875 to 0.0546875
- norm_second: float32 [3, 8, 512], replicated, may hold values from 5.859375e-05 to 0.000234375
- decoder_weights: float32 [512, 227], replicated, may hold values from -0.25 to 0.25
- decoder_first: float32 [512, 227], replicated, may hold values from -0.0546875 to 0.0546875
- decoder_second: float32 [512, 227], replicated, may hold values from 5.859375e-05 to 0.000234375
Outputs:
- loss_total: float32 [], replicated
- mask_count: float32 [], replicated
- next_weights: float32 [3, 7, 512, 512], P(None, None, 'row')
- next_momentum: float32 [3, 7, 512, 512], P(None, None, 'row')
- next_average: float32 [3, 7, 512, 512], P(None, None, 'row')
- param_moment: float32 [3, 8, 512], replicated
- param_square: float32 [3, 8, 512], replicated
- param_values: float32 [3, 8, 512], replicated
- encoder_moment: float32 [231, 512], replicated
- encoder_square: float32 [231, 512], replicated
- encoder_values: float32 [231, 512], replicated
- decoder_moment: float32 [512, 227], replicated
- decoder_square: float32 [512, 227], replicated
- decoder_values: float32 [512, 227], replicated
The draws below stay inside these ranges and needn't reach their ends.
Inputs may be any that keep to these rules, and one draw needn't show every extreme that they name: `grid_to_mesh`: every mesh node of a band is named by some grid point of that band.
All inputs are finite; a program needn't handle non-finite values.
Results may differ from the reference program's by a relative error of at most 0.0003.
Values sent between devices are 32-bit elements; how exact they have to be, the bound alone decides.
A program may use at most 256 MiB of HBM per device.

```python
import math
import jax
import jax.numpy as jnp
from jax import lax

D = 512
CH = 227
LAYERS = 3
NS_ITERS = 2
STEP = 10
NODE_DEV = 320
EDGE_DEV = 1280
GRID_DEV = 960
BORDER = 64
EDGES = 10240
GRID = 7680
READS = 23040
N_BAND = 8


def draw_grid_to_mesh(key, part):
    key = jax.random.fold_in(key, 11)
    places = jnp.arange(N_BAND * GRID_DEV, dtype=jnp.int32) % GRID_DEV
    random_nodes = jax.random.randint(key, (N_BAND * GRID_DEV,), 0, NODE_DEV, dtype=jnp.int32)
    return jnp.where(places % 2 == 0, places // 2 % NODE_DEV, random_nodes).astype(jnp.int32)


def draw_loss_mask(key, part):
    key = jax.random.fold_in(key, 12)
    owner = jnp.arange(N_BAND * GRID_DEV, dtype=jnp.int32) // GRID_DEV
    limit = 250 + 500 * owner // max(N_BAND - 1, 1)
    picks = jax.random.randint(key, (N_BAND * GRID_DEV,), 0, 1000, dtype=jnp.int32)
    return (picks < limit).astype(jnp.int32)


def draw_processor_momentum(key, part):
    key = jax.random.fold_in(key, 13)
    shape = (LAYERS, 7, D, D)
    scale = 3.0 / (N_BAND * GRID_DEV) ** 0.5
    places = jnp.arange(D, dtype=jnp.float32) / max(D - 1, 1)
    base = jnp.clip(jax.random.normal(key, shape, jnp.float32), -4.0, 4.0)
    rising = 1.0 + 2.0 * places
    return base * scale * rising[None, None, :, None]


def touch_ends(entries, rng, smallest, largest):
    longest = entries.shape.index(max(entries.shape))
    spots = []
    for shift in (0, 1):
        where = [jax.random.randint(jax.random.fold_in(rng, axis), (), 0, length) for axis, length in enumerate(entries.shape)]
        where[longest] = (where[longest] + shift) % entries.shape[longest]
        spots.append(tuple(where))
    return entries.at[spots[0]].set(smallest).at[spots[1]].set(largest)


def steps_of(rng, shape, split, smallest, top_value):
    level = 1.0
    for position, shards_of in split:
        draws = jax.random.uniform(jax.random.fold_in(jax.random.fold_in(rng, 6), position), (shards_of,), jnp.float32, smallest / len(split), top_value / len(split))
        level = level * jnp.repeat(jnp.exp(draws), shape[position] // shards_of).reshape((-1,) + (1,) * (len(shape) - 1 - position))
    return level


def noise(own_key, extent, width, most, pieces=(), kind=jnp.bfloat16):
    factor_of = steps_of(own_key, extent, pieces, -0.22, 0.18) if pieces else 1.0
    drawn = jax.random.normal(own_key, extent, jnp.float32) * width * factor_of
    return jnp.minimum(jnp.maximum(drawn, -most), most).astype(kind)


def setup_inputs(seed: int = 0) -> dict:
    key_of = jax.random.split(jax.random.key(seed), 22)
    return {
        "grid_input": noise(key_of[0], (GRID, CH), 1.0, 6.0, ((0, 8),), jnp.float32),
        "grid_target": noise(key_of[1], (GRID, CH), 1.0, 6.0, ((0, 8),), jnp.float32),
        "edge_input": noise(key_of[2], (EDGES, 4), 1.0, 6.0, ((0, 8),), jnp.float32),
        "senders": touch_ends(jax.random.randint(key_of[3], (EDGES,), 0, NODE_DEV + N_BAND * BORDER), jax.random.fold_in(key_of[3], 1), 0, (NODE_DEV + N_BAND * BORDER) - 1).astype(jnp.int32),
        "receivers": touch_ends(jax.random.randint(key_of[4], (EDGES,), 0, NODE_DEV), jax.random.fold_in(key_of[4], 1), 0, NODE_DEV - 1).astype(jnp.int32),
        "border_nodes": touch_ends(jax.random.randint(key_of[5], (N_BAND * BORDER,), 0, NODE_DEV), jax.random.fold_in(key_of[5], 1), 0, NODE_DEV - 1).astype(jnp.int32),
        "grid_to_mesh": draw_grid_to_mesh(jax.random.fold_in(key_of[21], 71), 0),
        "mesh_to_grid": touch_ends(jax.random.randint(key_of[7], (READS,), 0, NODE_DEV + N_BAND * BORDER), jax.random.fold_in(key_of[7], 1), 0, (NODE_DEV + N_BAND * BORDER) - 1).astype(jnp.int32),
        "loss_mask": draw_loss_mask(jax.random.fold_in(key_of[21], 71), 0),
        "encoder_weights": noise(key_of[9], (CH + 4, D), CH ** -0.5, 0.375, (), jnp.float32),
        "encoder_first": noise(key_of[10], (CH + 4, D), (0.33 / (N_BAND * GRID_DEV) ** 0.5), 0.0546875, (), jnp.float32),
        "encoder_second": jnp.clip(jnp.exp(jax.random.uniform(key_of[11], (CH + 4, D), jnp.float32, math.log(5.859374869032763e-05), math.log(0.000234375))), 5.859374869032763e-05, 0.000234375),
        "processor_weights": noise(key_of[12], (LAYERS, 7, D, D), D ** -0.5, 0.25, ((2, 4),), jnp.float32),
        "processor_momentum": draw_processor_momentum(jax.random.fold_in(key_of[21], 71), 0),
        "processor_average": noise(key_of[14], (LAYERS, 7, D, D), D ** -0.5, 0.25, ((2, 4),), jnp.float32),
        "norm_params": noise(key_of[15], (LAYERS, 8, D), 0.3, 4.0, (), jnp.float32),
        "norm_first": noise(key_of[16], (LAYERS, 8, D), (0.33 / (N_BAND * GRID_DEV) ** 0.5), 0.0546875, (), jnp.float32),
        "norm_second": jnp.clip(jnp.exp(jax.random.uniform(key_of[17], (LAYERS, 8, D), jnp.float32, math.log(5.859374869032763e-05), math.log(0.000234375))), 5.859374869032763e-05, 0.000234375),
        "decoder_weights": noise(key_of[18], (D, CH), D ** -0.5, 0.25, (), jnp.float32),
        "decoder_first": noise(key_of[19], (D, CH), (0.33 / (N_BAND * GRID_DEV) ** 0.5), 0.0546875, (), jnp.float32),
        "decoder_second": jnp.clip(jnp.exp(jax.random.uniform(key_of[20], (D, CH), jnp.float32, math.log(5.859374869032763e-05), math.log(0.000234375))), 5.859374869032763e-05, 0.000234375),
    }


@jax.custom_vjp
def low(v):
    return lax.optimization_barrier(v.astype(jnp.bfloat16)).astype(jnp.float32)

@jax.custom_vjp
def low_back(v):
    return v

def low_keep(v):
    return (low(v), None)

def low_pass(kept, grad):
    return (grad,)

def back_keep(v):
    return (v, None)

def back_low(kept, grad):
    return (low(grad),)
low.defvjp(low_keep, low_pass)
low_back.defvjp(back_keep, back_low)
highest = lax.Precision.HIGHEST
coef_a = 3.4445
coef_b = -4.775
coef_c = 2.0315
momentum_decay = 0.95
muon_rate = 0.3
adam_rate = 0.02
param_rate = 0.1
beta_one = 0.9
beta_two = 0.95
adam_eps = 1e-08
weight_decay = 0.01
average_decay = 0.9
block_group = (0, 0, 0, 1, 2, 2, 3)
block_scale = (3.0 ** 0.5, 3.0 ** 0.5, 3.0 ** 0.5, 1.0, 2.0 ** 0.5, 2.0 ** 0.5, 1.0)

def matmul(left, right):
    return jnp.dot(left, right, precision=highest)

def silu(value):
    return value * jax.nn.sigmoid(value)

def layer_norm(value):
    centered = value - lax.optimization_barrier(jnp.mean(value, axis=-1, keepdims=True))
    return centered * lax.rsqrt(lax.optimization_barrier(jnp.mean(centered * centered, axis=-1, keepdims=True)) + 1e-05)

def encode(grid_input, edge_input, mesh_index, encoder_weights, node_count):
    channels = grid_input.shape[1]
    embedded = silu(matmul(grid_input, encoder_weights[:channels]))
    node_lat = layer_norm(jax.ops.segment_sum(embedded, mesh_index, num_segments=node_count))
    edge_lat = silu(matmul(edge_input, encoder_weights[channels:]))
    return (node_lat, edge_lat)

def processor(node_lat, edge_lat, send_lat, recv_index, weights, params):
    recv_lat = node_lat[recv_index]
    before = matmul(edge_lat, weights[0]) + matmul(send_lat, weights[1]) + matmul(recv_lat, weights[2]) + params[0]
    message = matmul(silu(before), weights[3]) + params[1]
    edge_lat = edge_lat + layer_norm(message) * (1.0 + params[2]) + params[3]
    summed = jax.ops.segment_sum(edge_lat, recv_index, num_segments=node_lat.shape[0])
    before = matmul(node_lat, weights[4]) + matmul(summed, weights[5]) + params[4]
    update = matmul(silu(before), weights[6]) + params[5]
    node_lat = node_lat + layer_norm(update) * (1.0 + params[6]) + params[7]
    return (node_lat, edge_lat)

def decode(read_lat, grid_input, grid_target, loss_mask, decoder_weights):
    gathered = lax.optimization_barrier(jnp.sum(read_lat.reshape(-1, 3, read_lat.shape[1]), axis=1))
    predicted = grid_input + matmul(silu(gathered), decoder_weights)
    missed = predicted - grid_target
    return jnp.sum(loss_mask.astype(jnp.float32)[:, None] * missed * missed)

def group_sum(values):
    return jnp.stack([values[:, 0] + values[:, 1] + values[:, 2], values[:, 3], values[:, 4] + values[:, 5], values[:, 6]], axis=1)

def spread(values):
    return jnp.take(values, jnp.array(block_group, dtype=jnp.int32), axis=1)

def orthogonalize(momentum, total_norm, total_gram):
    squares = total_norm(group_sum(lax.optimization_barrier(jnp.sum(momentum * momentum, axis=(2, 3)))))
    iterate = momentum / (jnp.sqrt(spread(squares)) + 1e-07)[:, :, None, None]
    for sweep in range(NS_ITERS):
        gram = total_gram(group_sum(jnp.einsum('lbrd,lbre->lbde', iterate, iterate, precision=highest)))
        polynom = coef_b * gram + coef_c * jnp.einsum('lgde,lgef->lgdf', gram, gram, precision=highest)
        iterate = coef_a * iterate + jnp.einsum('lbrd,lbde->lbre', iterate, spread(polynom), precision=highest)
    return iterate

def muon_finish(weights, ortho):
    scales = jnp.array(block_scale, dtype=weights.dtype)[None, :, None, None]
    return weights * (1.0 - muon_rate * weight_decay) - muon_rate * scales * ortho

def adam_update(values, first, second, gradient, rate):
    first = beta_one * first + (1.0 - beta_one) * gradient
    second = beta_two * second + (1.0 - beta_two) * gradient * gradient
    corrected = first / (1.0 - beta_one ** STEP) / (jnp.sqrt(second / (1.0 - beta_two ** STEP)) + adam_eps)
    return (first, second, values * (1.0 - rate * weight_decay) - rate * corrected)

def unchanged(value):
    return value

def global_index(local, owner, border_nodes):
    remote = jnp.maximum(local - NODE_DEV, 0)
    band_of = remote // BORDER
    listed = border_nodes[band_of * BORDER + remote % BORDER]
    return jnp.where(local < NODE_DEV, owner * NODE_DEV + local, band_of * NODE_DEV + listed).astype(jnp.int32)

def reference(grid_input, grid_target, edge_input, senders, receivers, border_nodes, grid_to_mesh, mesh_to_grid, loss_mask, encoder_weights, encoder_first, encoder_second, processor_weights, processor_momentum, processor_average, norm_params, norm_first, norm_second, decoder_weights, decoder_first, decoder_second):
    node_count = NODE_DEV * N_BAND
    edge_owner = (jnp.arange(senders.shape[0]) // EDGE_DEV).astype(jnp.int32)
    send_index = global_index(senders, edge_owner, border_nodes)
    recv_index = (edge_owner * NODE_DEV + receivers).astype(jnp.int32)
    grid_owner = (jnp.arange(grid_to_mesh.shape[0]) // GRID_DEV).astype(jnp.int32)
    mesh_index = (grid_owner * NODE_DEV + grid_to_mesh).astype(jnp.int32)
    read_owner = (jnp.arange(mesh_to_grid.shape[0]) // (3 * GRID_DEV)).astype(jnp.int32)
    read_index = global_index(mesh_to_grid, read_owner, border_nodes)
    mask_count = jnp.sum(loss_mask.astype(jnp.float32))

    def loss_of(encoder_now, weights_now, params_now, decoder_now):
        node_lat, edge_lat = encode(grid_input, edge_input, mesh_index, encoder_now, node_count)
        for depth in range(LAYERS):
            node_lat, edge_lat = processor(node_lat, edge_lat, node_lat[send_index], recv_index, weights_now[depth], params_now[depth])
        return decode(node_lat[read_index], grid_input, grid_target, loss_mask, decoder_now)
    loss_total, backward = jax.vjp(loss_of, encoder_weights, processor_weights, norm_params, decoder_weights)
    encoder_grad, weight_grad, param_grad, decoder_grad = backward(1.0 / mask_count)
    next_momentum = momentum_decay * processor_momentum + weight_grad
    next_weights = muon_finish(processor_weights, orthogonalize(next_momentum, unchanged, unchanged))
    next_average = average_decay * processor_average + (1.0 - average_decay) * next_weights
    param_moment, param_square, param_values = adam_update(norm_params, norm_first, norm_second, param_grad, param_rate)
    encoder_moment, encoder_square, encoder_values = adam_update(encoder_weights, encoder_first, encoder_second, encoder_grad, adam_rate)
    decoder_moment, decoder_square, decoder_values = adam_update(decoder_weights, decoder_first, decoder_second, decoder_grad, adam_rate)
    return (loss_total, mask_count, next_weights, next_momentum, next_average, param_moment, param_square, param_values, encoder_moment, encoder_square, encoder_values, decoder_moment, decoder_square, decoder_values)
```

```python
import functools

import jax
import jax.numpy as jnp
from jax import lax
from jax.experimental import pallas as pl
from jax.experimental.pallas import tpu as pltpu
from jax.sharding import PartitionSpec as P

LAYERS = 3
STEP = 10
NODE_DEV = 320


highest = lax.Precision.HIGHEST
coef_a = 3.4445
coef_b = -4.775
coef_c = 2.0315
momentum_decay = 0.95
muon_rate = 0.3
adam_rate = 0.02
param_rate = 0.1
beta_one = 0.9
beta_two = 0.95
adam_eps = 1e-08
weight_decay = 0.01
average_decay = 0.9
block_scale = (3.0**0.5, 3.0**0.5, 3.0**0.5, 1.0, 2.0**0.5, 2.0**0.5, 1.0)


def matmul(left, right):
    return jnp.dot(left, right, precision=highest)


def silu(value):
    return value * jax.nn.sigmoid(value)


def layer_norm(value):
    centered = value - jnp.mean(value, axis=-1, keepdims=True)
    return centered * lax.rsqrt(jnp.mean(centered * centered, axis=-1, keepdims=True) + 1e-05)


def encode(grid_input, edge_input, mesh_index, encoder_weights, node_count):
    channels = grid_input.shape[1]
    embedded = silu(matmul(grid_input, encoder_weights[:channels]))
    node_lat = layer_norm(jax.ops.segment_sum(embedded, mesh_index, num_segments=node_count))
    edge_lat = silu(matmul(edge_input, encoder_weights[channels:]))
    return (node_lat, edge_lat)


def processor(node_lat, edge_lat, send_lat, recv_index, weights, params):
    recv_lat = node_lat[recv_index]
    before = (
        matmul(edge_lat, weights[0])
        + matmul(send_lat, weights[1])
        + matmul(recv_lat, weights[2])
        + params[0]
    )
    message = matmul(silu(before), weights[3]) + params[1]
    edge_lat = edge_lat + layer_norm(message) * (1.0 + params[2]) + params[3]
    summed = jax.ops.segment_sum(edge_lat, recv_index, num_segments=node_lat.shape[0])
    before = matmul(node_lat, weights[4]) + matmul(summed, weights[5]) + params[4]
    update = matmul(silu(before), weights[6]) + params[5]
    node_lat = node_lat + layer_norm(update) * (1.0 + params[6]) + params[7]
    return (node_lat, edge_lat)


def decode(read_lat, grid_input, grid_target, loss_mask, decoder_weights):
    gathered = jnp.sum(read_lat.reshape(-1, 3, read_lat.shape[1]), axis=1)
    predicted = grid_input + matmul(silu(gathered), decoder_weights)
    missed = predicted - grid_target
    return jnp.sum(loss_mask.astype(jnp.float32)[:, None] * missed * missed)


MESH = pl.DeviceIdType.MESH
NN = (((1,), (0,)), ((), ()))
NT = (((1,), (1,)), ((), ()))
TN = (((0,), (0,)), ((), ()))
OWNER_CHIPS = 4
SLOTS = 3
ANY = pl.BlockSpec(memory_space=pl.ANY)
VMEM = pl.BlockSpec(memory_space=pltpu.VMEM)


def pieces(value):
    high = value.astype(jnp.bfloat16)
    return high, (value - high.astype(jnp.float32)).astype(jnp.bfloat16)


def dot(left, right, dims=NN):
    return lax.dot_general(left, right, dims, preferred_element_type=jnp.float32)


def product(left, right, dims=NN):
    left_high, left_low = pieces(left)
    right_high, right_low = pieces(right)
    return (
        dot(left_high, right_high, dims)
        + dot(left_low, right_high, dims)
        + dot(left_high, right_low, dims)
    )


def slot_block(owner, slot):
    third = owner // 3
    last = third // 2
    return (1 - last) * (7 * (owner % 3) + 4 * third + slot) + last * (
        3 + 14 * (owner - 6) + 7 * slot
    )


def slot_used(owner, slot):
    return owner < (8, 7, 6)[slot]


def spread_slots(blocks, rows_dev, width):
    empty = jnp.zeros((rows_dev, width), jnp.float32)
    order = []
    for core in range(2):
        for chip in range(OWNER_CHIPS):
            owner = 2 * chip + core
            for slot in range(SLOTS):
                order.append(blocks[slot_block(owner, slot)] if slot_used(owner, slot) else empty)
    return jnp.stack(order).reshape(2, OWNER_CHIPS, SLOTS, rows_dev, width)


def remote(src, dst, send_sem, recv_sem, device):
    return pltpu.make_async_remote_copy(
        src_ref=src,
        dst_ref=dst,
        send_sem=send_sem,
        recv_sem=recv_sem,
        device_id=device,
        device_id_type=MESH,
    )


def newton(mom_ref, out_ref, first, count, gram, poly, temp, later):
    def add_square(i, total):
        block = mom_ref[first + i]
        return total + jnp.sum(jnp.sum(block * block, axis=0, keepdims=True), axis=1, keepdims=True)

    total = lax.fori_loop(0, count, add_square, jnp.zeros((1, 1), jnp.float32))
    scale = 1.0 / (jnp.sqrt(total) + 1e-07)
    gram[...] = jnp.zeros_like(gram)

    def add_gram(i, carry):
        block = mom_ref[first + i] * scale
        mom_ref[first + i] = block
        gram[...] += product(block, block, TN)
        return carry

    lax.fori_loop(0, count, add_gram, 0)
    poly[...] = coef_b * gram[...] + coef_c * product(gram[...], gram[...])
    temp[...] = coef_a * gram[...] + product(gram[...], poly[...])
    gram[...] = coef_a * temp[...] + product(temp[...], poly[...])
    later[...] = coef_b * gram[...] + coef_c * product(gram[...], gram[...])
    temp[...] = coef_a * (poly[...] + later[...]) + product(poly[...], later[...])

    def finish(i, carry):
        block = mom_ref[first + i]
        out_ref[first + i] = (coef_a * coef_a) * block + product(block, temp[...])
        return carry

    lax.fori_loop(0, count, finish, 0)


def tail_kernel(
    bands,
    rows,
    grad_ref,
    small_ref,
    mom_ref,
    total_ref,
    ortho_ref,
    shared_ref,
    sib_grad,
    sib_small,
    part,
    part_small,
    land,
    land_small,
    mine,
    mine_small,
    held,
    matrix,
    result,
    back,
    gram,
    poly,
    temp,
    later,
    load_sem,
    sib_send,
    sib_recv,
    red_send,
    red_recv,
    all_send,
    all_recv,
    pass_send,
    pass_recv,
    up_send,
    up_recv,
    down_send,
    down_recv,
    keep_sem,
):
    chips = bands // 2
    band = lax.axis_index("band")
    row = lax.axis_index("row")
    chip, core = band // 2, band % 2
    sibling = (chip * 2 + 1 - core, row)
    rows_dev = held.shape[1]
    everyone = chips == OWNER_CHIPS

    def guard(cond, body):
        if cond is True:
            body()
        else:
            pl.when(cond)(body)

    def owns(at_chip):
        return True if everyone else at_chip < OWNER_CHIPS

    def both(one, two):
        if one is True:
            return two
        if two is True:
            return one
        return jnp.logical_and(one, two)

    def used(at_chip, slot):
        owner = at_chip * 2 + core
        return both(owns(at_chip), True if slot in (0, 3) else slot_used(owner, slot))

    barrier = pltpu.get_barrier_semaphore()
    partners = [((chip + j) % chips * 2 + core, row) for j in range(1, chips)] + [sibling]
    partners += [(band, (row + j) % rows) for j in range(1, rows)]
    for partner in partners:
        pl.semaphore_signal(barrier, inc=1, device_id=partner, device_id_type=MESH)
    pl.semaphore_wait(barrier, len(partners))

    first = remote(grad_ref.at[1 - core], sib_grad, sib_send.at[0], sib_recv.at[0], sibling)
    second = remote(small_ref.at[1 - core], sib_small, sib_send.at[1], sib_recv.at[1], sibling)
    first.start()
    second.start()
    owner = band

    def load(slot):
        return pltpu.make_async_copy(
            mom_ref.at[slot_block(owner, slot)], held.at[slot], load_sem.at[slot]
        )

    for slot in range(SLOTS):
        guard(used(chip, slot), lambda slot=slot: load(slot).start())
    first.wait()
    second.wait()
    for at in range(OWNER_CHIPS):
        part[at] = grad_ref[core, at] + sib_grad[at]
    part_small[...] = small_ref[core] + sib_small[...]

    def to_owner(j):
        to = (chip + j) % chips
        return (
            remote(part.at[to], land.at[j - 1], red_send.at[j - 1, 0], red_recv.at[j - 1, 0], (to * 2 + core, row)),
            remote(part_small.at[to], land_small.at[j - 1], red_send.at[j - 1, 1], red_recv.at[j - 1, 1], (to * 2 + core, row)),
        )

    for j in range(1, chips):
        def send(j=j):
            for copy in to_owner(j):
                copy.start()

        guard(owns((chip + j) % chips), send)

    def reduce():
        mine[...] = part[chip]
        mine_small[...] = part_small[chip]
        for j in range(1, chips):
            for copy in to_owner(j):
                copy.wait_recv()
            mine[...] += land[j - 1]
            mine_small[...] += land_small[j - 1]

    guard(owns(chip), reduce)

    def source(kind, slot):
        if slot == 3:
            return mine_small
        return (mine, back)[kind].at[slot]

    def target(kind, slot, at_chip, at_core):
        at_owner = at_chip * 2 + at_core
        if slot == 3:
            return shared_ref.at[at_owner]
        return (total_ref, ortho_ref)[kind].at[slot_block(at_owner, slot)]

    def keep(kind, slot):
        return pltpu.make_async_copy(
            source(kind, slot), target(kind, slot, chip, core), keep_sem.at[kind, slot]
        )

    def out(kind, slot, j):
        return remote(
            source(kind, slot),
            target(kind, slot, chip, core),
            all_send.at[kind, j - 1, slot],
            all_recv.at[kind, j - 1, slot],
            ((chip + j) % chips * 2 + core, row),
        )

    def across(kind, slot, at_chip, j):
        src = source(kind, slot) if j == 0 else target(kind, slot, at_chip, core)
        return remote(
            src,
            target(kind, slot, at_chip, core),
            pass_send.at[kind, j, slot],
            pass_recv.at[kind, j, slot],
            sibling,
        )

    def crossed(kind, slot, at_chip, j):
        return remote(
            source(kind, slot),
            target(kind, slot, at_chip, 1 - core),
            pass_send.at[kind, j, slot],
            pass_recv.at[kind, j, slot],
            sibling,
        )

    def used_other(at_chip, slot):
        at_owner = at_chip * 2 + 1 - core
        return both(owns(at_chip), True if slot in (0, 3) else slot_used(at_owner, slot))

    def publish(kind, slots):
        for slot in slots:
            def start(slot=slot):
                for j in range(1, chips):
                    out(kind, slot, j).start()
                keep(kind, slot).start()
                across(kind, slot, chip, 0).start()

            guard(used(chip, slot), start)

    def relay(kind, slots):
        for j in range(1, chips):
            origin = (chip - j + chips) % chips
            for slot in slots:
                def start(slot=slot, j=j, origin=origin):
                    remote(
                        source(kind, slot),
                        target(kind, slot, origin, core),
                        all_send.at[kind, j - 1, slot],
                        all_recv.at[kind, j - 1, slot],
                        (origin * 2 + core, row),
                    ).wait_recv()
                    across(kind, slot, origin, j).start()

                guard(used(origin, slot), start)

    def settle(kind, slots):
        for j in range(chips):
            origin = (chip - j + chips) % chips
            for slot in slots:
                def finish(slot=slot, j=j, origin=origin):
                    across(kind, slot, origin, j).wait_send()

                def arrive(slot=slot, j=j, origin=origin):
                    crossed(kind, slot, origin, j).wait_recv()

                guard(used(origin, slot), finish)
                guard(used_other(origin, slot), arrive)
        for slot in slots:
            def sent(slot=slot):
                for j in range(1, chips):
                    out(kind, slot, j).wait_send()
                keep(kind, slot).wait()

            guard(used(chip, slot), sent)

    third = owner // 3
    row_a = rows // 2 - 1 + core
    row_b = rows // 2 - core
    split_at = 3 - third

    def home(slot):
        if slot == 0:
            return row_a
        late = (slot + third) // 3
        return row_a + late * (row_b - row_a)

    def up(slot, from_row):
        at = pl.ds(pl.multiple_of(from_row * rows_dev, rows_dev), rows_dev)
        step = (from_row - home(slot) + rows) % rows
        return remote(
            held.at[slot],
            matrix.at[slot, at],
            up_send.at[slot],
            up_recv.at[slot, step],
            (band, home(slot)),
        )

    for slot in range(SLOTS):
        def momentum(slot=slot):
            load(slot).wait()
            held[slot] = momentum_decay * held[slot] + mine[slot]

            @pl.when(row == home(slot))
            def _():
                at = pl.ds(pl.multiple_of(row * rows_dev, rows_dev), rows_dev)
                matrix[slot, at] = held[slot]

            @pl.when(row != home(slot))
            def _():
                up(slot, row).start()

        guard(used(chip, slot), momentum)
    publish(0, (0, 1, 2, 3))

    def down(slot, to_row):
        at = pl.ds(pl.multiple_of(to_row * rows_dev, rows_dev), rows_dev)
        step = (to_row - home(slot) + rows) % rows
        return remote(
            result.at[slot, at],
            back.at[slot],
            down_send.at[slot, step],
            down_recv.at[slot],
            (band, to_row),
        )

    for slot in range(SLOTS):
        def arrived(slot=slot):
            @pl.when(row == home(slot))
            def _():
                for step in range(1, rows):
                    up(slot, (row + step) % rows).wait_recv()

        guard(used(chip, slot), arrived)

    def at_a():
        newton(matrix, result, 0, split_at, gram, poly, temp, later)

    def at_b():
        newton(matrix, result, split_at, 1, gram, poly, temp, later)

    guard(both(owns(chip), row == row_a), at_a)
    guard(
        both(owns(chip), jnp.logical_and(row == row_b, jnp.logical_and(owner > 2, owner < 7))), at_b
    )

    for slot in range(SLOTS):
        def give(slot=slot):
            @pl.when(row == home(slot))
            def _():
                for step in range(1, rows):
                    down(slot, (row + step) % rows).start()
                at = pl.ds(pl.multiple_of(row * rows_dev, rows_dev), rows_dev)
                back[slot] = result[slot, at]

        guard(used(chip, slot), give)
    relay(0, (0, 1, 2, 3))
    for slot in range(SLOTS):
        def take(slot=slot):
            @pl.when(row != home(slot))
            def _():
                down(slot, row).wait_recv()

        guard(used(chip, slot), take)
    publish(1, (0, 1, 2))
    relay(1, (0, 1, 2))
    settle(0, (0, 1, 2, 3))
    settle(1, (0, 1, 2))
    for j in range(1, chips):
        def reduced(j=j):
            for copy in to_owner(j):
                copy.wait_send()

        guard(owns((chip + j) % chips), reduced)
    for slot in range(SLOTS):
        def closed(slot=slot):
            @pl.when(row != home(slot))
            def _():
                up(slot, row).wait_send()

            @pl.when(row == home(slot))
            def _():
                for step in range(1, rows):
                    down(slot, (row + step) % rows).wait_send()

        guard(used(chip, slot), closed)


def tail(bands, rows, grads, small, momentum):
    blocks, rows_dev, width = momentum.shape
    chips = bands // 2
    chunk = small.shape[2]
    f32 = jnp.float32
    dma = pltpu.SemaphoreType.DMA
    square = pltpu.VMEM((width, width), f32)
    return pl.pallas_call(
        functools.partial(tail_kernel, bands, rows),
        out_shape=(
            jax.ShapeDtypeStruct((blocks, rows_dev, width), f32),
            jax.ShapeDtypeStruct((blocks, rows_dev, width), f32),
            jax.ShapeDtypeStruct((2 * OWNER_CHIPS, chunk, width), f32),
        ),
        in_specs=[VMEM, VMEM, ANY],
        out_specs=[ANY, ANY, ANY],
        scratch_shapes=[
            pltpu.VMEM((OWNER_CHIPS, SLOTS, rows_dev, width), f32),
            pltpu.VMEM((OWNER_CHIPS, chunk, width), f32),
            pltpu.VMEM((OWNER_CHIPS, SLOTS, rows_dev, width), f32),
            pltpu.VMEM((OWNER_CHIPS, chunk, width), f32),
            pltpu.VMEM((chips - 1, SLOTS, rows_dev, width), f32),
            pltpu.VMEM((chips - 1, chunk, width), f32),
            pltpu.VMEM((SLOTS, rows_dev, width), f32),
            pltpu.VMEM((chunk, width), f32),
            pltpu.VMEM((SLOTS, rows_dev, width), f32),
            pltpu.VMEM((SLOTS, width, width), f32),
            pltpu.VMEM((SLOTS, width, width), f32),
            pltpu.VMEM((SLOTS, rows_dev, width), f32),
            square,
            square,
            square,
            square,
            dma((SLOTS,)),
            dma((2,)),
            dma((2,)),
            dma((chips - 1, 2)),
            dma((chips - 1, 2)),
            dma((2, chips - 1, SLOTS + 1)),
            dma((2, chips - 1, SLOTS + 1)),
            dma((2, chips, SLOTS + 1)),
            dma((2, chips, SLOTS + 1)),
            dma((SLOTS,)),
            dma((SLOTS, rows)),
            dma((SLOTS, rows)),
            dma((SLOTS,)),
            dma((2, SLOTS + 1)),
        ],
        compiler_params=pltpu.CompilerParams(
            collective_id=0, has_side_effects=True, vmem_limit_bytes=56 * 2**20
        ),
        name="tail",
    )(grads, small, momentum)


def muon_finish(weights, ortho):
    scales = jnp.array(block_scale, dtype=weights.dtype)[None, :, None, None]
    return weights * (1.0 - muon_rate * weight_decay) - muon_rate * scales * ortho


def adam_update(values, first, second, gradient, rate):
    first = beta_one * first + (1.0 - beta_one) * gradient
    second = beta_two * second + (1.0 - beta_two) * gradient * gradient
    corrected = (
        first / (1.0 - beta_one**STEP) / (jnp.sqrt(second / (1.0 - beta_two**STEP)) + adam_eps)
    )
    return (first, second, values * (1.0 - rate * weight_decay) - rate * corrected)


def body(
    grid_input,
    grid_target,
    edge_input,
    senders,
    receivers,
    border_nodes,
    grid_to_mesh,
    mesh_to_grid,
    loss_mask,
    encoder_weights,
    encoder_first,
    encoder_second,
    processor_weights,
    processor_momentum,
    processor_average,
    norm_params,
    norm_first,
    norm_second,
    decoder_weights,
    decoder_first,
    decoder_second,
):
    full_weights = lax.all_gather(processor_weights, "row", axis=2, tiled=True)

    def share_border(node_lat):
        return lax.all_gather(node_lat[border_nodes], "band", axis=0, tiled=True)

    def return_border(table_grad, node_grad):
        owned = lax.psum_scatter(table_grad, "band", scatter_dimension=0, tiled=True)
        return node_grad + jax.ops.segment_sum(owned, border_nodes, num_segments=NODE_DEV)

    def encode_local(encoder_now):
        return encode(grid_input, edge_input, grid_to_mesh, encoder_now, NODE_DEV)

    def layer_local(node_lat, edge_lat, table, weights, params):
        combined = jnp.concatenate([node_lat, table], axis=0)
        return processor(node_lat, edge_lat, combined[senders], receivers, weights, params)

    def decode_local(node_lat, table, decoder_now):
        combined = jnp.concatenate([node_lat, table], axis=0)
        return decode(combined[mesh_to_grid], grid_input, grid_target, loss_mask, decoder_now)

    node_lat, edge_lat = encode_local(encoder_weights)
    kept = []
    for depth in range(LAYERS):
        table = share_border(node_lat)
        kept.append((node_lat, edge_lat, table))
        node_lat, edge_lat = layer_local(
            node_lat, edge_lat, table, full_weights[depth], norm_params[depth]
        )
    table = share_border(node_lat)
    local_loss, decode_back = jax.vjp(decode_local, node_lat, table, decoder_weights)
    loss_total, mask_count = lax.psum((local_loss, jnp.sum(loss_mask.astype(jnp.float32))), "band")
    node_grad, table_grad, decoder_grad = decode_back(1.0 / mask_count)
    node_grad = return_border(table_grad, node_grad)
    edge_grad = jnp.zeros_like(edge_lat)
    weight_list = [None] * LAYERS
    param_list = [None] * LAYERS
    for depth in reversed(range(LAYERS)):
        saved_nodes, saved_edges, saved_table = kept[depth]
        outputs, layer_back = jax.vjp(
            layer_local,
            saved_nodes,
            saved_edges,
            saved_table,
            full_weights[depth],
            norm_params[depth],
        )
        node_grad, edge_grad, table_grad, weight_list[depth], param_list[depth] = layer_back(
            (node_grad, edge_grad)
        )
        node_grad = return_border(table_grad, node_grad)
    outputs, encode_back = jax.vjp(encode_local, encoder_weights)
    (encoder_grad,) = encode_back((node_grad, edge_grad))
    layers, blocks, rows_dev, width = processor_weights.shape
    row_start = lax.axis_index("row") * rows_dev
    row_grads = [
        lax.dynamic_slice_in_dim(weight_list[depth][block], row_start, rows_dev, 0)
        for depth in range(layers)
        for block in range(blocks)
    ]
    small_shapes = (encoder_weights.shape, decoder_weights.shape, norm_params.shape)
    small = jnp.concatenate(
        [encoder_grad.reshape(-1), decoder_grad.reshape(-1), jnp.stack(param_list).reshape(-1)]
    )
    chunk = -(-small.shape[0] // (2 * OWNER_CHIPS * width * 8)) * 8
    padded = jnp.pad(small, (0, 2 * OWNER_CHIPS * chunk * width - small.shape[0]))
    padded = padded.reshape(OWNER_CHIPS, 2, chunk, width).swapaxes(0, 1)
    total, ortho, small = tail(
        lax.axis_size("band"),
        lax.axis_size("row"),
        spread_slots(row_grads, rows_dev, width),
        padded,
        processor_momentum.reshape(layers * blocks, rows_dev, width),
    )
    small = small.reshape(-1)
    parts = []
    start = 0
    for shape in small_shapes:
        size = shape[0] * shape[1] * (shape[2] if len(shape) > 2 else 1)
        parts.append(small[start : start + size].reshape(shape))
        start += size
    encoder_grad, decoder_grad, param_grad = parts
    next_momentum = momentum_decay * processor_momentum + total.reshape(processor_weights.shape)
    next_weights = muon_finish(processor_weights, ortho.reshape(processor_weights.shape))
    next_average = average_decay * processor_average + (1.0 - average_decay) * next_weights
    param_moment, param_square, param_values = adam_update(
        norm_params, norm_first, norm_second, param_grad, param_rate
    )
    encoder_moment, encoder_square, encoder_values = adam_update(
        encoder_weights, encoder_first, encoder_second, encoder_grad, adam_rate
    )
    decoder_moment, decoder_square, decoder_values = adam_update(
        decoder_weights, decoder_first, decoder_second, decoder_grad, adam_rate
    )
    return (
        loss_total,
        mask_count,
        next_weights,
        next_momentum,
        next_average,
        param_moment,
        param_square,
        param_values,
        encoder_moment,
        encoder_square,
        encoder_values,
        decoder_moment,
        decoder_square,
        decoder_values,
    )


def solution(mesh):
    return jax.shard_map(
        body,
        mesh=mesh,
        in_specs=(
            P("band", None),
            P("band", None),
            P("band", None),
            P("band"),
            P("band"),
            P("band"),
            P("band"),
            P("band"),
            P("band"),
            P(),
            P(),
            P(),
            P(None, None, "row", None),
            P(None, None, "row", None),
            P(None, None, "row", None),
            P(),
            P(),
            P(),
            P(),
            P(),
            P(),
        ),
        out_specs=(
            P(),
            P(),
            P(None, None, "row", None),
            P(None, None, "row", None),
            P(None, None, "row", None),
            P(),
            P(),
            P(),
            P(),
            P(),
            P(),
            P(),
            P(),
            P(),
        ),
        check_vma=False,
    )
```

```python
import functools

import jax
import jax.numpy as jnp
from jax import lax
from jax.experimental import pallas as pl
from jax.experimental.pallas import tpu as pltpu
from jax.sharding import PartitionSpec as P

STEP = 10
NODE_DEV = 320


coef_a = 3.4445
coef_b = -4.775
coef_c = 2.0315
momentum_decay = 0.95
muon_rate = 0.3
adam_rate = 0.02
param_rate = 0.1
beta_one = 0.9
beta_two = 0.95
adam_eps = 1e-08
weight_decay = 0.01
average_decay = 0.9
block_scale = (3.0**0.5, 3.0**0.5, 3.0**0.5, 1.0, 2.0**0.5, 2.0**0.5, 1.0)


MESH = pl.DeviceIdType.MESH
NN = (((1,), (0,)), ((), ()))
NT = (((1,), (1,)), ((), ()))
TN = (((0,), (0,)), ((), ()))
OWNER_CHIPS = 4
SLOTS = 3
VMEM_BYTES = 62 * 2**20
ANY = pl.BlockSpec(memory_space=pl.ANY)
VMEM = pl.BlockSpec(memory_space=pltpu.VMEM)


def pieces(value):
    high = value.astype(jnp.bfloat16)
    return high, (value - high.astype(jnp.float32)).astype(jnp.bfloat16)


def dot(left, right, dims=NN):
    return lax.dot_general(left, right, dims, preferred_element_type=jnp.float32)


def product(left, right, dims=NN):
    left_high, left_low = pieces(left)
    right_high, right_low = pieces(right)
    return (
        dot(left_high, right_high, dims)
        + dot(left_low, right_high, dims)
        + dot(left_high, right_low, dims)
    )


def slot_block(owner, slot):
    third = owner // 3
    last = third // 2
    return (1 - last) * (7 * (owner % 3) + 4 * third + slot) + last * (
        3 + 14 * (owner - 6) + 7 * slot
    )


def slot_used(owner, slot):
    return owner < (8, 7, 6)[slot]


def remote(src, dst, send_sem, recv_sem, device):
    return pltpu.make_async_remote_copy(
        src_ref=src,
        dst_ref=dst,
        send_sem=send_sem,
        recv_sem=recv_sem,
        device_id=device,
        device_id_type=MESH,
    )


def silu(value):
    return value / (1.0 + jnp.exp(-value))


def silu_back(value):
    gate = 1.0 / (1.0 + jnp.exp(-value))
    return gate * (1.0 + value * (1.0 - gate))


def normed(value):
    centered = value - jnp.mean(value, axis=-1, keepdims=True)
    scale = lax.rsqrt(jnp.mean(centered * centered, axis=-1, keepdims=True) + 1e-05)
    return centered * scale, scale


def normed_back(grad, norm, scale):
    inner = jnp.mean(grad * norm, axis=-1, keepdims=True)
    return (grad - jnp.mean(grad, axis=-1, keepdims=True) - norm * inner) * scale


def column(value):
    return jnp.sum(value, axis=0, keepdims=True)


def hot(mask):
    return jnp.where(mask, 1.0, 0.0).astype(jnp.bfloat16)


def chosen(choice, high, low, dims=NN):
    return dot(choice, high, dims) + dot(choice, low, dims)


def picked(choice, value):
    high, low = pieces(value)
    return chosen(choice, high, low)


def fill_rows(out_ref, make, tile=128):
    def step(t, carry):
        at = pl.multiple_of(t * tile, tile)
        out_ref[pl.ds(at, tile)] = make(at, tile)
        return carry

    lax.fori_loop(0, out_ref.shape[0] // tile, step, 0)


def iota(shape, axis):
    return lax.broadcasted_iota(jnp.int32, shape, axis)


class Weights:
    def __init__(self, full_ref, stage, high, low, sem):
        self.full, self.stage, self.high, self.low, self.sem = full_ref, stage, high, low, sem

    def copy(self, block, slot):
        return pltpu.make_async_copy(self.full.at[block], self.stage.at[slot], self.sem.at[slot])

    def load(self, first, blocks):
        for n, block in enumerate(blocks[:2]):
            self.copy(first + block, n % 2).start()
        for n, block in enumerate(blocks):
            self.copy(first + block, n % 2).wait()
            high, low = pieces(self.stage[n % 2])
            self.high[block] = high
            self.low[block] = low
            if n + 2 < len(blocks):
                self.copy(first + blocks[n + 2], n % 2).start()

    def times(self, high, low, block, dims=NN):
        weight = self.high[block]
        return dot(high, weight, dims) + dot(low, weight, dims) + dot(high, self.low[block], dims)

    def apply(self, value, block, dims=NN):
        high, low = pieces(value)
        return self.times(high, low, block, dims)


def place(bands, rows):
    band = lax.axis_index("band")
    row = lax.axis_index("row")
    return band, row, band // 2, band % 2


def meet(partners):
    barrier = pltpu.get_barrier_semaphore()
    for partner in partners:
        pl.semaphore_signal(barrier, inc=1, device_id=partner, device_id_type=MESH)
    pl.semaphore_wait(barrier, len(partners))


def forward_kernel(
    bands,
    rows,
    chunks,
    tile,
    grid_ref,
    edge_ref,
    send_ref,
    recv_ref,
    recv_row_ref,
    border_ref,
    feed_ref,
    mask_ref,
    w_ref,
    enc_ref,
    enc_edge_ref,
    param_ref,
    full_ref,
    before_ref,
    message_ref,
    edges_ref,
    embed_ref,
    nodes_ref,
    fed_ref,
    agg_ref,
    inner_ref,
    update_ref,
    table_ref,
    count_ref,
    edge_buf,
    before_buf,
    message_buf,
    pick,
    gather_t,
    src_high,
    src_low,
    high,
    low,
    stage,
    table,
    border_buf,
    count_buf,
    stage_sem,
    save_sem,
    own_sem,
    z_send,
    z_recv,
    a_send,
    a_recv,
    b_send,
    b_recv,
    s_send,
    s_recv,
    x_send,
    x_recv,
    p_send,
    p_recv,
):
    band, row, chip, core = place(bands, rows)
    chips = bands // 2
    layers, blocks = agg_ref.shape[0], w_ref.shape[0] // agg_ref.shape[0]
    rows_dev = w_ref.shape[1]
    nodes, width = fed_ref.shape
    edges = edge_buf.shape[1]
    border = border_ref.shape[0]
    weights = Weights(full_ref, stage, high, low, stage_sem)
    quad, pos = chip // 4, chip % 4
    pos_x, pos_y = pos + 1 - 2 * (pos % 2), pos + 2 - 4 * (pos // 2)
    sibling = (chip * 2 + 1 - core, row)
    near = (((quad * 4 + pos_x) * 2 + core, row), ((quad * 4 + pos_y) * 2 + core, row))
    near_pos = (pos_x, pos_y)
    partners = [((chip + j) % chips * 2 + core, row) for j in range(1, chips)] + [sibling]
    partners += [(band, (row + j) % rows) for j in range(1, rows)]
    meet(partners)

    piece = rows_dev // 8

    def part(g, from_row, of_core, of_pos, first=0, size=None):
        start, count = chunks[g]
        size = piece if size is None else size
        at = from_row * rows_dev + (of_core * 4 + of_pos) * piece + first
        return full_ref.at[pl.ds(start, count), pl.ds(pl.multiple_of(at, 8), size)]

    def z_copy(g, j, from_row):
        start, count = chunks[g]
        at = pl.multiple_of((core * 4 + pos) * piece, 8)
        return remote(
            w_ref.at[pl.ds(start, count), pl.ds(at, piece)],
            part(g, from_row, core, pos),
            z_send.at[g, j - 1],
            z_recv.at[g, j - 1],
            (band, (from_row + j) % rows),
        )

    def a_copy(g, side, j, of_pos):
        region = part(g, (row - j + rows) % rows, core, of_pos)
        return remote(region, region, a_send.at[g, side, j - 1], a_recv.at[g, side, j - 1], near[side])

    def b_copy(g, side, j, of_pos):
        half = piece // 2
        region = part(g, (row - j + rows) % rows, core, of_pos, side * half, half)
        return remote(region, region, b_send.at[g, side, j - 1], b_recv.at[g, side, j - 1], near[side])

    def s_copy(g, j, of_core):
        region = part(g, (row - j + rows) % rows, of_core, 0, 0, 4 * piece)
        return remote(region, region, s_send.at[g, j - 1], s_recv.at[g, j - 1], sibling)

    others = range(1, rows)
    far = 3 - pos

    def start_z(g):
        for j in others:
            z_copy(g, j, row).start()

    def start_a(g):
        for j in others:
            z_copy(g, j, (row - j + rows) % rows).wait_recv()
            for side in range(2):
                a_copy(g, side, j, pos).start()

    def start_b(g):
        for j in others:
            for side in range(2):
                a_copy(g, side, j, near_pos[side]).wait_recv()
                b_copy(g, 1 - side, j, near_pos[side]).start()

    def start_s(g):
        for j in others:
            for side in range(2):
                b_copy(g, side, j, far).wait_recv()
            s_copy(g, j, core).start()

    def ready(g):
        for j in others:
            s_copy(g, j, 1 - core).wait_recv()

    def tick(t):
        for g, stage_of in ((t - 4, ready), (t - 3, start_s), (t - 2, start_b), (t - 1, start_a), (t + 1, start_z)):
            if 0 <= g < len(chunks):
                stage_of(g)

    own = pltpu.make_async_copy(
        w_ref,
        full_ref.at[:, pl.ds(pl.multiple_of(row * rows_dev, rows_dev), rows_dev)],
        own_sem,
    )
    start_z(0)
    start_z(1)
    own.start()

    def table_of(e):
        return table_ref if (layers - e) % 2 == 0 else table

    def items(e):
        par = e % 2
        found = [(0, border_buf.at[par], lambda k, c: table_of(e).at[k, c])]
        if e == 0:
            found.append((1, count_buf, lambda k, c: count_ref.at[k, c]))
        return found

    def out(e, item, src, dst, j):
        return remote(
            src,
            dst(core, chip),
            x_send.at[e + item * 4, j - 1],
            x_recv.at[e + item * 4, j - 1],
            ((chip + j) % chips * 2 + core, row),
        )

    def across(e, item, src, dst, j, of_core):
        origin = (chip - j + chips) % chips
        return remote(
            src if j == 0 else dst(of_core, origin),
            dst(of_core, origin),
            p_send.at[e + item * 4, j],
            p_recv.at[e + item * 4, j],
            sibling,
        )

    def share(e, value):
        par = e % 2
        choice = hot(iota((border, nodes), 1) == border_ref[...])
        rows_out = picked(choice, value)
        border_buf[par] = rows_out
        table_of(e)[core, chip] = rows_out
        for item, src, dst in items(e):
            for j in range(1, chips):
                out(e, item, src, dst, j).start()
            across(e, item, src, dst, 0, core).start()

    def relay(e):
        for item, src, dst in items(e):
            for j in range(1, chips):
                out(e, item, src, dst, j).wait_recv()
                across(e, item, src, dst, j, core).start()

    def gathered(e):
        for item, src, dst in items(e):
            for j in range(chips):
                across(e, item, src, dst, j, 1 - core).wait_recv()
            for j in range(chips):
                across(e, item, src, dst, j, core).wait_send()
            for j in range(1, chips):
                out(e, item, src, dst, j).wait_send()

    def put_src(at, value):
        value_high, value_low = pieces(value)
        size = value.shape[0]
        src_high[pl.ds(at, size)] = value_high
        src_low[pl.ds(at, size)] = value_low

    def save(kind, layer, src):
        dst = (before_ref, message_ref, edges_ref, embed_ref)[kind]
        return pltpu.make_async_copy(src, dst if layer is None else dst.at[layer], save_sem.at[kind])

    embed_buf = before_buf.at[pl.ds(0, grid_ref.shape[0])]
    embed_buf[...] = product(grid_ref[...], enc_ref[...])
    save(3, None, embed_buf).start()
    feed = hot(iota((nodes, grid_ref.shape[0]), 0) == feed_ref[...])
    fed = picked(feed, silu(embed_buf[...]))
    fed_ref[...] = fed
    nodes_ref[0] = normed(fed)[0]
    count = jnp.sum(mask_ref[...].astype(jnp.float32), axis=1, keepdims=True)
    counts = jnp.broadcast_to(count, count_buf.shape)
    count_buf[...] = counts
    count_ref[core, chip] = counts
    fill_rows(
        edge_buf.at[0], lambda at, size: silu(product(edge_ref[pl.ds(at, size)], enc_edge_ref[...])), 256
    )
    tick(1)
    table_rows = 2 * chips * border
    inputs = src_high.shape[0]

    def choose(at, size):
        columns = iota((size, inputs), 1)
        sent = columns == send_ref[pl.ds(at, size)]
        received = columns == recv_ref[pl.ds(at, size)] + (nodes + table_rows)
        return hot(jnp.logical_or(sent, received))

    fill_rows(pick, choose)

    def choose_receiver(at, size):
        return hot(iota((size, edges), 0) + at == recv_row_ref[...])

    fill_rows(gather_t, choose_receiver, 64)
    tick(2)
    tick(3)
    own.wait()
    for layer in range(layers):
        first = layer * blocks
        now, later = layer % 2, (layer + 1) % 2
        tick(4 + 2 * layer)
        weights.load(first, (1, 2, 0))
        node = nodes_ref[layer]
        node_high, node_low = pieces(node)
        sender = weights.times(node_high, node_low, 1)
        share(layer, sender)
        put_src(0, sender)
        put_src(nodes + table_rows, weights.times(node_high, node_low, 2))
        if layer > 0:
            save(0, layer - 1, before_buf).wait()
            save(1, layer - 1, message_buf).wait()
            save(2, layer - 1, edge_buf.at[later]).wait()
        else:
            save(3, None, embed_buf).wait()
        save(2, layer, edge_buf.at[now]).start()
        tick(5 + 2 * layer)
        relay(layer)
        weights.load(first, (3, 4, 5, 6))
        inner = weights.times(node_high, node_low, 4) + param_ref[layer, pl.ds(4, 1)]
        gathered(layer)
        table_now = table_of(layer)
        for side in range(2):
            for at in range(chips):
                put_src(nodes + (side * chips + at) * border, table_now[side, at])
        agg_ref[layer] = jnp.zeros((nodes, width), jnp.float32)

        def edge_tile(t, carry):
            at = pl.ds(pl.multiple_of(t * tile, tile), tile)
            edge = edge_buf[now, at]
            before = (
                weights.apply(edge, 0)
                + chosen(pick[at], src_high[...], src_low[...])
                + param_ref[layer, pl.ds(0, 1)]
            )
            before_buf[at] = before
            message = weights.apply(silu(before), 3) + param_ref[layer, pl.ds(1, 1)]
            message_buf[at] = message
            edge = (
                edge
                + normed(message)[0] * (1.0 + param_ref[layer, pl.ds(2, 1)])
                + param_ref[layer, pl.ds(3, 1)]
            )
            if layer < layers - 1:
                edge_buf[later, at] = edge
            agg_ref[layer] += picked(gather_t[:, at], edge)
            return carry

        lax.fori_loop(0, edges // tile, edge_tile, 0)
        save(0, layer, before_buf).start()
        save(1, layer, message_buf).start()
        inner = inner + weights.apply(agg_ref[layer], 5)
        inner_ref[layer] = inner
        update = weights.apply(silu(inner), 6) + param_ref[layer, pl.ds(5, 1)]
        update_ref[layer] = update
        nodes_ref[layer + 1] = (
            node
            + normed(update)[0] * (1.0 + param_ref[layer, pl.ds(6, 1)])
            + param_ref[layer, pl.ds(7, 1)]
        )
    share(layers, nodes_ref[layers])
    relay(layers)
    gathered(layers)
    save(0, layers - 1, before_buf).wait()
    save(1, layers - 1, message_buf).wait()
    save(2, layers - 1, edge_buf.at[(layers - 1) % 2]).wait()
    for g in range(len(chunks)):
        for j in others:
            z_copy(g, j, row).wait_send()
            for side in range(2):
                a_copy(g, side, j, pos).wait_send()
                b_copy(g, 1 - side, j, near_pos[side]).wait_send()
            s_copy(g, j, core).wait_send()


def forward(bands, rows, layers, grid, edge, send, recv, border, feed, mask, blocks, enc, enc_edge, params):
    f32, bf16 = jnp.float32, jnp.bfloat16
    dma = pltpu.SemaphoreType.DMA
    width = blocks.shape[2]
    edges, grids, rim = edge.shape[0], grid.shape[0], border.shape[0]
    nodes = NODE_DEV
    chips = bands // 2
    inputs = 2 * nodes + bands * rim
    each = blocks.shape[0] // layers
    chunks = []
    for layer in range(layers):
        chunks += [(layer * each, 3), (layer * each + 3, each - 3)]
    groups = len(chunks)
    tile = edges // 2

    def array(*shape):
        return jax.ShapeDtypeStruct(shape, f32)

    return pl.pallas_call(
        functools.partial(forward_kernel, bands, rows, tuple(chunks), tile),
        out_shape=(
            array(blocks.shape[0], width, width),
            array(layers, edges, width),
            array(layers, edges, width),
            array(layers, edges, width),
            array(grids, width),
            array(layers + 1, nodes, width),
            array(nodes, width),
            array(layers, nodes, width),
            array(layers, nodes, width),
            array(layers, nodes, width),
            array(2, chips, rim, width),
            array(2, chips, 8, 128),
        ),
        in_specs=[VMEM] * 12,
        out_specs=[ANY] * 5 + [VMEM] * 7,
        scratch_shapes=[
            pltpu.VMEM((2, edges, width), f32),
            pltpu.VMEM((edges, width), f32),
            pltpu.VMEM((edges, width), f32),
            pltpu.VMEM((edges, inputs), bf16),
            pltpu.VMEM((nodes, edges), bf16),
            pltpu.VMEM((inputs, width), bf16),
            pltpu.VMEM((inputs, width), bf16),
            pltpu.VMEM((each, width, width), bf16),
            pltpu.VMEM((each, width, width), bf16),
            pltpu.VMEM((2, width, width), f32),
            pltpu.VMEM((2, chips, rim, width), f32),
            pltpu.VMEM((2, rim, width), f32),
            pltpu.VMEM((8, 128), f32),
            dma((2,)),
            dma((4,)),
            dma,
            dma((groups, rows - 1)),
            dma((groups, rows - 1)),
            dma((groups, 2, rows - 1)),
            dma((groups, 2, rows - 1)),
            dma((groups, 2, rows - 1)),
            dma((groups, 2, rows - 1)),
            dma((groups, rows - 1)),
            dma((groups, rows - 1)),
            dma((5, chips - 1)),
            dma((5, chips - 1)),
            dma((5, chips)),
            dma((5, chips)),
        ],
        compiler_params=pltpu.CompilerParams(
            collective_id=1, has_side_effects=True, vmem_limit_bytes=VMEM_BYTES
        ),
        name="forward",
    )(
        grid,
        edge,
        send[:, None],
        recv[:, None],
        recv[None, :],
        border[:, None],
        feed[None, :],
        mask[None, :],
        blocks,
        enc,
        enc_edge,
        params,
    )


def slot_of(block):
    for owner in range(2 * OWNER_CHIPS):
        for slot in range(SLOTS):
            if slot_used(owner, slot) and slot_block(owner, slot) == block:
                return owner % 2, owner // 2, slot


def backward_kernel(
    bands,
    rows,
    each,
    tile,
    grid_ref,
    target_ref,
    mask_ref,
    edge_ref,
    read_ref,
    send_row_ref,
    recv_row_ref,
    recv_ref,
    border_row_ref,
    enc_edge_ref,
    dec_ref,
    param_ref,
    full_ref,
    before_ref,
    message_ref,
    edges_ref,
    embed_ref,
    nodes_ref,
    fed_ref,
    agg_ref,
    inner_ref,
    update_ref,
    table_ref,
    count_ref,
    grads_ref,
    small_ref,
    edge_buf,
    before_buf,
    message_buf,
    node_buf,
    agg_buf,
    inner_buf,
    update_buf,
    edge_grad,
    node_grad,
    part_high,
    part_low,
    pick_t,
    gather,
    high,
    low,
    stage,
    table,
    sib,
    land,
    stage_sem,
    load_sem,
    d_send,
    d_recv,
    r_send,
    r_recv,
):
    band, row, chip, core = place(bands, rows)
    chips = bands // 2
    layers = param_ref.shape[0]
    nodes, width = node_buf.shape
    edges = edge_buf.shape[0]
    grids = grid_ref.shape[0]
    border = border_row_ref.shape[1]
    table_rows = bands * border
    rows_dev = grads_ref.shape[3]
    weights = Weights(full_ref, stage, high, low, stage_sem)
    sibling = (chip * 2 + 1 - core, row)
    partners = [((chip + j) % chips * 2 + core, row) for j in range(1, chips)] + [sibling]
    own_rows = pl.ds(pl.multiple_of(row * rows_dev, rows_dev), rows_dev)

    def load(kind, layer):
        src = (before_ref, message_ref, edges_ref, agg_ref, inner_ref, update_ref, nodes_ref)[kind]
        dst = (before_buf, message_buf, edge_buf, agg_buf, inner_buf, update_buf, node_buf)[kind]
        return pltpu.make_async_copy(src.at[layer], dst, load_sem.at[kind])

    table_load = pltpu.make_async_copy(table_ref, table, load_sem.at[7])
    embed_buf = before_buf.at[pl.ds(0, grids)]
    fed_buf = agg_buf
    embed_load = pltpu.make_async_copy(embed_ref, embed_buf, load_sem.at[8])
    fed_load = pltpu.make_async_copy(fed_ref, fed_buf, load_sem.at[9])
    load(6, layers).start()
    table_load.start()
    for kind in range(6):
        load(kind, layers - 1).start()
    meet(partners)

    def to_sibling(e):
        return remote(table.at[1 - core], sib.at[e % 2], d_send.at[e], d_recv.at[e], sibling)

    def to_band(e, j):
        to = (chip + j) % chips
        return remote(
            table.at[core, to], land.at[e % 2, j - 1], r_send.at[e, j - 1], r_recv.at[e, j - 1], (to * 2 + core, row)
        )

    def give(e):
        to_sibling(e).wait()
        table[core] += sib[e % 2]
        for j in range(1, chips):
            to_band(e, j).start()

    def returned(e):
        total = table[core, chip]
        for j in range(1, chips):
            to_band(e, j).wait_recv()
            total = total + land[e % 2, j - 1]
        for j in range(1, chips):
            to_band(e, j).wait_send()
        return picked(hot(iota((nodes, border), 0) == border_row_ref[...]), total)

    def put_table(value_high, value_low, count):
        side_rows = chips * border
        for side in range(2):
            choice = pick_t[pl.ds(nodes + side * side_rows, side_rows), pl.ds(0, count)]
            table[side] = chosen(choice, value_high, value_low).reshape(chips, border, width)

    def put_grad(layer, block, value):
        grads_ref[slot_of(layer * each + block)] = value

    def add_grad(layer, block, value):
        grads_ref[slot_of(layer * each + block)] += value

    def choose_reads(at, size):
        line = iota((size, grids), 0) + at
        counts = jnp.zeros((size, grids), jnp.float32)
        for way in range(read_ref.shape[0]):
            counts = counts + jnp.where(line == read_ref[pl.ds(way, 1)], 1.0, 0.0)
        return counts.astype(jnp.bfloat16)

    def fill_reads(t, carry):
        at = pl.multiple_of(t * 64, 64)
        pick_t[pl.ds(at, 64), pl.ds(0, grids)] = choose_reads(at, 64)
        return carry

    lax.fori_loop(0, (nodes + table_rows) // 64, fill_reads, 0)

    def choose_gather(at, size):
        return hot(iota((size, nodes), 1) == recv_ref[pl.ds(at, size)])

    fill_rows(gather, choose_gather)
    load(6, layers).wait()
    table_load.wait()
    reads = edge_grad.at[pl.ds(0, grids)]
    own_high, own_low = pieces(node_buf[...])
    reads[...] = chosen(pick_t[pl.ds(0, nodes), pl.ds(0, grids)], own_high, own_low, TN)
    side_rows = chips * border
    for side in range(2):
        side_high, side_low = pieces(table[side].reshape(side_rows, width))
        choice = pick_t[pl.ds(nodes + side * side_rows, side_rows), pl.ds(0, grids)]
        reads[...] += chosen(choice, side_high, side_low, TN)
    load(6, layers - 1).start()
    weights.load((layers - 1) * each, (6, 4, 5, 3, 0, 1, 2))
    active = silu(reads[...])
    mask = mask_ref[:, 0:1].astype(jnp.float32)
    missed = grid_ref[...] + product(active, dec_ref[...]) - target_ref[...]
    total = jnp.sum(jnp.sum(count_ref[:, :, 0:1, 0:1], axis=0), axis=0)
    masked = mask * missed
    loss = jnp.sum(column(masked * missed), axis=1, keepdims=True)
    grad = (2.0 / total) * masked
    encs = grid_ref.shape[1]
    decs = dec_ref.shape[1]
    decoder_at = encs + 8 + layers * 8
    small_ref[pl.ds(decoder_at, decs)] = product(grad, active, TN)
    tail_rows = small_ref.shape[0] - decoder_at - decs
    small_ref[pl.ds(decoder_at + decs, tail_rows)] = jnp.broadcast_to(loss, (tail_rows, width))
    read_high, read_low = pieces(product(grad, dec_ref[...], NT) * silu_back(reads[...]))
    put_table(read_high, read_low, grids)
    to_sibling(0).start()
    node_grad[...] = chosen(pick_t[pl.ds(0, nodes), pl.ds(0, grids)], read_high, read_low)

    def choose(at, size):
        line = iota((size, edges), 0) + at
        sent = line == send_row_ref[...]
        received = line == recv_row_ref[...] + (nodes + table_rows)
        return hot(jnp.logical_or(sent, received))

    fill_rows(pick_t, choose, 64)
    give(0)
    edge_grad[...] = jnp.zeros_like(edge_grad)
    node_grad[...] += returned(0)

    for depth in range(layers):
        layer = layers - 1 - depth
        e = depth + 1
        base = encs + 8 + layer * 8

        def put_param(index, value, base=base):
            small_ref[pl.ds(base + index, 1)] = value

        def add_param(index, value, base=base):
            small_ref[pl.ds(base + index, 1)] += value

        for kind in (3, 4, 5, 6):
            load(kind, layer).wait()
        grad = node_grad[...]
        norm, scale = normed(update_buf[...])
        put_param(7, column(grad))
        put_param(6, column(grad * norm))
        grad = normed_back(grad * (1.0 + param_ref[layer, pl.ds(6, 1)]), norm, scale)
        put_param(5, column(grad))
        grad_high, grad_low = pieces(grad)
        put_grad(layer, 6, product(silu(inner_buf[:, own_rows]), grad, TN))
        grad = weights.times(grad_high, grad_low, 6, NT) * silu_back(inner_buf[...])
        put_param(4, column(grad))
        grad_high, grad_low = pieces(grad)
        put_grad(layer, 4, product(node_buf[:, own_rows], grad, TN))
        put_grad(layer, 5, product(agg_buf[:, own_rows], grad, TN))
        node_grad[...] += weights.times(grad_high, grad_low, 4, NT)
        agg_high, agg_low = pieces(weights.times(grad_high, grad_low, 5, NT))
        for kind in (0, 1, 2):
            load(kind, layer).wait()
        for index in range(4):
            put_param(index, jnp.zeros((1, width), jnp.float32))
        for block in (0, 3):
            put_grad(layer, block, jnp.zeros((rows_dev, width), jnp.float32))

        def edge_tile(t, carry):
            at = pl.ds(pl.multiple_of(t * tile, tile), tile)
            grad = edge_grad[at] + chosen(gather[at], agg_high, agg_low)
            edge_grad[at] = grad
            norm, scale = normed(message_buf[at])
            add_param(3, column(grad))
            add_param(2, column(grad * norm))
            grad = normed_back(grad * (1.0 + param_ref[layer, pl.ds(2, 1)]), norm, scale)
            add_param(1, column(grad))
            grad_high, grad_low = pieces(grad)
            add_grad(layer, 3, product(silu(before_buf[at, own_rows]), grad, TN))
            grad = weights.times(grad_high, grad_low, 3, NT) * silu_back(before_buf[at])
            add_param(0, column(grad))
            add_grad(layer, 0, product(edge_buf[at, own_rows], grad, TN))
            grad_high, grad_low = pieces(grad)
            part_high[at] = grad_high
            part_low[at] = grad_low
            return carry

        lax.fori_loop(0, edges // tile, edge_tile, 0)
        if layer > 0:
            for kind in range(6):
                load(kind, layer - 1).start()
        else:
            embed_load.start()
            fed_load.start()
        put_table(part_high[...], part_low[...], edges)
        to_sibling(e).start()
        sender = chosen(pick_t[pl.ds(0, nodes)], part_high[...], part_low[...])
        give(e)
        received = chosen(pick_t[pl.ds(nodes + table_rows, nodes)], part_high[...], part_low[...])

        def edge_back(t, carry):
            at = pl.ds(pl.multiple_of(t * tile, tile), tile)
            edge_grad[at] += weights.times(part_high[at], part_low[at], 0, NT)
            return carry

        lax.fori_loop(0, edges // tile, edge_back, 0)
        put_grad(layer, 2, product(node_buf[:, own_rows], received, TN))
        node_grad[...] += weights.apply(received, 2, NT)
        sender = sender + returned(e)
        put_grad(layer, 1, product(node_buf[:, own_rows], sender, TN))
        node_grad[...] += weights.apply(sender, 1, NT)
        if layer > 0:
            load(6, layer - 1).start()
            weights.load((layer - 1) * each, (6, 4, 5, 3, 0, 1, 2))

    embed_load.wait()
    fed_load.wait()
    norm, scale = normed(fed_buf[...])
    fed_grad = normed_back(node_grad[...], norm, scale)
    feed = hot(iota((grids, nodes), 1) == mask_ref[:, 1:2])
    grad = picked(feed, fed_grad) * silu_back(embed_buf[...])
    small_ref[pl.ds(0, encs)] = product(grid_ref[...], grad, TN)
    small_ref[pl.ds(encs, 8)] = jnp.zeros((8, width), jnp.float32)

    def embed_tile(t, carry):
        at = pl.ds(pl.multiple_of(t * tile, tile), tile)
        grad = edge_grad[at] * silu_back(product(edge_ref[at], enc_edge_ref[...]))
        small_ref[pl.ds(encs, 8)] += product(edge_ref[at], grad, TN)[:8]
        return carry

    lax.fori_loop(0, edges // tile, embed_tile, 0)


def backward(bands, rows, layers, rows_dev, inputs, saved):
    f32, bf16 = jnp.float32, jnp.bfloat16
    dma = pltpu.SemaphoreType.DMA
    grid, edge, border = inputs[0], inputs[3], inputs[8]
    full = saved[0]
    width = full.shape[2]
    each = full.shape[0] // layers
    edges, grids, rim = edge.shape[0], grid.shape[0], border.shape[1]
    nodes = NODE_DEV
    chips = bands // 2
    decs = inputs[10].shape[1]
    small = grid.shape[1] + 8 + layers * 8 + decs + 8
    small = -(-small // (16 * OWNER_CHIPS)) * 16 * OWNER_CHIPS
    tile = edges // 2
    node = pltpu.VMEM((nodes, width), f32)
    return pl.pallas_call(
        functools.partial(backward_kernel, bands, rows, each, tile),
        out_shape=(
            jax.ShapeDtypeStruct((2, OWNER_CHIPS, SLOTS, rows_dev, width), f32),
            jax.ShapeDtypeStruct((small, width), f32),
        ),
        in_specs=[VMEM] * 12 + [ANY] * 11 + [VMEM],
        out_specs=[VMEM, VMEM],
        scratch_shapes=[
            pltpu.VMEM((edges, width), f32),
            pltpu.VMEM((edges, width), f32),
            pltpu.VMEM((edges, width), f32),
            node,
            node,
            node,
            node,
            pltpu.VMEM((edges, width), f32),
            node,
            pltpu.VMEM((edges, width), bf16),
            pltpu.VMEM((edges, width), bf16),
            pltpu.VMEM((2 * nodes + bands * rim, edges), bf16),
            pltpu.VMEM((edges, nodes), bf16),
            pltpu.VMEM((each, width, width), bf16),
            pltpu.VMEM((each, width, width), bf16),
            pltpu.VMEM((2, width, width), f32),
            pltpu.VMEM((2, chips, rim, width), f32),
            pltpu.VMEM((2, chips, rim, width), f32),
            pltpu.VMEM((2, chips - 1, rim, width), f32),
            dma((2,)),
            dma((10,)),
            dma((layers + 1,)),
            dma((layers + 1,)),
            dma((layers + 1, chips - 1)),
            dma((layers + 1, chips - 1)),
        ],
        compiler_params=pltpu.CompilerParams(
            collective_id=2, has_side_effects=True, vmem_limit_bytes=VMEM_BYTES
        ),
        name="backward",
    )(*inputs, *saved)


def newton(mom_ref, out_ref, first, count, gram, poly, temp, later):
    def add_square(i, total):
        block = mom_ref[first + i]
        return total + jnp.sum(jnp.sum(block * block, axis=0, keepdims=True), axis=1, keepdims=True)

    total = lax.fori_loop(0, count, add_square, jnp.zeros((1, 1), jnp.float32))
    scale = 1.0 / (jnp.sqrt(total) + 1e-07)
    gram[...] = jnp.zeros_like(gram)

    def add_gram(i, carry):
        block = mom_ref[first + i] * scale
        mom_ref[first + i] = block
        gram[...] += product(block, block, TN)
        return carry

    lax.fori_loop(0, count, add_gram, 0)
    poly[...] = coef_b * gram[...] + coef_c * product(gram[...], gram[...])
    temp[...] = coef_a * gram[...] + product(gram[...], poly[...])
    gram[...] = coef_a * temp[...] + product(temp[...], poly[...])
    later[...] = coef_b * gram[...] + coef_c * product(gram[...], gram[...])
    temp[...] = coef_a * (poly[...] + later[...]) + product(poly[...], later[...])

    def finish(i, carry):
        block = mom_ref[first + i]
        out_ref[first + i] = (coef_a * coef_a) * block + product(block, temp[...])
        return carry

    lax.fori_loop(0, count, finish, 0)


def tail_kernel(
    bands,
    rows,
    grad_ref,
    small_ref,
    mom_ref,
    total_ref,
    ortho_ref,
    shared_ref,
    sib_grad,
    sib_small,
    part,
    part_small,
    land,
    land_small,
    mine,
    mine_small,
    held,
    matrix,
    result,
    back,
    gram,
    poly,
    temp,
    later,
    load_sem,
    sib_send,
    sib_recv,
    red_send,
    red_recv,
    all_send,
    all_recv,
    pass_send,
    pass_recv,
    up_send,
    up_recv,
    down_send,
    down_recv,
    keep_sem,
):
    chips = bands // 2
    band = lax.axis_index("band")
    row = lax.axis_index("row")
    chip, core = band // 2, band % 2
    sibling = (chip * 2 + 1 - core, row)
    rows_dev = held.shape[1]
    everyone = chips == OWNER_CHIPS

    def guard(cond, body):
        if cond is True:
            body()
        else:
            pl.when(cond)(body)

    def owns(at_chip):
        return True if everyone else at_chip < OWNER_CHIPS

    def both(one, two):
        if one is True:
            return two
        if two is True:
            return one
        return jnp.logical_and(one, two)

    def used(at_chip, slot):
        owner = at_chip * 2 + core
        return both(owns(at_chip), True if slot in (0, 3) else slot_used(owner, slot))

    barrier = pltpu.get_barrier_semaphore()
    partners = [((chip + j) % chips * 2 + core, row) for j in range(1, chips)] + [sibling]
    partners += [(band, (row + j) % rows) for j in range(1, rows)]
    for partner in partners:
        pl.semaphore_signal(barrier, inc=1, device_id=partner, device_id_type=MESH)
    pl.semaphore_wait(barrier, len(partners))

    first = remote(grad_ref.at[1 - core], sib_grad, sib_send.at[0], sib_recv.at[0], sibling)
    second = remote(small_ref.at[1 - core], sib_small, sib_send.at[1], sib_recv.at[1], sibling)
    first.start()
    second.start()
    owner = band

    def load(slot):
        return pltpu.make_async_copy(
            mom_ref.at[slot_block(owner, slot)], held.at[slot], load_sem.at[slot]
        )

    for slot in range(SLOTS):
        guard(used(chip, slot), lambda slot=slot: load(slot).start())
    first.wait()
    second.wait()
    for at in range(OWNER_CHIPS):
        part[at] = grad_ref[core, at] + sib_grad[at]
    part_small[...] = small_ref[core] + sib_small[...]

    def to_owner(j):
        to = (chip + j) % chips
        return (
            remote(part.at[to], land.at[j - 1], red_send.at[j - 1, 0], red_recv.at[j - 1, 0], (to * 2 + core, row)),
            remote(part_small.at[to], land_small.at[j - 1], red_send.at[j - 1, 1], red_recv.at[j - 1, 1], (to * 2 + core, row)),
        )

    for j in range(1, chips):
        def send(j=j):
            for copy in to_owner(j):
                copy.start()

        guard(owns((chip + j) % chips), send)

    def reduce():
        mine[...] = part[chip]
        mine_small[...] = part_small[chip]
        for j in range(1, chips):
            for copy in to_owner(j):
                copy.wait_recv()
            mine[...] += land[j - 1]
            mine_small[...] += land_small[j - 1]

    guard(owns(chip), reduce)

    def source(kind, slot):
        if slot == 3:
            return mine_small
        return (mine, back)[kind].at[slot]

    def target(kind, slot, at_chip, at_core):
        at_owner = at_chip * 2 + at_core
        if slot == 3:
            return shared_ref.at[at_core * OWNER_CHIPS + at_chip]
        return (total_ref, ortho_ref)[kind].at[slot_block(at_owner, slot)]

    def keep(kind, slot):
        return pltpu.make_async_copy(
            source(kind, slot), target(kind, slot, chip, core), keep_sem.at[kind, slot]
        )

    def out(kind, slot, j):
        return remote(
            source(kind, slot),
            target(kind, slot, chip, core),
            all_send.at[kind, j - 1, slot],
            all_recv.at[kind, j - 1, slot],
            ((chip + j) % chips * 2 + core, row),
        )

    def across(kind, slot, at_chip, j):
        src = source(kind, slot) if j == 0 else target(kind, slot, at_chip, core)
        return remote(
            src,
            target(kind, slot, at_chip, core),
            pass_send.at[kind, j, slot],
            pass_recv.at[kind, j, slot],
            sibling,
        )

    def crossed(kind, slot, at_chip, j):
        return remote(
            source(kind, slot),
            target(kind, slot, at_chip, 1 - core),
            pass_send.at[kind, j, slot],
            pass_recv.at[kind, j, slot],
            sibling,
        )

    def used_other(at_chip, slot):
        at_owner = at_chip * 2 + 1 - core
        return both(owns(at_chip), True if slot in (0, 3) else slot_used(at_owner, slot))

    def publish(kind, slots):
        for slot in slots:
            def start(slot=slot):
                for j in range(1, chips):
                    out(kind, slot, j).start()
                keep(kind, slot).start()
                across(kind, slot, chip, 0).start()

            guard(used(chip, slot), start)

    def relay(kind, slots):
        for j in range(1, chips):
            origin = (chip - j + chips) % chips
            for slot in slots:
                def start(slot=slot, j=j, origin=origin):
                    remote(
                        source(kind, slot),
                        target(kind, slot, origin, core),
                        all_send.at[kind, j - 1, slot],
                        all_recv.at[kind, j - 1, slot],
                        (origin * 2 + core, row),
                    ).wait_recv()
                    across(kind, slot, origin, j).start()

                guard(used(origin, slot), start)

    def settle(kind, slots):
        for j in range(chips):
            origin = (chip - j + chips) % chips
            for slot in slots:
                def finish(slot=slot, j=j, origin=origin):
                    across(kind, slot, origin, j).wait_send()

                def arrive(slot=slot, j=j, origin=origin):
                    crossed(kind, slot, origin, j).wait_recv()

                guard(used(origin, slot), finish)
                guard(used_other(origin, slot), arrive)
        for slot in slots:
            def sent(slot=slot):
                for j in range(1, chips):
                    out(kind, slot, j).wait_send()
                keep(kind, slot).wait()

            guard(used(chip, slot), sent)

    third = owner // 3
    row_a = rows // 2 - 1 + core
    row_b = rows // 2 - core
    split_at = 3 - third

    def home(slot):
        if slot == 0:
            return row_a
        late = (slot + third) // 3
        return row_a + late * (row_b - row_a)

    def up(slot, from_row):
        at = pl.ds(pl.multiple_of(from_row * rows_dev, rows_dev), rows_dev)
        step = (from_row - home(slot) + rows) % rows
        return remote(
            held.at[slot],
            matrix.at[slot, at],
            up_send.at[slot],
            up_recv.at[slot, step],
            (band, home(slot)),
        )

    for slot in range(SLOTS):
        def momentum(slot=slot):
            load(slot).wait()
            held[slot] = momentum_decay * held[slot] + mine[slot]

            @pl.when(row == home(slot))
            def _():
                at = pl.ds(pl.multiple_of(row * rows_dev, rows_dev), rows_dev)
                matrix[slot, at] = held[slot]

            @pl.when(row != home(slot))
            def _():
                up(slot, row).start()

        guard(used(chip, slot), momentum)
    publish(0, (0, 1, 2, 3))

    def down(slot, to_row):
        at = pl.ds(pl.multiple_of(to_row * rows_dev, rows_dev), rows_dev)
        step = (to_row - home(slot) + rows) % rows
        return remote(
            result.at[slot, at],
            back.at[slot],
            down_send.at[slot, step],
            down_recv.at[slot],
            (band, to_row),
        )

    for slot in range(SLOTS):
        def arrived(slot=slot):
            @pl.when(row == home(slot))
            def _():
                for step in range(1, rows):
                    up(slot, (row + step) % rows).wait_recv()

        guard(used(chip, slot), arrived)

    def at_a():
        newton(matrix, result, 0, split_at, gram, poly, temp, later)

    def at_b():
        newton(matrix, result, split_at, 1, gram, poly, temp, later)

    guard(both(owns(chip), row == row_a), at_a)
    guard(
        both(owns(chip), jnp.logical_and(row == row_b, jnp.logical_and(owner > 2, owner < 7))), at_b
    )

    for slot in range(SLOTS):
        def give(slot=slot):
            @pl.when(row == home(slot))
            def _():
                for step in range(1, rows):
                    down(slot, (row + step) % rows).start()
                at = pl.ds(pl.multiple_of(row * rows_dev, rows_dev), rows_dev)
                back[slot] = result[slot, at]

        guard(used(chip, slot), give)
    relay(0, (0, 1, 2, 3))
    for slot in range(SLOTS):
        def take(slot=slot):
            @pl.when(row != home(slot))
            def _():
                down(slot, row).wait_recv()

        guard(used(chip, slot), take)
    publish(1, (0, 1, 2))
    relay(1, (0, 1, 2))
    settle(0, (0, 1, 2, 3))
    settle(1, (0, 1, 2))
    for j in range(1, chips):
        def reduced(j=j):
            for copy in to_owner(j):
                copy.wait_send()

        guard(owns((chip + j) % chips), reduced)
    for slot in range(SLOTS):
        def closed(slot=slot):
            @pl.when(row != home(slot))
            def _():
                up(slot, row).wait_send()

            @pl.when(row == home(slot))
            def _():
                for step in range(1, rows):
                    down(slot, (row + step) % rows).wait_send()

        guard(used(chip, slot), closed)


def tail(bands, rows, grads, small, momentum):
    blocks, rows_dev, width = momentum.shape
    chips = bands // 2
    chunk = small.shape[2]
    f32 = jnp.float32
    dma = pltpu.SemaphoreType.DMA
    square = pltpu.VMEM((width, width), f32)
    return pl.pallas_call(
        functools.partial(tail_kernel, bands, rows),
        out_shape=(
            jax.ShapeDtypeStruct((blocks, rows_dev, width), f32),
            jax.ShapeDtypeStruct((blocks, rows_dev, width), f32),
            jax.ShapeDtypeStruct((2 * OWNER_CHIPS, chunk, width), f32),
        ),
        in_specs=[VMEM, VMEM, ANY],
        out_specs=[ANY, ANY, ANY],
        scratch_shapes=[
            pltpu.VMEM((OWNER_CHIPS, SLOTS, rows_dev, width), f32),
            pltpu.VMEM((OWNER_CHIPS, chunk, width), f32),
            pltpu.VMEM((OWNER_CHIPS, SLOTS, rows_dev, width), f32),
            pltpu.VMEM((OWNER_CHIPS, chunk, width), f32),
            pltpu.VMEM((chips - 1, SLOTS, rows_dev, width), f32),
            pltpu.VMEM((chips - 1, chunk, width), f32),
            pltpu.VMEM((SLOTS, rows_dev, width), f32),
            pltpu.VMEM((chunk, width), f32),
            pltpu.VMEM((SLOTS, rows_dev, width), f32),
            pltpu.VMEM((SLOTS, width, width), f32),
            pltpu.VMEM((SLOTS, width, width), f32),
            pltpu.VMEM((SLOTS, rows_dev, width), f32),
            square,
            square,
            square,
            square,
            dma((SLOTS,)),
            dma((2,)),
            dma((2,)),
            dma((chips - 1, 2)),
            dma((chips - 1, 2)),
            dma((2, chips - 1, SLOTS + 1)),
            dma((2, chips - 1, SLOTS + 1)),
            dma((2, chips, SLOTS + 1)),
            dma((2, chips, SLOTS + 1)),
            dma((SLOTS,)),
            dma((SLOTS, rows)),
            dma((SLOTS, rows)),
            dma((SLOTS,)),
            dma((2, SLOTS + 1)),
        ],
        compiler_params=pltpu.CompilerParams(
            collective_id=0, has_side_effects=True, vmem_limit_bytes=VMEM_BYTES
        ),
        name="tail",
    )(grads, small, momentum)


def muon_finish(weights, ortho):
    scales = jnp.array(block_scale, dtype=weights.dtype)[None, :, None, None]
    return weights * (1.0 - muon_rate * weight_decay) - muon_rate * scales * ortho


def adam_update(values, first, second, gradient, rate):
    first = beta_one * first + (1.0 - beta_one) * gradient
    second = beta_two * second + (1.0 - beta_two) * gradient * gradient
    corrected = (
        first / (1.0 - beta_one**STEP) / (jnp.sqrt(second / (1.0 - beta_two**STEP)) + adam_eps)
    )
    return (first, second, values * (1.0 - rate * weight_decay) - rate * corrected)


def body(
    grid_input,
    grid_target,
    edge_input,
    senders,
    receivers,
    border_nodes,
    grid_to_mesh,
    mesh_to_grid,
    loss_mask,
    encoder_weights,
    encoder_first,
    encoder_second,
    processor_weights,
    processor_momentum,
    processor_average,
    norm_params,
    norm_first,
    norm_second,
    decoder_weights,
    decoder_first,
    decoder_second,
):
    bands, rows = lax.axis_size("band"), lax.axis_size("row")
    layers, blocks, rows_dev, width = processor_weights.shape
    channels = grid_input.shape[1]
    edge_channels = edge_input.shape[1]
    wide = -(-channels // 128) * 128
    grids, rim = grid_input.shape[0], border_nodes.shape[0]

    def widen(value, size, axis):
        pads = [(0, 0), (0, 0)]
        pads[axis] = (0, size - value.shape[axis])
        return jnp.pad(value, pads)

    def table_place(index):
        owner, spot = (index - NODE_DEV) // rim, (index - NODE_DEV) % rim
        moved = NODE_DEV + (owner % 2 * (bands // 2) + owner // 2) * rim + spot
        return jnp.where(index < NODE_DEV, index, moved)

    sent = table_place(senders)
    reads = table_place(mesh_to_grid).reshape(grids, -1).T
    grid_wide = widen(grid_input, wide, 1)
    edge_wide = widen(edge_input, 128, 1)
    edge_embed = widen(encoder_weights[channels:], 128, 0)
    flat_weights = processor_weights.reshape(layers * blocks, rows_dev, width)
    saved = forward(
        bands,
        rows,
        layers,
        grid_wide,
        edge_wide,
        sent,
        receivers,
        border_nodes,
        grid_to_mesh,
        loss_mask,
        flat_weights,
        widen(encoder_weights[:channels], wide, 0),
        edge_embed,
        norm_params,
    )
    inputs = (
        grid_wide,
        widen(grid_target, wide, 1),
        jnp.stack([loss_mask, grid_to_mesh], axis=1),
        edge_wide,
        reads,
        sent[None, :],
        receivers[None, :],
        receivers[:, None],
        border_nodes[None, :],
        edge_embed,
        widen(decoder_weights, wide, 1),
        norm_params,
    )
    grads, small = backward(bands, rows, layers, rows_dev, inputs, saved)
    mask_count = jnp.sum(saved[-1][:, :, 0, 0])
    total, ortho, small = tail(
        bands,
        rows,
        grads,
        small.reshape(2, OWNER_CHIPS, -1, width),
        processor_momentum.reshape(layers * blocks, rows_dev, width),
    )
    small = small.reshape(-1, width)
    params_at = wide + 8
    decoder_at = params_at + layers * 8
    encoder_grad = jnp.concatenate([small[:channels], small[wide : wide + edge_channels]])
    param_grad = small[params_at:decoder_at].reshape(norm_params.shape)
    decoder_grad = small[decoder_at : decoder_at + channels].T
    loss_total = small[decoder_at + wide, 0]
    next_momentum = momentum_decay * processor_momentum + total.reshape(processor_weights.shape)
    next_weights = muon_finish(processor_weights, ortho.reshape(processor_weights.shape))
    next_average = average_decay * processor_average + (1.0 - average_decay) * next_weights
    param_moment, param_square, param_values = adam_update(
        norm_params, norm_first, norm_second, param_grad, param_rate
    )
    encoder_moment, encoder_square, encoder_values = adam_update(
        encoder_weights, encoder_first, encoder_second, encoder_grad, adam_rate
    )
    decoder_moment, decoder_square, decoder_values = adam_update(
        decoder_weights, decoder_first, decoder_second, decoder_grad, adam_rate
    )
    return (
        loss_total,
        mask_count,
        next_weights,
        next_momentum,
        next_average,
        param_moment,
        param_square,
        param_values,
        encoder_moment,
        encoder_square,
        encoder_values,
        decoder_moment,
        decoder_square,
        decoder_values,
    )


def solution(mesh):
    return jax.shard_map(
        body,
        mesh=mesh,
        in_specs=(
            P("band", None),
            P("band", None),
            P("band", None),
            P("band"),
            P("band"),
            P("band"),
            P("band"),
            P("band"),
            P("band"),
            P(),
            P(),
            P(),
            P(None, None, "row", None),
            P(None, None, "row", None),
            P(None, None, "row", None),
            P(),
            P(),
            P(),
            P(),
            P(),
            P(),
        ),
        out_specs=(
            P(),
            P(),
            P(None, None, "row", None),
            P(None, None, "row", None),
            P(None, None, "row", None),
            P(),
            P(),
            P(),
            P(),
            P(),
            P(),
            P(),
            P(),
            P(),
        ),
        check_vma=False,
    )
```

```python
import functools

import jax
import jax.numpy as jnp
from jax import lax
from jax.experimental import pallas as pl
from jax.experimental.pallas import tpu as pltpu
from jax.sharding import PartitionSpec as P

STEP = 10
NODE_DEV = 320


coef_a = 3.4445
coef_b = -4.775
coef_c = 2.0315
momentum_decay = 0.95
muon_rate = 0.3
adam_rate = 0.02
param_rate = 0.1
beta_one = 0.9
beta_two = 0.95
adam_eps = 1e-08
weight_decay = 0.01
average_decay = 0.9
block_scale = (3.0**0.5, 3.0**0.5, 3.0**0.5, 1.0, 2.0**0.5, 2.0**0.5, 1.0)


MESH = pl.DeviceIdType.MESH
NN = (((1,), (0,)), ((), ()))
NT = (((1,), (1,)), ((), ()))
TN = (((0,), (0,)), ((), ()))
OWNER_CHIPS = 4
SLOTS = 3
VMEM_BYTES = 62 * 2**20
ANY = pl.BlockSpec(memory_space=pl.ANY)
VMEM = pl.BlockSpec(memory_space=pltpu.VMEM)


def pieces(value):
    high = value.astype(jnp.bfloat16)
    return high, (value - high.astype(jnp.float32)).astype(jnp.bfloat16)


def dot(left, right, dims=NN):
    return lax.dot_general(left, right, dims, preferred_element_type=jnp.float32)


def product(left, right, dims=NN):
    left_high, left_low = pieces(left)
    right_high, right_low = pieces(right)
    return (
        dot(left_high, right_high, dims)
        + dot(left_low, right_high, dims)
        + dot(left_high, right_low, dims)
    )


def slot_block(owner, slot):
    third = owner // 3
    last = third // 2
    return (1 - last) * (7 * (owner % 3) + 4 * third + slot) + last * (
        3 + 14 * (owner - 6) + 7 * slot
    )


def slot_used(owner, slot):
    return owner < (8, 7, 6)[slot]


def remote(src, dst, send_sem, recv_sem, device):
    return pltpu.make_async_remote_copy(
        src_ref=src,
        dst_ref=dst,
        send_sem=send_sem,
        recv_sem=recv_sem,
        device_id=device,
        device_id_type=MESH,
    )


def silu(value):
    return value / (1.0 + jnp.exp(-value))


def silu_back(value):
    gate = 1.0 / (1.0 + jnp.exp(-value))
    return gate * (1.0 + value * (1.0 - gate))


def normed(value):
    centered = value - jnp.mean(value, axis=-1, keepdims=True)
    scale = lax.rsqrt(jnp.mean(centered * centered, axis=-1, keepdims=True) + 1e-05)
    return centered * scale, scale


def normed_back(grad, norm, scale):
    inner = jnp.mean(grad * norm, axis=-1, keepdims=True)
    return (grad - jnp.mean(grad, axis=-1, keepdims=True) - norm * inner) * scale


def column(value):
    return jnp.sum(value, axis=0, keepdims=True)


def hot(mask):
    return jnp.where(mask, 1.0, 0.0).astype(jnp.bfloat16)


def chosen(choice, high, low, dims=NN):
    return dot(choice, high, dims) + dot(choice, low, dims)


def picked(choice, value):
    high, low = pieces(value)
    return chosen(choice, high, low)


def fill_rows(out_ref, make, tile=128):
    def step(t, carry):
        at = pl.multiple_of(t * tile, tile)
        out_ref[pl.ds(at, tile)] = make(at, tile)
        return carry

    lax.fori_loop(0, out_ref.shape[0] // tile, step, 0)


def iota(shape, axis):
    return lax.broadcasted_iota(jnp.int32, shape, axis)


SEND_ROW, RECV_ROW, BORDER_ROW, FEED_ROW, MASK_ROW, READ_ROW = range(6)


class Weights:
    def __init__(self, full_ref, stage, high, low, sem):
        self.full, self.stage, self.high, self.low, self.sem = full_ref, stage, high, low, sem

    def copy(self, block, slot):
        return pltpu.make_async_copy(self.full.at[block], self.stage.at[slot], self.sem.at[slot])

    def load(self, first, blocks):
        for n, block in enumerate(blocks[:2]):
            self.copy(first + block, n % 2).start()
        for n, block in enumerate(blocks):
            self.copy(first + block, n % 2).wait()
            high, low = pieces(self.stage[n % 2])
            self.high[block] = high
            self.low[block] = low
            if n + 2 < len(blocks):
                self.copy(first + blocks[n + 2], n % 2).start()

    def times(self, high, low, block, dims=NN):
        weight = self.high[block]
        return dot(high, weight, dims) + dot(low, weight, dims) + dot(high, self.low[block], dims)

    def apply(self, value, block, dims=NN):
        high, low = pieces(value)
        return self.times(high, low, block, dims)


def place(bands, rows):
    band = lax.axis_index("band")
    row = lax.axis_index("row")
    return band, row, band // 2, band % 2


def meet(partners):
    barrier = pltpu.get_barrier_semaphore()
    for partner in partners:
        pl.semaphore_signal(barrier, inc=1, device_id=partner, device_id_type=MESH)
    pl.semaphore_wait(barrier, len(partners))


def forward_kernel(
    bands,
    rows,
    chunks,
    tile,
    grid_ref,
    edge_ref,
    send_ref,
    recv_ref,
    border_ref,
    feed_ref,
    mask_ref,
    read_ref,
    w_ref,
    enc_ref,
    enc_edge_ref,
    param_ref,
    full_ref,
    before_ref,
    message_ref,
    edges_ref,
    embed_ref,
    nodes_ref,
    fed_ref,
    agg_ref,
    inner_ref,
    update_ref,
    table_ref,
    count_ref,
    index_ref,
    edge_buf,
    before_buf,
    message_buf,
    index_t,
    pick,
    gather_t,
    src_high,
    src_low,
    high,
    low,
    stage,
    table,
    border_buf,
    count_buf,
    stage_sem,
    save_sem,
    own_sem,
    z_send,
    z_recv,
    a_send,
    a_recv,
    b_send,
    b_recv,
    s_send,
    s_recv,
    x_send,
    x_recv,
    p_send,
    p_recv,
):
    band, row, chip, core = place(bands, rows)
    chips = bands // 2
    layers, blocks = agg_ref.shape[0], w_ref.shape[0] // agg_ref.shape[0]
    rows_dev = w_ref.shape[1]
    nodes, width = fed_ref.shape
    edges = edge_buf.shape[1]
    border = border_buf.shape[1]
    grids = grid_ref.shape[0]
    weights = Weights(full_ref, stage, high, low, stage_sem)
    quad, pos = chip // 4, chip % 4
    pos_x, pos_y = pos + 1 - 2 * (pos % 2), pos + 2 - 4 * (pos // 2)
    sibling = (chip * 2 + 1 - core, row)
    near = (((quad * 4 + pos_x) * 2 + core, row), ((quad * 4 + pos_y) * 2 + core, row))
    near_pos = (pos_x, pos_y)
    partners = [((chip + j) % chips * 2 + core, row) for j in range(1, chips)] + [sibling]
    partners += [(band, (row + j) % rows) for j in range(1, rows)]
    meet(partners)

    piece = rows_dev // 8

    def part(g, from_row, of_core, of_pos, first=0, size=None):
        start, count = chunks[g]
        size = piece if size is None else size
        at = from_row * rows_dev + (of_core * 4 + of_pos) * piece + first
        return full_ref.at[pl.ds(start, count), pl.ds(pl.multiple_of(at, 8), size)]

    def z_copy(g, j, from_row):
        start, count = chunks[g]
        at = pl.multiple_of((core * 4 + pos) * piece, 8)
        return remote(
            w_ref.at[pl.ds(start, count), pl.ds(at, piece)],
            part(g, from_row, core, pos),
            z_send.at[g, j - 1],
            z_recv.at[g, j - 1],
            (band, (from_row + j) % rows),
        )

    def a_copy(g, side, j, of_pos):
        region = part(g, (row - j + rows) % rows, core, of_pos)
        return remote(region, region, a_send.at[g, side, j - 1], a_recv.at[g, side, j - 1], near[side])

    def b_copy(g, side, j, of_pos):
        half = piece // 2
        region = part(g, (row - j + rows) % rows, core, of_pos, side * half, half)
        return remote(region, region, b_send.at[g, side, j - 1], b_recv.at[g, side, j - 1], near[side])

    def s_copy(g, j, of_core):
        region = part(g, (row - j + rows) % rows, of_core, 0, 0, 4 * piece)
        return remote(region, region, s_send.at[g, j - 1], s_recv.at[g, j - 1], sibling)

    others = range(1, rows)
    far = 3 - pos

    def start_z(g):
        for j in others:
            z_copy(g, j, row).start()

    def start_a(g):
        for j in others:
            z_copy(g, j, (row - j + rows) % rows).wait_recv()
            for side in range(2):
                a_copy(g, side, j, pos).start()

    def start_b(g):
        for j in others:
            for side in range(2):
                a_copy(g, side, j, near_pos[side]).wait_recv()
                b_copy(g, 1 - side, j, near_pos[side]).start()

    def start_s(g):
        for j in others:
            for side in range(2):
                b_copy(g, side, j, far).wait_recv()
            s_copy(g, j, core).start()

    def ready(g):
        for j in others:
            s_copy(g, j, 1 - core).wait_recv()

    def tick(t):
        for g, stage_of in ((t - 5, ready), (t - 4, start_s), (t - 3, start_b), (t - 1, start_a), (t + 1, start_z)):
            if 0 <= g < len(chunks):
                stage_of(g)

    own = pltpu.make_async_copy(
        w_ref,
        full_ref.at[:, pl.ds(pl.multiple_of(row * rows_dev, rows_dev), rows_dev)],
        own_sem,
    )
    start_z(0)
    start_z(1)
    own.start()

    def table_of(e):
        return table_ref if (layers - e) % 2 == 0 else table

    def items(e):
        par = e % 2
        found = [(0, border_buf.at[par], lambda k, c: table_of(e).at[k, c])]
        if e == 0:
            found.append((1, count_buf, lambda k, c: count_ref.at[k, c]))
        return found

    def out(e, item, src, dst, j):
        return remote(
            src,
            dst(core, chip),
            x_send.at[e + item * 4, j - 1],
            x_recv.at[e + item * 4, j - 1],
            ((chip + j) % chips * 2 + core, row),
        )

    def across(e, item, src, dst, j, of_core):
        origin = (chip - j + chips) % chips
        return remote(
            src if j == 0 else dst(of_core, origin),
            dst(of_core, origin),
            p_send.at[e + item * 4, j],
            p_recv.at[e + item * 4, j],
            sibling,
        )

    def share(e, value):
        par = e % 2
        choice = hot(iota((border, nodes), 1) == index_t[pl.ds(0, border), BORDER_ROW : BORDER_ROW + 1])
        rows_out = picked(choice, value)
        border_buf[par] = rows_out
        table_of(e)[core, chip] = rows_out
        for item, src, dst in items(e):
            for j in range(1, chips):
                out(e, item, src, dst, j).start()
            across(e, item, src, dst, 0, core).start()

    def relay(e):
        for item, src, dst in items(e):
            for j in range(1, chips):
                out(e, item, src, dst, j).wait_recv()
                across(e, item, src, dst, j, core).start()

    def gathered(e):
        for item, src, dst in items(e):
            for j in range(chips):
                across(e, item, src, dst, j, 1 - core).wait_recv()
            for j in range(chips):
                across(e, item, src, dst, j, core).wait_send()
            for j in range(1, chips):
                out(e, item, src, dst, j).wait_send()

    def put_src(at, value):
        value_high, value_low = pieces(value)
        size = value.shape[0]
        src_high[pl.ds(at, size)] = value_high
        src_low[pl.ds(at, size)] = value_low

    def save(kind, layer, src):
        dst = (before_ref, message_ref, edges_ref, embed_ref)[kind]
        return pltpu.make_async_copy(src, dst if layer is None else dst.at[layer], save_sem.at[kind])

    def table_place(index):
        far = (index - nodes).astype(jnp.float32)
        owner = jnp.floor((far + 0.5) * (1.0 / border))
        at_chip = jnp.floor(owner * 0.5)
        moved = ((owner - 2.0 * at_chip) * chips + at_chip) * border + far - owner * border
        return jnp.where(index < nodes, index, moved.astype(jnp.int32) + nodes)

    index_ref[...] = jnp.zeros_like(index_ref)
    index_ref[SEND_ROW : SEND_ROW + 1] = table_place(send_ref[...])
    index_ref[RECV_ROW : RECV_ROW + 1] = recv_ref[...]
    index_ref[BORDER_ROW : BORDER_ROW + 1, pl.ds(0, border)] = border_ref[...]
    index_ref[FEED_ROW : FEED_ROW + 1, pl.ds(0, grids)] = feed_ref[...]
    index_ref[MASK_ROW : MASK_ROW + 1, pl.ds(0, grids)] = mask_ref[...]
    index_ref[READ_ROW:, pl.ds(0, grids)] = table_place(read_ref[...])
    index_t[...] = index_ref[...].T
    embed_buf = before_buf.at[pl.ds(0, grids)]
    embed_buf[...] = product(grid_ref[...], enc_ref[...])
    save(3, None, embed_buf).start()
    tick(1)
    feed = hot(iota((nodes, grids), 0) == index_ref[FEED_ROW : FEED_ROW + 1, pl.ds(0, grids)])
    fed = picked(feed, silu(embed_buf[...]))
    fed_ref[...] = fed
    nodes_ref[0] = normed(fed)[0]
    mask = index_ref[MASK_ROW : MASK_ROW + 1, pl.ds(0, grids)].astype(jnp.float32)
    counts = jnp.broadcast_to(jnp.sum(mask, axis=1, keepdims=True), count_buf.shape)
    count_buf[...] = counts
    count_ref[core, chip] = counts
    tick(2)
    fill_rows(
        edge_buf.at[0], lambda at, size: silu(product(edge_ref[pl.ds(at, size)], enc_edge_ref[...])), 256
    )
    inputs = src_high.shape[0]
    near_inputs = 2 * nodes

    def choose(at, size):
        columns = iota((size, inputs), 1)
        sent = index_t[pl.ds(at, size), SEND_ROW : SEND_ROW + 1]
        received = index_t[pl.ds(at, size), RECV_ROW : RECV_ROW + 1] + nodes
        sent = jnp.where(sent < nodes, sent, sent + nodes)
        return hot(jnp.logical_or(columns == sent, columns == received))

    fill_rows(pick, choose)
    tick(3)

    def choose_receiver(at, size):
        return hot(iota((size, edges), 0) + at == index_ref[RECV_ROW : RECV_ROW + 1])

    fill_rows(gather_t, choose_receiver, 64)
    own.wait()
    tick(4)
    tick(5)
    for layer in range(layers):
        first = layer * blocks
        now, later = layer % 2, (layer + 1) % 2
        weights.load(first, (1, 2))
        node = nodes_ref[layer]
        node_high, node_low = pieces(node)
        sender = weights.times(node_high, node_low, 1)
        share(layer, sender)
        put_src(0, sender)
        put_src(nodes, weights.times(node_high, node_low, 2))
        if layer > 0:
            save(0, layer - 1, before_buf).wait()
            save(1, layer - 1, message_buf).wait()
            save(2, layer - 1, edge_buf.at[later]).wait()
        else:
            save(3, None, embed_buf).wait()
        save(2, layer, edge_buf.at[now]).start()
        tick(6 + 4 * layer)
        weights.load(first, (0,))

        def near_part(t):
            at = pl.ds(t * tile, tile)
            before_buf[at] = (
                weights.apply(edge_buf[now, at], 0)
                + chosen(
                    pick[at, pl.ds(0, near_inputs)],
                    src_high[pl.ds(0, near_inputs)],
                    src_low[pl.ds(0, near_inputs)],
                )
                + param_ref[layer, pl.ds(0, 1)]
            )

        near_part(0)
        tick(7 + 4 * layer)
        relay(layer)
        near_part(1)
        weights.load(first, (3, 4))
        inner = weights.times(node_high, node_low, 4) + param_ref[layer, pl.ds(4, 1)]
        gathered(layer)
        table_now = table_of(layer)
        for side in range(2):
            put_src(
                near_inputs + side * chips * border,
                table_now[side].reshape(chips * border, width),
            )
        agg_ref[layer] = jnp.zeros((nodes, width), jnp.float32)

        def edge_tile(t):
            at = pl.ds(t * tile, tile)
            far_inputs = pl.ds(near_inputs, inputs - near_inputs)
            before = before_buf[at] + chosen(
                pick[at, far_inputs], src_high[far_inputs], src_low[far_inputs]
            )
            before_buf[at] = before
            message = weights.apply(silu(before), 3) + param_ref[layer, pl.ds(1, 1)]
            message_buf[at] = message
            edge = (
                edge_buf[now, at]
                + normed(message)[0] * (1.0 + param_ref[layer, pl.ds(2, 1)])
                + param_ref[layer, pl.ds(3, 1)]
            )
            if layer < layers - 1:
                edge_buf[later, at] = edge
            agg_ref[layer] += picked(gather_t[:, at], edge)

        edge_tile(0)
        tick(8 + 4 * layer)
        edge_tile(1)
        save(0, layer, before_buf).start()
        save(1, layer, message_buf).start()
        weights.load(first, (5, 6))
        inner = inner + weights.apply(agg_ref[layer], 5)
        inner_ref[layer] = inner
        update = weights.apply(silu(inner), 6) + param_ref[layer, pl.ds(5, 1)]
        update_ref[layer] = update
        nodes_ref[layer + 1] = (
            node
            + normed(update)[0] * (1.0 + param_ref[layer, pl.ds(6, 1)])
            + param_ref[layer, pl.ds(7, 1)]
        )
        tick(9 + 4 * layer)
    share(layers, nodes_ref[layers])
    relay(layers)
    gathered(layers)
    save(0, layers - 1, before_buf).wait()
    save(1, layers - 1, message_buf).wait()
    save(2, layers - 1, edge_buf.at[(layers - 1) % 2]).wait()
    for g in range(len(chunks)):
        for j in others:
            z_copy(g, j, row).wait_send()
            for side in range(2):
                a_copy(g, side, j, pos).wait_send()
                b_copy(g, 1 - side, j, near_pos[side]).wait_send()
            s_copy(g, j, core).wait_send()


def forward(bands, rows, grid, edge, indices, blocks, enc, enc_edge, params):
    f32, bf16 = jnp.float32, jnp.bfloat16
    dma = pltpu.SemaphoreType.DMA
    width = blocks.shape[2]
    edges, grids = edge.shape[0], grid.shape[0]
    layers = params.shape[0]
    rim = indices[2].shape[1]
    index_rows = READ_ROW + indices[5].shape[0]
    nodes = NODE_DEV
    chips = bands // 2
    inputs = 2 * nodes + bands * rim
    each = blocks.shape[0] // layers
    chunks = []
    for layer in range(layers):
        chunks += [(layer * each + first, size) for first, size in ((1, 2), (0, 1), (3, 2), (5, 2))]
    groups = len(chunks)
    tile = edges // 2

    def array(*shape):
        return jax.ShapeDtypeStruct(shape, f32)

    return pl.pallas_call(
        functools.partial(forward_kernel, bands, rows, tuple(chunks), tile),
        out_shape=(
            array(blocks.shape[0], width, width),
            array(layers, edges, width),
            array(layers, edges, width),
            array(layers, edges, width),
            array(grids, width),
            array(layers + 1, nodes, width),
            array(nodes, width),
            array(layers, nodes, width),
            array(layers, nodes, width),
            array(layers, nodes, width),
            array(2, chips, rim, width),
            array(2, chips, 8, 128),
            jax.ShapeDtypeStruct((index_rows, edges), jnp.int32),
        ),
        in_specs=[VMEM] * 12,
        out_specs=[ANY] * 5 + [VMEM] * 8,
        scratch_shapes=[
            pltpu.VMEM((2, edges, width), f32),
            pltpu.VMEM((edges, width), f32),
            pltpu.VMEM((edges, width), f32),
            pltpu.VMEM((edges, index_rows), jnp.int32),
            pltpu.VMEM((edges, inputs), bf16),
            pltpu.VMEM((nodes, edges), bf16),
            pltpu.VMEM((inputs, width), bf16),
            pltpu.VMEM((inputs, width), bf16),
            pltpu.VMEM((each, width, width), bf16),
            pltpu.VMEM((each, width, width), bf16),
            pltpu.VMEM((2, width, width), f32),
            pltpu.VMEM((2, chips, rim, width), f32),
            pltpu.VMEM((2, rim, width), f32),
            pltpu.VMEM((8, 128), f32),
            dma((2,)),
            dma((4,)),
            dma,
            dma((groups, rows - 1)),
            dma((groups, rows - 1)),
            dma((groups, 2, rows - 1)),
            dma((groups, 2, rows - 1)),
            dma((groups, 2, rows - 1)),
            dma((groups, 2, rows - 1)),
            dma((groups, rows - 1)),
            dma((groups, rows - 1)),
            dma((5, chips - 1)),
            dma((5, chips - 1)),
            dma((5, chips)),
            dma((5, chips)),
        ],
        compiler_params=pltpu.CompilerParams(
            collective_id=1, has_side_effects=True, vmem_limit_bytes=VMEM_BYTES
        ),
        name="forward",
    )(
        grid,
        edge,
        *indices,
        blocks,
        enc,
        enc_edge,
        params,
    )


def groups(layer):
    return (
        (layer, 0, 0, 3),
        (3 + layer, 0, 4, 3),
        (6 + layer // 2, layer % 2, 3, 1),
    )


class Reducer:
    def __init__(self, bands, layer, at, grads, sib, land, total, sems):
        band, row, self.chip, self.core = place(bands, 1)
        self.row = row
        self.chips = bands // 2
        self.sibling = (self.chip * 2 + 1 - self.core, row)
        self.layer, self.at = layer, at
        self.grads, self.sib, self.land, self.total = grads, sib, land, total
        (self.c_send, self.c_recv, self.r_send, self.r_recv) = sems[:4]
        (self.o_send, self.o_recv, self.p_send, self.p_recv, self.k_sem) = sems[4:]

    def each(self):
        for q, (owner, slot, block, count) in enumerate(groups(self.layer)):
            yield q, owner // 2, owner % 2, slot, pl.ds(block, count), count

    def to_sibling(self, q, rows):
        return remote(
            self.grads.at[rows],
            self.sib.at[rows],
            self.c_send.at[self.at, q],
            self.c_recv.at[self.at, q],
            self.sibling,
        )

    def to_owner(self, q, at_chip, at_core, rows, count):
        step = (at_chip - self.chip + self.chips) % self.chips
        return remote(
            self.grads.at[rows],
            self.land.at[self.at, step - 1, pl.ds(0, count)],
            self.r_send.at[self.at, q],
            self.r_recv.at[self.at, step - 1],
            (at_chip * 2 + at_core, self.row),
        )

    def to_chip(self, q, rows, j):
        return remote(
            self.grads.at[rows],
            self.total.at[rows],
            self.o_send.at[self.at, j - 1],
            self.o_recv.at[self.at, q],
            ((self.chip + j) % self.chips * 2 + self.core, self.row),
        )

    def across(self, q, rows, src):
        return remote(
            src.at[rows],
            self.total.at[rows],
            self.p_send.at[self.at, q],
            self.p_recv.at[self.at, q],
            self.sibling,
        )

    def keep(self, rows):
        return pltpu.make_async_copy(self.grads.at[rows], self.total.at[rows], self.k_sem.at[self.at])

    def start(self):
        for q, at_chip, at_core, slot, rows, count in self.each():
            @pl.when(self.core != at_core)
            def _():
                self.to_sibling(q, rows).start()

    def pair(self):
        for q, at_chip, at_core, slot, rows, count in self.each():
            @pl.when(self.core == at_core)
            def _():
                self.to_sibling(q, rows).wait_recv()
                self.grads[rows] += self.sib[rows]

                @pl.when(self.chip != at_chip)
                def _():
                    self.to_owner(q, at_chip, at_core, rows, count).start()

    def reduce(self, take, load):
        for q, at_chip, at_core, slot, rows, count in self.each():
            @pl.when(jnp.logical_and(self.core == at_core, self.chip == at_chip))
            def _():
                value = self.grads[rows]
                for j in range(1, self.chips):
                    landed = self.land.at[self.at, j - 1, pl.ds(0, count)]
                    remote(
                        landed,
                        landed,
                        self.r_send.at[self.at, q],
                        self.r_recv.at[self.at, j - 1],
                        self.sibling,
                    ).wait_recv()
                    value = value + load(landed, count)
                self.grads[rows] = value
                take(slot, count, value)
                for j in range(1, self.chips):
                    self.to_chip(q, rows, j).start()
                self.across(q, rows, self.grads).start()
                self.keep(rows).start()

    def relay(self):
        for q, at_chip, at_core, slot, rows, count in self.each():
            @pl.when(jnp.logical_and(self.core == at_core, self.chip != at_chip))
            def _():
                self.to_chip(q, rows, 1).wait_recv()
                self.across(q, rows, self.total).start()

    def finish(self):
        for q, at_chip, at_core, slot, rows, count in self.each():
            @pl.when(self.core != at_core)
            def _():
                self.to_sibling(q, rows).wait_send()
                self.across(q, rows, self.total).wait_recv()

            @pl.when(self.core == at_core)
            def _():
                self.across(q, rows, self.total).wait_send()

                @pl.when(self.chip != at_chip)
                def _():
                    self.to_owner(q, at_chip, at_core, rows, count).wait_send()

                @pl.when(self.chip == at_chip)
                def _():
                    for j in range(1, self.chips):
                        self.to_chip(q, rows, j).wait_send()
                    self.keep(rows).wait()


def reducer_sems(count, chips):
    dma = pltpu.SemaphoreType.DMA
    return [
        dma((count, 3)),
        dma((count, 3)),
        dma((count, 3)),
        dma((count, chips - 1)),
        dma((count, chips - 1)),
        dma((count, 3)),
        dma((count, 3)),
        dma((count, 3)),
        dma((count,)),
    ]


class Spreader:
    def __init__(self, bands, at, grads, sib, land, landed, total, sems):
        band, self.row, self.chip, self.core = place(bands, 1)
        self.chips = bands // 2
        self.sibling = (self.chip * 2 + 1 - self.core, self.row)
        self.at = at
        self.grads, self.sib, self.land, self.landed, self.total = grads, sib, land, landed, total
        self.half = grads.shape[1] // 2
        self.piece = self.half // OWNER_CHIPS
        (self.c_sem, self.r_send, self.r_recv, self.o_send, self.o_recv, self.p_sem, self.k_sem) = sems

    def rows(self, core):
        return pl.ds(pl.multiple_of(core * self.half, 8), self.half)

    def part(self, core, chip):
        return pl.ds(pl.multiple_of(core * self.half + chip * self.piece, 8), self.piece)

    def to_sibling(self):
        return remote(
            self.grads.at[:, self.rows(1 - self.core)],
            self.sib,
            self.c_sem.at[self.at, 0],
            self.c_sem.at[self.at, 1],
            self.sibling,
        )

    def to_owner(self, chip):
        step = (chip - self.chip + self.chips) % self.chips
        return remote(
            self.grads.at[:, self.part(self.core, chip)],
            self.land.at[step - 1],
            self.r_send.at[self.at, chip],
            self.r_recv.at[self.at, step - 1],
            (chip * 2 + self.core, self.row),
        )

    def to_chip(self, j, chip):
        part = self.part(self.core, chip)
        return remote(
            self.grads.at[:, part],
            self.total.at[:, part],
            self.o_send.at[self.at, j - 1],
            self.o_recv.at[self.at, chip],
            ((self.chip + j) % self.chips * 2 + self.core, self.row),
        )

    def keep(self):
        part = self.part(self.core, self.chip)
        return pltpu.make_async_copy(
            self.grads.at[:, part], self.total.at[:, part], self.k_sem.at[self.at, 0]
        )

    def across(self, core):
        region = self.total.at[:, self.rows(core)]
        return remote(region, region, self.p_sem.at[self.at, 0], self.p_sem.at[self.at, 1], self.sibling)

    def owned(self, body):
        if self.chips == OWNER_CHIPS:
            body()
        else:
            pl.when(self.chip < OWNER_CHIPS)(body)

    def start(self):
        self.to_sibling().start()

    def pair(self):
        self.to_sibling().wait()
        self.grads[:, self.rows(self.core)] += self.sib[...]
        for chip in range(OWNER_CHIPS):
            pl.when(self.chip != chip)(self.to_owner(chip).start)

    def reduce(self):
        def body():
            part = self.part(self.core, self.chip)
            for j in range(1, self.chips):
                remote(
                    self.landed,
                    self.land.at[j - 1],
                    self.r_send.at[self.at, 0],
                    self.r_recv.at[self.at, j - 1],
                    self.sibling,
                ).wait_recv()
                copy = pltpu.make_async_copy(self.land.at[j - 1], self.landed, self.k_sem.at[self.at, 1])
                copy.start()
                copy.wait()
                self.grads[:, part] += self.landed[...]
            for j in range(1, self.chips):
                self.to_chip(j, self.chip).start()
            self.keep().start()

        self.owned(body)

    def relay(self):
        for chip in range(OWNER_CHIPS):
            pl.when(self.chip != chip)(self.to_chip(1, chip).wait_recv)
        self.owned(lambda: self.keep().wait())
        self.across(self.core).start()

    def finish(self):
        self.across(self.core).wait_send()
        self.across(1 - self.core).wait_recv()
        for chip in range(OWNER_CHIPS):
            pl.when(self.chip != chip)(self.to_owner(chip).wait_send)

        def body():
            for j in range(1, self.chips):
                self.to_chip(j, self.chip).wait_send()

        self.owned(body)


def spreader_sems(count, chips):
    dma = pltpu.SemaphoreType.DMA
    return [
        dma((count, 2)),
        dma((count, OWNER_CHIPS)),
        dma((count, chips - 1)),
        dma((count, chips - 1)),
        dma((count, OWNER_CHIPS)),
        dma((count, 2)),
        dma((count, 2)),
    ]


def backward_kernel(
    bands,
    rows,
    each,
    tile,
    grid_ref,
    target_ref,
    edge_ref,
    index_ref,
    enc_edge_ref,
    dec_ref,
    param_ref,
    full_ref,
    before_ref,
    message_ref,
    edges_ref,
    embed_ref,
    nodes_ref,
    fed_ref,
    agg_ref,
    inner_ref,
    update_ref,
    table_ref,
    count_ref,
    grads_ref,
    small_ref,
    total_ref,
    land_grads,
    edge_buf,
    before_buf,
    message_buf,
    node_buf,
    agg_buf,
    inner_buf,
    update_buf,
    index_t,
    edge_grad,
    node_grad,
    part_high,
    part_low,
    pick_t,
    gather,
    high,
    low,
    stage,
    table,
    sib,
    land,
    grads_buf,
    sib_grads,
    landed_buf,
    stage_sem,
    load_sem,
    d_send,
    d_recv,
    r_send,
    r_recv,
    *sems,
):
    band, row, chip, core = place(bands, rows)
    chips = bands // 2
    layers = param_ref.shape[0]
    nodes, width = node_buf.shape
    edges = edge_buf.shape[0]
    grids = grid_ref.shape[0]
    border = table.shape[2]
    table_rows = bands * border
    rows_dev = grads_ref.shape[1]
    weights = Weights(full_ref, stage, high, low, stage_sem)
    sibling = (chip * 2 + 1 - core, row)
    partners = [((chip + j) % chips * 2 + core, row) for j in range(1, chips)] + [sibling]
    own_rows = pl.ds(pl.multiple_of(row * rows_dev, rows_dev), rows_dev)

    def load(kind, layer):
        src = (before_ref, message_ref, edges_ref, agg_ref, inner_ref, update_ref, nodes_ref)[kind]
        dst = (before_buf, message_buf, edge_buf, agg_buf, inner_buf, update_buf, node_buf)[kind]
        return pltpu.make_async_copy(src.at[layer], dst, load_sem.at[kind])

    table_load = pltpu.make_async_copy(table_ref, table, load_sem.at[7])
    embed_buf = before_buf.at[pl.ds(0, grids)]
    fed_buf = agg_buf
    embed_load = pltpu.make_async_copy(embed_ref, embed_buf, load_sem.at[8])
    fed_load = pltpu.make_async_copy(fed_ref, fed_buf, load_sem.at[9])
    load(6, layers).start()
    table_load.start()
    for kind in range(6):
        load(kind, layers - 1).start()
    meet(partners)

    def to_sibling(e):
        return remote(table.at[1 - core], sib.at[e % 2], d_send.at[e], d_recv.at[e], sibling)

    def to_band(e, j):
        to = (chip + j) % chips
        return remote(
            table.at[core, to], land.at[e % 2, j - 1], r_send.at[e, j - 1], r_recv.at[e, j - 1], (to * 2 + core, row)
        )

    def give(e):
        to_sibling(e).wait()
        table[core] += sib[e % 2]
        for j in range(1, chips):
            to_band(e, j).start()

    def returned(e):
        total = table[core, chip]
        for j in range(1, chips):
            to_band(e, j).wait_recv()
            total = total + land[e % 2, j - 1]
        for j in range(1, chips):
            to_band(e, j).wait_send()
        return picked(hot(iota((nodes, border), 0) == index_ref[BORDER_ROW : BORDER_ROW + 1, pl.ds(0, border)]), total)

    def put_table(value_high, value_low, count):
        side_rows = chips * border
        for side in range(2):
            choice = pick_t[pl.ds(nodes + side * side_rows, side_rows), pl.ds(0, count)]
            table[side] = chosen(choice, value_high, value_low).reshape(chips, border, width)

    def grads_of(layer):
        return grads_buf.at[layer - 1] if layer > 0 else grads_ref

    reducers = [None] + [
        Spreader(
            bands,
            layer - 1,
            grads_of(layer),
            sib_grads,
            land_grads.at[layer - 1],
            landed_buf,
            total_ref.at[pl.ds(layer * each, each)],
            sems,
        )
        for layer in range(1, layers)
    ]

    def put_grad(layer, block, value):
        grads_of(layer)[block] = value

    def add_grad(layer, block, value):
        grads_of(layer)[block] += value

    index_t[...] = index_ref[...].T

    def choose_reads(at, size):
        line = iota((size, grids), 0) + at
        counts = jnp.zeros((size, grids), jnp.float32)
        for way in range(READ_ROW, index_ref.shape[0]):
            counts = counts + jnp.where(line == index_ref[way : way + 1, pl.ds(0, grids)], 1.0, 0.0)
        return counts.astype(jnp.bfloat16)

    def fill_reads(t, carry):
        at = pl.multiple_of(t * 64, 64)
        pick_t[pl.ds(at, 64), pl.ds(0, grids)] = choose_reads(at, 64)
        return carry

    lax.fori_loop(0, (nodes + table_rows) // 64, fill_reads, 0)

    def choose_gather(at, size):
        return hot(iota((size, nodes), 1) == index_t[pl.ds(at, size), RECV_ROW : RECV_ROW + 1])

    fill_rows(gather, choose_gather)
    load(6, layers).wait()
    table_load.wait()
    reads = edge_grad.at[pl.ds(0, grids)]
    own_high, own_low = pieces(node_buf[...])
    reads[...] = chosen(pick_t[pl.ds(0, nodes), pl.ds(0, grids)], own_high, own_low, TN)
    side_rows = chips * border
    for side in range(2):
        side_high, side_low = pieces(table[side].reshape(side_rows, width))
        choice = pick_t[pl.ds(nodes + side * side_rows, side_rows), pl.ds(0, grids)]
        reads[...] += chosen(choice, side_high, side_low, TN)
    load(6, layers - 1).start()
    weights.load((layers - 1) * each, (6, 4, 5, 3, 0, 1, 2))
    active = silu(reads[...])
    mask = index_t[pl.ds(0, grids), MASK_ROW : MASK_ROW + 1].astype(jnp.float32)
    missed = grid_ref[...] + product(active, dec_ref[...]) - target_ref[...]
    total = jnp.sum(jnp.sum(count_ref[:, :, 0:1, 0:1], axis=0), axis=0)
    masked = mask * missed
    loss = jnp.sum(column(masked * missed), axis=1, keepdims=True)
    grad = (2.0 / total) * masked
    encs = grid_ref.shape[1]
    decs = dec_ref.shape[1]
    decoder_at = encs + 8 + layers * 8
    small_ref[pl.ds(decoder_at, decs)] = product(grad, active, TN)
    tail_rows = small_ref.shape[0] - decoder_at - decs
    small_ref[pl.ds(decoder_at + decs, tail_rows)] = jnp.broadcast_to(loss, (tail_rows, width))
    read_high, read_low = pieces(product(grad, dec_ref[...], NT) * silu_back(reads[...]))
    put_table(read_high, read_low, grids)
    to_sibling(0).start()
    node_grad[...] = chosen(pick_t[pl.ds(0, nodes), pl.ds(0, grids)], read_high, read_low)

    def choose(at, size):
        line = iota((size, edges), 0) + at
        sent = line == index_ref[SEND_ROW : SEND_ROW + 1]
        received = line == index_ref[RECV_ROW : RECV_ROW + 1] + (nodes + table_rows)
        return hot(jnp.logical_or(sent, received))

    fill_rows(pick_t, choose, 64)
    give(0)
    edge_grad[...] = jnp.zeros_like(edge_grad)
    node_grad[...] += returned(0)

    for depth in range(layers):
        layer = layers - 1 - depth
        e = depth + 1
        base = encs + 8 + layer * 8

        def put_param(index, value, base=base):
            small_ref[pl.ds(base + index, 1)] = value

        def add_param(index, value, base=base):
            small_ref[pl.ds(base + index, 1)] += value

        for kind in (3, 4, 5, 6):
            load(kind, layer).wait()
        if layer + 1 < layers:
            reducers[layer + 1].pair()
        if layer + 2 < layers:
            reducers[layer + 2].reduce()
        grad = node_grad[...]
        norm, scale = normed(update_buf[...])
        put_param(7, column(grad))
        put_param(6, column(grad * norm))
        grad = normed_back(grad * (1.0 + param_ref[layer, pl.ds(6, 1)]), norm, scale)
        put_param(5, column(grad))
        grad_high, grad_low = pieces(grad)
        put_grad(layer, 6, product(silu(inner_buf[:, own_rows]), grad, TN))
        grad = weights.times(grad_high, grad_low, 6, NT) * silu_back(inner_buf[...])
        put_param(4, column(grad))
        grad_high, grad_low = pieces(grad)
        put_grad(layer, 4, product(node_buf[:, own_rows], grad, TN))
        put_grad(layer, 5, product(agg_buf[:, own_rows], grad, TN))
        node_grad[...] += weights.times(grad_high, grad_low, 4, NT)
        agg_high, agg_low = pieces(weights.times(grad_high, grad_low, 5, NT))
        for kind in (0, 1, 2):
            load(kind, layer).wait()
        for index in range(4):
            put_param(index, jnp.zeros((1, width), jnp.float32))
        for block in (0, 3):
            put_grad(layer, block, jnp.zeros((rows_dev, width), jnp.float32))

        def edge_tile(t, carry):
            at = pl.ds(pl.multiple_of(t * tile, tile), tile)
            grad = edge_grad[at] + chosen(gather[at], agg_high, agg_low)
            edge_grad[at] = grad
            norm, scale = normed(message_buf[at])
            add_param(3, column(grad))
            add_param(2, column(grad * norm))
            grad = normed_back(grad * (1.0 + param_ref[layer, pl.ds(2, 1)]), norm, scale)
            add_param(1, column(grad))
            grad_high, grad_low = pieces(grad)
            add_grad(layer, 3, product(silu(before_buf[at, own_rows]), grad, TN))
            grad = weights.times(grad_high, grad_low, 3, NT) * silu_back(before_buf[at])
            add_param(0, column(grad))
            add_grad(layer, 0, product(edge_buf[at, own_rows], grad, TN))
            grad_high, grad_low = pieces(grad)
            part_high[at] = grad_high
            part_low[at] = grad_low
            return carry

        lax.fori_loop(0, edges // tile, edge_tile, 0)
        if layer > 0:
            for kind in range(6):
                load(kind, layer - 1).start()
        else:
            embed_load.start()
            fed_load.start()
        put_table(part_high[...], part_low[...], edges)
        to_sibling(e).start()
        sender = chosen(pick_t[pl.ds(0, nodes)], part_high[...], part_low[...])
        give(e)
        received = chosen(pick_t[pl.ds(nodes + table_rows, nodes)], part_high[...], part_low[...])

        def edge_back(t, carry):
            at = pl.ds(pl.multiple_of(t * tile, tile), tile)
            edge_grad[at] += weights.times(part_high[at], part_low[at], 0, NT)
            return carry

        lax.fori_loop(0, edges // tile, edge_back, 0)
        put_grad(layer, 2, product(node_buf[:, own_rows], received, TN))
        node_grad[...] += weights.apply(received, 2, NT)
        if layer > 0:
            weights.load((layer - 1) * each, (6, 4, 5, 3, 0))
        sender = sender + returned(e)
        put_grad(layer, 1, product(node_buf[:, own_rows], sender, TN))
        node_grad[...] += weights.apply(sender, 1, NT)
        if layer > 0:
            load(6, layer - 1).start()
            weights.load((layer - 1) * each, (1, 2))
            reducers[layer].start()

    reducers[1].reduce()
    embed_load.wait()
    fed_load.wait()
    norm, scale = normed(fed_buf[...])
    fed_grad = normed_back(node_grad[...], norm, scale)
    feed = hot(iota((grids, nodes), 1) == index_t[pl.ds(0, grids), FEED_ROW : FEED_ROW + 1])
    grad = picked(feed, fed_grad) * silu_back(embed_buf[...])
    small_ref[pl.ds(0, encs)] = product(grid_ref[...], grad, TN)
    small_ref[pl.ds(encs, 8)] = jnp.zeros((8, width), jnp.float32)

    def embed_tile(t, carry):
        at = pl.ds(pl.multiple_of(t * tile, tile), tile)
        grad = edge_grad[at] * silu_back(product(edge_ref[at], enc_edge_ref[...]))
        small_ref[pl.ds(encs, 8)] += product(edge_ref[at], grad, TN)[:8]
        return carry

    lax.fori_loop(0, edges // tile, embed_tile, 0)
    for layer in range(layers - 1, 0, -1):
        reducers[layer].relay()
    for layer in range(1, layers):
        reducers[layer].finish()


def backward(bands, rows, rim, rows_dev, inputs, saved):
    f32, bf16 = jnp.float32, jnp.bfloat16
    dma = pltpu.SemaphoreType.DMA
    grid, edge, index, decoder, params = inputs[0], inputs[2], inputs[3], inputs[5], inputs[6]
    layers = params.shape[0]
    full = saved[0]
    width = full.shape[2]
    each = full.shape[0] // layers
    edges, grids = edge.shape[0], grid.shape[0]
    nodes = NODE_DEV
    chips = bands // 2
    decs = decoder.shape[1]
    small = grid.shape[1] + 8 + layers * 8 + decs + 8
    small = -(-small // (16 * OWNER_CHIPS)) * 16 * OWNER_CHIPS
    tile = edges // 2
    node = pltpu.VMEM((nodes, width), f32)
    return pl.pallas_call(
        functools.partial(backward_kernel, bands, rows, each, tile),
        out_shape=(
            jax.ShapeDtypeStruct((each, rows_dev, width), f32),
            jax.ShapeDtypeStruct((small, width), f32),
            jax.ShapeDtypeStruct((full.shape[0], rows_dev, width), f32),
            jax.ShapeDtypeStruct((layers - 1, chips - 1, each, rows_dev // 8, width), f32),
        ),
        in_specs=[VMEM] * 7 + [ANY] * 11 + [VMEM],
        out_specs=[VMEM, VMEM, ANY, ANY],
        scratch_shapes=[
            pltpu.VMEM((edges, width), f32),
            pltpu.VMEM((edges, width), f32),
            pltpu.VMEM((edges, width), f32),
            node,
            node,
            node,
            node,
            pltpu.VMEM((edges, index.shape[0]), jnp.int32),
            pltpu.VMEM((edges, width), f32),
            node,
            pltpu.VMEM((edges, width), bf16),
            pltpu.VMEM((edges, width), bf16),
            pltpu.VMEM((2 * nodes + bands * rim, edges), bf16),
            pltpu.VMEM((edges, nodes), bf16),
            pltpu.VMEM((each, width, width), bf16),
            pltpu.VMEM((each, width, width), bf16),
            pltpu.VMEM((2, width, width), f32),
            pltpu.VMEM((2, chips, rim, width), f32),
            pltpu.VMEM((2, chips, rim, width), f32),
            pltpu.VMEM((2, chips - 1, rim, width), f32),
            pltpu.VMEM((layers - 1, each, rows_dev, width), f32),
            pltpu.VMEM((each, rows_dev // 2, width), f32),
            pltpu.VMEM((each, rows_dev // 8, width), f32),
            dma((2,)),
            dma((10,)),
            dma((layers + 1,)),
            dma((layers + 1,)),
            dma((layers + 1, chips - 1)),
            dma((layers + 1, chips - 1)),
            ]
        + spreader_sems(layers - 1, chips),
        compiler_params=pltpu.CompilerParams(
            collective_id=2, has_side_effects=True, vmem_limit_bytes=VMEM_BYTES
        ),
        name="backward",
    )(*inputs, *saved)


def newton(mom_ref, out_ref, first, count, gram, poly, temp, later):
    def add_square(i, total):
        block = mom_ref[first + i]
        return total + jnp.sum(jnp.sum(block * block, axis=0, keepdims=True), axis=1, keepdims=True)

    total = lax.fori_loop(0, count, add_square, jnp.zeros((1, 1), jnp.float32))
    scale = 1.0 / (jnp.sqrt(total) + 1e-07)
    gram[...] = jnp.zeros_like(gram)

    def add_gram(i, carry):
        block = mom_ref[first + i] * scale
        mom_ref[first + i] = block
        gram[...] += product(block, block, TN)
        return carry

    lax.fori_loop(0, count, add_gram, 0)
    poly[...] = coef_b * gram[...] + coef_c * product(gram[...], gram[...])
    temp[...] = coef_a * gram[...] + product(gram[...], poly[...])
    gram[...] = coef_a * temp[...] + product(temp[...], poly[...])
    later[...] = coef_b * gram[...] + coef_c * product(gram[...], gram[...])
    temp[...] = coef_a * (poly[...] + later[...]) + product(poly[...], later[...])

    def finish(i, carry):
        block = mom_ref[first + i]
        out_ref[first + i] = (coef_a * coef_a) * block + product(block, temp[...])
        return carry

    lax.fori_loop(0, count, finish, 0)


def late_slot(owner, slot):
    return owner in (0, 3) or (owner == 6 and slot == 0)


def tail_kernel(
    bands,
    rows,
    grads_ref,
    small_ref,
    mom_ref,
    given_ref,
    total_ref,
    ortho_ref,
    shared_ref,
    land,
    grads,
    sib,
    landed_buf,
    sib_small,
    part_small,
    land_small,
    held,
    matrix,
    result,
    back,
    gram,
    poly,
    temp,
    later,
    load_sem,
    landed_sem,
    m_pair,
    m_red_send,
    m_red_recv,
    m_out_send,
    m_out_recv,
    m_pass,
    m_keep,
    up_send,
    up_recv,
    down_send,
    down_recv,
    o_send,
    o_recv,
    p_send,
    p_recv,
    keep_sem,
    *sems,
):
    band, row, chip, core = place(bands, rows)
    chips = bands // 2
    rows_dev = held.shape[1]
    sibling = (chip * 2 + 1 - core, row)
    partners = [((chip + j) % chips * 2 + core, row) for j in range(1, chips)] + [sibling]
    partners += [(band, (row + j) % rows) for j in range(1, rows)]
    reducer = Reducer(bands, 0, 0, grads, sib.at[0], land, total_ref.at[pl.ds(0, grads.shape[0])], sems)
    grads[...] = grads_ref[...]

    def load(slot):
        return pltpu.make_async_copy(
            mom_ref.at[slot_block(band, slot)], held.at[slot], load_sem.at[slot]
        )

    owned = [band < (8, 7, 6)[slot] for slot in range(SLOTS)]
    third = band // 3
    last = [jnp.logical_and(band < 7, band % 3 == 0)]
    last += [jnp.logical_and(band < 6, band % 3 == 0)] * 2
    for slot in range(SLOTS):
        pl.when(owned[slot])(load(slot).start)
    meet(partners)

    small_pair = remote(small_ref.at[1 - core], sib_small, m_pair.at[0], m_pair.at[1], sibling)

    def small_to(at):
        step = (at - chip + chips) % chips
        return remote(
            part_small.at[at],
            land_small.at[step - 1],
            m_red_send.at[at],
            m_red_recv.at[step - 1],
            (at * 2 + core, row),
        )

    def small_out(at, j):
        home = shared_ref.at[core * OWNER_CHIPS + at]
        return remote(
            part_small.at[at],
            home,
            m_out_send.at[j - 1],
            m_out_recv.at[at],
            ((chip + j) % chips * 2 + core, row),
        )

    def small_across(at, of_core, local):
        home = shared_ref.at[of_core * OWNER_CHIPS + at]
        return remote(
            part_small.at[at] if local else home, home, m_pass.at[0, at], m_pass.at[1, at], sibling
        )

    def small_keep(at):
        return pltpu.make_async_copy(
            part_small.at[at], shared_ref.at[core * OWNER_CHIPS + at], m_keep
        )

    row_a = rows // 2 - 1 + core
    row_b = rows // 2 - core
    split_at = 3 - third

    def home(slot):
        if slot == 0:
            return row_a
        return row_a + (slot + third) // 3 * (row_b - row_a)

    def rows_of(at_row):
        return pl.ds(pl.multiple_of(at_row * rows_dev, rows_dev), rows_dev)

    def up(slot, from_row):
        step = (from_row - home(slot) + rows) % rows
        return remote(
            held.at[slot],
            matrix.at[slot, rows_of(from_row)],
            up_send.at[slot],
            up_recv.at[slot, step],
            (band, home(slot)),
        )

    def down(slot, to_row):
        step = (to_row - home(slot) + rows) % rows
        return remote(
            result.at[slot, rows_of(to_row)],
            back.at[slot],
            down_send.at[slot, step],
            down_recv.at[slot],
            (band, to_row),
        )

    def momentum(slot, value):
        load(slot).wait()
        held[slot] = momentum_decay * held[slot] + value

        @pl.when(row == home(slot))
        def _():
            matrix[slot, rows_of(row)] = held[slot]

        @pl.when(row != home(slot))
        def _():
            up(slot, row).start()

    def solve(when):
        own_b = jnp.logical_and(row == row_b, jnp.logical_and(band > 2, band < 7))
        own_b = jnp.logical_and(own_b, jnp.logical_not(band == 3) if when == 0 else band == 3)
        own_a = jnp.logical_and(row == row_a, band < 8)
        own_a = jnp.logical_and(own_a, jnp.logical_not(last[0]) if when == 0 else last[0])

        @pl.when(jnp.logical_or(own_a, own_b))
        def _():
            second = (row - row_a) * (row_b - row_a)
            first = second * split_at
            count = (1 - second) * split_at + second
            for slot in range(SLOTS):
                @pl.when(jnp.logical_and(slot >= first, slot < first + count))
                def _():
                    for step in range(1, rows):
                        up(slot, (row + step) % rows).wait_recv()

            newton(matrix, result, first, count, gram, poly, temp, later)
            for slot in range(SLOTS):
                @pl.when(jnp.logical_and(slot >= first, slot < first + count))
                def _():
                    for step in range(1, rows):
                        down(slot, (row + step) % rows).start()
                    back[slot] = result[slot, rows_of(row)]

    units = [
        (owner, slot)
        for owner in range(2 * OWNER_CHIPS)
        for slot in range(SLOTS)
        if slot_used(owner, slot)
    ]

    def target(owner, slot):
        return ortho_ref.at[slot_block(owner, slot)]

    def out(owner, slot, j):
        return remote(
            back.at[slot],
            target(owner, slot),
            o_send.at[slot, j - 1],
            o_recv.at[owner // 2, slot],
            ((chip + j) % chips * 2 + core, row),
        )

    def across(owner, slot, local):
        return remote(
            back.at[slot] if local else target(owner, slot),
            target(owner, slot),
            p_send.at[owner // 2, slot],
            p_recv.at[owner // 2, slot],
            sibling,
        )

    def keep(owner, slot):
        return pltpu.make_async_copy(back.at[slot], target(owner, slot), keep_sem.at[slot])

    def publish(when):
        for owner, slot in units:
            if late_slot(owner, slot) != (when == 1):
                continue

            @pl.when(band == owner)
            def _():
                @pl.when(row != home(slot))
                def _():
                    down(slot, row).wait_recv()

                for j in range(1, chips):
                    out(owner, slot, j).start()
                across(owner, slot, True).start()
                keep(owner, slot).start()

    def relay(when):
        for owner, slot in units:
            if late_slot(owner, slot) != (when == 1):
                continue

            @pl.when(jnp.logical_and(core == owner % 2, chip != owner // 2))
            def _():
                out(owner, slot, 1).wait_recv()
                across(owner, slot, False).start()

    reducer.start()
    small_pair.start()
    for slot in range(SLOTS):
        @pl.when(jnp.logical_and(owned[slot], jnp.logical_not(last[slot])))
        def _():
            ready = pltpu.make_async_copy(
                total_ref.at[slot_block(band, slot)], back.at[slot], load_sem.at[SLOTS + slot]
            )
            ready.start()
            ready.wait()
            momentum(slot, back[slot])

    reducer.pair()
    small_pair.wait()
    part_small[...] = small_ref[core] + sib_small[...]
    for at in range(OWNER_CHIPS):
        pl.when(chip != at)(small_to(at).start)
    solve(0)

    def take(slot, count, value):
        for n in range(count):
            momentum(slot + n, value[n])

    def load_landed(src, count):
        dst = landed_buf.at[pl.ds(0, count)]
        copy = pltpu.make_async_copy(src, dst, landed_sem)
        copy.start()
        copy.wait()
        return dst[...]

    reducer.reduce(take, load_landed)
    for at in range(OWNER_CHIPS):
        @pl.when(chip == at)
        def _():
            for j in range(1, chips):
                remote(
                    land_small.at[j - 1],
                    land_small.at[j - 1],
                    m_red_send.at[at],
                    m_red_recv.at[j - 1],
                    sibling,
                ).wait_recv()
                part_small[at] += land_small[j - 1]
            for j in range(1, chips):
                small_out(at, j).start()
            small_across(at, core, True).start()
            small_keep(at).start()

    publish(0)
    solve(1)
    reducer.relay()
    for at in range(OWNER_CHIPS):
        @pl.when(chip != at)
        def _():
            small_out(at, 1).wait_recv()
            small_across(at, core, False).start()

    publish(1)
    relay(0)
    relay(1)
    reducer.finish()
    for at in range(OWNER_CHIPS):
        small_across(at, core, False).wait_send()
        small_across(at, 1 - core, False).wait_recv()

        @pl.when(chip != at)
        def _():
            small_to(at).wait_send()

        @pl.when(chip == at)
        def _():
            for j in range(1, chips):
                small_out(at, j).wait_send()
            small_keep(at).wait()

    for owner, slot in units:
        @pl.when(core == owner % 2)
        def _():
            across(owner, slot, False).wait_send()

        @pl.when(core != owner % 2)
        def _():
            across(owner, slot, False).wait_recv()

        @pl.when(band == owner)
        def _():
            for j in range(1, chips):
                out(owner, slot, j).wait_send()
            keep(owner, slot).wait()

            @pl.when(row != home(slot))
            def _():
                up(slot, row).wait_send()

            @pl.when(row == home(slot))
            def _():
                for step in range(1, rows):
                    down(slot, (row + step) % rows).wait_send()


def tail(bands, rows, grads, small, momentum, given):
    blocks, rows_dev, width = momentum.shape
    each = grads.shape[0]
    chips = bands // 2
    chunk = small.shape[2]
    f32 = jnp.float32
    dma = pltpu.SemaphoreType.DMA
    square = pltpu.VMEM((width, width), f32)
    slots = pltpu.VMEM((SLOTS, rows_dev, width), f32)
    return pl.pallas_call(
        functools.partial(tail_kernel, bands, rows),
        out_shape=(
            jax.ShapeDtypeStruct(given.shape, f32),
            jax.ShapeDtypeStruct((blocks, rows_dev, width), f32),
            jax.ShapeDtypeStruct((2 * OWNER_CHIPS, chunk, width), f32),
            jax.ShapeDtypeStruct((1, chips - 1, SLOTS, rows_dev, width), f32),
        ),
        in_specs=[VMEM, VMEM, ANY, ANY],
        out_specs=[ANY, ANY, ANY, ANY],
        input_output_aliases={3: 0},
        scratch_shapes=[
            pltpu.VMEM((each, rows_dev, width), f32),
            pltpu.VMEM((1, each, rows_dev, width), f32),
            slots,
            pltpu.VMEM((OWNER_CHIPS, chunk, width), f32),
            pltpu.VMEM((OWNER_CHIPS, chunk, width), f32),
            pltpu.VMEM((chips - 1, chunk, width), f32),
            slots,
            pltpu.VMEM((SLOTS, width, width), f32),
            pltpu.VMEM((SLOTS, width, width), f32),
            slots,
            square,
            square,
            square,
            square,
            dma((2 * SLOTS,)),
            dma,
            dma((2,)),
            dma((OWNER_CHIPS,)),
            dma((chips - 1,)),
            dma((chips - 1,)),
            dma((OWNER_CHIPS,)),
            dma((2, OWNER_CHIPS)),
            dma,
            dma((SLOTS,)),
            dma((SLOTS, rows)),
            dma((SLOTS, rows)),
            dma((SLOTS,)),
            dma((SLOTS, chips - 1)),
            dma((OWNER_CHIPS, SLOTS)),
            dma((OWNER_CHIPS, SLOTS)),
            dma((OWNER_CHIPS, SLOTS)),
            dma((SLOTS,)),
        ]
        + reducer_sems(1, chips),
        compiler_params=pltpu.CompilerParams(
            collective_id=0, has_side_effects=True, vmem_limit_bytes=VMEM_BYTES
        ),
        name="tail",
    )(grads, small, momentum, given)


def finish_kernel(
    shapes,
    channels,
    edge_channels,
    w_ref,
    average_ref,
    mom_ref,
    total_ref,
    ortho_ref,
    small_ref,
    count_ref,
    enc_ref,
    enc_first_ref,
    enc_second_ref,
    dec_ref,
    dec_first_ref,
    dec_second_ref,
    param_ref,
    param_first_ref,
    param_second_ref,
    loss_ref,
    total_count_ref,
    new_w_ref,
    new_mom_ref,
    new_average_ref,
    enc_outs,
    dec_outs,
    param_outs,
):
    wide, params_at, decoder_at, loss_at = shapes
    step = pl.program_id(0)
    for n in range(w_ref.shape[0]):
        block = lax.rem(step * w_ref.shape[0] + n, len(block_scale))
        scale = jnp.where(block < 3, block_scale[0], jnp.where(block == 4, block_scale[4], 1.0))
        scale = jnp.where(block == 5, block_scale[5], scale)
        fresh = w_ref[n] * (1.0 - muon_rate * weight_decay) - (muon_rate * scale) * ortho_ref[n]
        new_w_ref[n] = fresh
        new_average_ref[n] = average_decay * average_ref[n] + (1.0 - average_decay) * fresh
        new_mom_ref[n] = momentum_decay * mom_ref[n] + total_ref[n]

    def put(outs, at, values):
        for ref, value in zip(outs, values):
            ref[at] = value

    @pl.when(step == 0)
    def _():
        for at, grad in (
            (pl.ds(0, channels), small_ref[pl.ds(0, channels)]),
            (pl.ds(channels, edge_channels), small_ref[pl.ds(wide, edge_channels)]),
        ):
            put(enc_outs, at, adam_update(enc_ref[at], enc_first_ref[at], enc_second_ref[at], grad, adam_rate))
        grad = small_ref[pl.ds(decoder_at, channels)]
        put(dec_outs, ..., adam_update(dec_ref[...], dec_first_ref[...], dec_second_ref[...], grad, adam_rate))
        for layer in range(param_ref.shape[0]):
            grad = small_ref[pl.ds(params_at + layer * 8, 8)]
            put(
                param_outs,
                layer,
                adam_update(param_ref[layer], param_first_ref[layer], param_second_ref[layer], grad, param_rate),
            )
        loss_ref[...] = small_ref[pl.ds(loss_at, 1), 0:1]
        total_count_ref[...] = jnp.sum(jnp.sum(count_ref[:, :, 0:1, 0:1], axis=0), axis=0)


def finish(shapes, edge_channels, blocks, small, counts, encoder, decoder, params):
    f32 = jnp.float32
    channels = decoder[0].shape[0]
    big = blocks[0]
    tiled = pl.BlockSpec((SLOTS,) + big.shape[1:], lambda i: (i, 0, 0))

    def whole(value):
        return pl.BlockSpec(value.shape, lambda i: (0,) * value.ndim)

    def like(value):
        return jax.ShapeDtypeStruct(value.shape, f32)

    scalar = jax.ShapeDtypeStruct((1, 1), f32)
    return pl.pallas_call(
        functools.partial(finish_kernel, shapes, channels, edge_channels),
        grid=(big.shape[0] // SLOTS,),
        out_shape=(
            scalar,
            scalar,
            like(big),
            like(big),
            like(big),
            (like(encoder[0]),) * 3,
            (like(decoder[0]),) * 3,
            (like(params[0]),) * 3,
        ),
        in_specs=[tiled] * 5 + [whole(value) for value in (small, counts, *encoder, *decoder, *params)],
        out_specs=(
            whole(scalar),
            whole(scalar),
            tiled,
            tiled,
            tiled,
            (whole(encoder[0]),) * 3,
            (whole(decoder[0]),) * 3,
            (whole(params[0]),) * 3,
        ),
        compiler_params=pltpu.CompilerParams(vmem_limit_bytes=VMEM_BYTES),
        name="finish",
    )(*blocks, small, counts, *encoder, *decoder, *params)


def adam_update(values, first, second, gradient, rate):
    first = beta_one * first + (1.0 - beta_one) * gradient
    second = beta_two * second + (1.0 - beta_two) * gradient * gradient
    corrected = (
        first / (1.0 - beta_one**STEP) / (jnp.sqrt(second / (1.0 - beta_two**STEP)) + adam_eps)
    )
    return (first, second, values * (1.0 - rate * weight_decay) - rate * corrected)


def body(
    grid_input,
    grid_target,
    edge_input,
    senders,
    receivers,
    border_nodes,
    grid_to_mesh,
    mesh_to_grid,
    loss_mask,
    encoder_weights,
    encoder_first,
    encoder_second,
    processor_weights,
    processor_momentum,
    processor_average,
    norm_params,
    norm_first,
    norm_second,
    decoder_weights,
    decoder_first,
    decoder_second,
):
    bands, rows = lax.axis_size("band"), lax.axis_size("row")
    layers, blocks, rows_dev, width = processor_weights.shape
    channels = grid_input.shape[1]
    edge_channels = edge_input.shape[1]
    wide = -(-channels // 128) * 128
    grids, rim = grid_input.shape[0], border_nodes.shape[0]

    def widen(value, size, axis):
        pads = [(0, 0), (0, 0)]
        pads[axis] = (0, size - value.shape[axis])
        return jnp.pad(value, pads)

    reads = mesh_to_grid.reshape(grids, -1).T
    indices = tuple(
        value[None, :] for value in (senders, receivers, border_nodes, grid_to_mesh, loss_mask)
    ) + (reads,)
    grid_wide = widen(grid_input, wide, 1)
    edge_wide = widen(edge_input, 128, 1)
    edge_embed = widen(encoder_weights[channels:], 128, 0)
    flat_weights = processor_weights.reshape(layers * blocks, rows_dev, width)
    *saved, index = forward(
        bands,
        rows,
        grid_wide,
        edge_wide,
        indices,
        flat_weights,
        widen(encoder_weights[:channels], wide, 0),
        edge_embed,
        norm_params,
    )
    inputs = (
        grid_wide,
        widen(grid_target, wide, 1),
        edge_wide,
        index,
        edge_embed,
        widen(decoder_weights, wide, 1),
        norm_params,
    )
    grads, small, total, _ = backward(bands, rows, rim, rows_dev, inputs, saved)
    flat_momentum = processor_momentum.reshape(layers * blocks, rows_dev, width)
    total, ortho, small, _ = tail(
        bands,
        rows,
        grads,
        small.reshape(2, OWNER_CHIPS, -1, width),
        flat_momentum,
        total,
    )
    params_at = wide + 8
    decoder_at = params_at + layers * 8
    loss_total, mask_count, next_weights, next_momentum, next_average, encoder, decoder, params = finish(
        (wide, params_at, decoder_at, decoder_at + wide),
        edge_channels,
        (flat_weights, processor_average.reshape(flat_momentum.shape), flat_momentum, total, ortho),
        small.reshape(-1, width),
        saved[-1],
        (encoder_weights, encoder_first, encoder_second),
        (decoder_weights.T, decoder_first.T, decoder_second.T),
        (norm_params, norm_first, norm_second),
    )
    encoder_moment, encoder_square, encoder_values = encoder
    decoder_moment, decoder_square, decoder_values = (value.T for value in decoder)
    param_moment, param_square, param_values = params
    loss_total, mask_count = loss_total[0, 0], mask_count[0, 0]
    next_weights, next_momentum, next_average = (
        value.reshape(processor_weights.shape) for value in (next_weights, next_momentum, next_average)
    )
    return (
        loss_total,
        mask_count,
        next_weights,
        next_momentum,
        next_average,
        param_moment,
        param_square,
        param_values,
        encoder_moment,
        encoder_square,
        encoder_values,
        decoder_moment,
        decoder_square,
        decoder_values,
    )


def solution(mesh):
    return jax.shard_map(
        body,
        mesh=mesh,
        in_specs=(
            P("band", None),
            P("band", None),
            P("band", None),
            P("band"),
            P("band"),
            P("band"),
            P("band"),
            P("band"),
            P("band"),
            P(),
            P(),
            P(),
            P(None, None, "row", None),
            P(None, None, "row", None),
            P(None, None, "row", None),
            P(),
            P(),
            P(),
            P(),
            P(),
            P(),
        ),
        out_specs=(
            P(),
            P(),
            P(None, None, "row", None),
            P(None, None, "row", None),
            P(None, None, "row", None),
            P(),
            P(),
            P(),
            P(),
            P(),
            P(),
            P(),
            P(),
            P(),
        ),
        check_vma=False,
    )
```

```python
import functools

import jax
import jax.numpy as jnp
from jax import lax
from jax.experimental import pallas as pl
from jax.experimental.pallas import tpu as pltpu
from jax.sharding import PartitionSpec as P

STEP = 10
NODE_DEV = 320


coef_a = 3.4445
coef_b = -4.775
coef_c = 2.0315
momentum_decay = 0.95
muon_rate = 0.3
adam_rate = 0.02
param_rate = 0.1
beta_one = 0.9
beta_two = 0.95
adam_eps = 1e-08
weight_decay = 0.01
average_decay = 0.9
block_scale = (3.0**0.5, 3.0**0.5, 3.0**0.5, 1.0, 2.0**0.5, 2.0**0.5, 1.0)


MESH = pl.DeviceIdType.MESH
NN = (((1,), (0,)), ((), ()))
NT = (((1,), (1,)), ((), ()))
TN = (((0,), (0,)), ((), ()))
OWNER_CHIPS = 4
SLOTS = 3
VMEM_BYTES = 62 * 2**20
ANY = pl.BlockSpec(memory_space=pl.ANY)
VMEM = pl.BlockSpec(memory_space=pltpu.VMEM)


def pieces(value):
    high = value.astype(jnp.bfloat16)
    return high, (value - high.astype(jnp.float32)).astype(jnp.bfloat16)


def dot(left, right, dims=NN):
    return lax.dot_general(left, right, dims, preferred_element_type=jnp.float32)


def product(left, right, dims=NN):
    left_high, left_low = pieces(left)
    right_high, right_low = pieces(right)
    return (
        dot(left_high, right_high, dims)
        + dot(left_low, right_high, dims)
        + dot(left_high, right_low, dims)
    )


def slot_block(owner, slot):
    third = owner // 3
    last = third // 2
    return (1 - last) * (7 * (owner % 3) + 4 * third + slot) + last * (
        3 + 14 * (owner - 6) + 7 * slot
    )


def slot_used(owner, slot):
    return owner < (8, 7, 6)[slot]


def remote(src, dst, send_sem, recv_sem, device):
    return pltpu.make_async_remote_copy(
        src_ref=src,
        dst_ref=dst,
        send_sem=send_sem,
        recv_sem=recv_sem,
        device_id=device,
        device_id_type=MESH,
    )


def silu(value):
    return value / (1.0 + jnp.exp(-value))


def silu_back(value):
    gate = 1.0 / (1.0 + jnp.exp(-value))
    return gate * (1.0 + value * (1.0 - gate))


def normed(value):
    centered = value - jnp.mean(value, axis=-1, keepdims=True)
    scale = lax.rsqrt(jnp.mean(centered * centered, axis=-1, keepdims=True) + 1e-05)
    return centered * scale, scale


def normed_back(grad, norm, scale):
    inner = jnp.mean(grad * norm, axis=-1, keepdims=True)
    return (grad - jnp.mean(grad, axis=-1, keepdims=True) - norm * inner) * scale


def column(value):
    return jnp.sum(value, axis=0, keepdims=True)


def hot(mask):
    return jnp.where(mask, 1.0, 0.0).astype(jnp.bfloat16)


def chosen(choice, high, low, dims=NN):
    return dot(choice, high, dims) + dot(choice, low, dims)


def picked(choice, value):
    high, low = pieces(value)
    return chosen(choice, high, low)


def fill_rows(out_ref, make, tile=128):
    def step(t, carry):
        at = pl.multiple_of(t * tile, tile)
        out_ref[pl.ds(at, tile)] = make(at, tile)
        return carry

    lax.fori_loop(0, out_ref.shape[0] // tile, step, 0)


def iota(shape, axis):
    return lax.broadcasted_iota(jnp.int32, shape, axis)


SEND_ROW, RECV_ROW, BORDER_ROW, FEED_ROW, MASK_ROW, READ_ROW = range(6)


def edge_rows(edge_ref, size):
    empty = jnp.zeros((size - edge_ref.shape[0], edge_ref.shape[1]), jnp.float32)
    return jnp.concatenate([edge_ref[...], empty], axis=0)


def embedded_edges(edge_t, enc_ref, first, count, at, size):
    total = edge_t[pl.ds(at, size), 0:1] * enc_ref[pl.ds(first, 1)]
    for n in range(1, count):
        total = total + edge_t[pl.ds(at, size), n : n + 1] * enc_ref[pl.ds(first + n, 1)]
    return total


class Weights:
    def __init__(self, full_ref, stage, high, low, sem):
        self.full, self.stage, self.high, self.low, self.sem = full_ref, stage, high, low, sem

    def copy(self, block, slot):
        return pltpu.make_async_copy(self.full.at[block], self.stage.at[slot], self.sem.at[slot])

    def load(self, first, blocks):
        for n, block in enumerate(blocks[:2]):
            self.copy(first + block, n % 2).start()
        for n, block in enumerate(blocks):
            self.copy(first + block, n % 2).wait()
            high, low = pieces(self.stage[n % 2])
            self.high[block] = high
            self.low[block] = low
            if n + 2 < len(blocks):
                self.copy(first + blocks[n + 2], n % 2).start()

    def times(self, high, low, block, dims=NN):
        weight = self.high[block]
        return dot(high, weight, dims) + dot(low, weight, dims) + dot(high, self.low[block], dims)

    def apply(self, value, block, dims=NN):
        high, low = pieces(value)
        return self.times(high, low, block, dims)


def place(bands, rows):
    band = lax.axis_index("band")
    row = lax.axis_index("row")
    return band, row, band // 2, band % 2


def meet(partners):
    barrier = pltpu.get_barrier_semaphore()
    for partner in partners:
        pl.semaphore_signal(barrier, inc=1, device_id=partner, device_id_type=MESH)
    pl.semaphore_wait(barrier, len(partners))


def forward_kernel(
    bands,
    rows,
    chunks,
    tile,
    grid_ref,
    edge_ref,
    ends_ref,
    border_ref,
    feed_ref,
    mask_ref,
    read_ref,
    w_ref,
    enc_ref,
    param_ref,
    full_ref,
    before_ref,
    message_ref,
    edges_ref,
    embed_ref,
    nodes_ref,
    fed_ref,
    agg_ref,
    inner_ref,
    update_ref,
    table_ref,
    count_ref,
    index_ref,
    edge_buf,
    before_buf,
    message_buf,
    index_t,
    edge_t,
    pick,
    gather_t,
    src_high,
    src_low,
    high,
    low,
    stage,
    table,
    border_buf,
    count_buf,
    stage_sem,
    save_sem,
    own_sem,
    z_send,
    z_recv,
    a_send,
    a_recv,
    b_send,
    b_recv,
    s_send,
    s_recv,
    x_send,
    x_recv,
    p_send,
    p_recv,
):
    band, row, chip, core = place(bands, rows)
    chips = bands // 2
    layers, blocks = agg_ref.shape[0], w_ref.shape[0] // agg_ref.shape[0]
    rows_dev = w_ref.shape[1]
    nodes, width = fed_ref.shape
    edges = edge_buf.shape[1]
    border = border_buf.shape[1]
    grids = grid_ref.shape[1]
    weights = Weights(full_ref, stage, high, low, stage_sem)
    quad, pos = chip // 4, chip % 4
    pos_x, pos_y = pos + 1 - 2 * (pos % 2), pos + 2 - 4 * (pos // 2)
    sibling = (chip * 2 + 1 - core, row)
    near = (((quad * 4 + pos_x) * 2 + core, row), ((quad * 4 + pos_y) * 2 + core, row))
    near_pos = (pos_x, pos_y)
    partners = [((chip + j) % chips * 2 + core, row) for j in range(1, chips)] + [sibling]
    partners += [(band, (row + j) % rows) for j in range(1, rows)]
    meet(partners)

    piece = rows_dev // 8

    def part(g, from_row, of_core, of_pos, first=0, size=None):
        start, count = chunks[g]
        size = piece if size is None else size
        at = from_row * rows_dev + (of_core * 4 + of_pos) * piece + first
        return full_ref.at[pl.ds(start, count), pl.ds(pl.multiple_of(at, 8), size)]

    def z_copy(g, j, from_row):
        start, count = chunks[g]
        at = pl.multiple_of((core * 4 + pos) * piece, 8)
        return remote(
            w_ref.at[pl.ds(start, count), pl.ds(at, piece)],
            part(g, from_row, core, pos),
            z_send.at[g, j - 1],
            z_recv.at[g, j - 1],
            (band, (from_row + j) % rows),
        )

    def a_copy(g, side, j, of_pos):
        region = part(g, (row - j + rows) % rows, core, of_pos)
        return remote(region, region, a_send.at[g, side, j - 1], a_recv.at[g, side, j - 1], near[side])

    def b_copy(g, side, j, of_pos):
        half = piece // 2
        region = part(g, (row - j + rows) % rows, core, of_pos, side * half, half)
        return remote(region, region, b_send.at[g, side, j - 1], b_recv.at[g, side, j - 1], near[side])

    def s_copy(g, j, of_core):
        region = part(g, (row - j + rows) % rows, of_core, 0, 0, 4 * piece)
        return remote(region, region, s_send.at[g, j - 1], s_recv.at[g, j - 1], sibling)

    others = range(1, rows)
    far = 3 - pos

    def start_z(g):
        for j in others:
            z_copy(g, j, row).start()

    def start_a(g):
        for j in others:
            z_copy(g, j, (row - j + rows) % rows).wait_recv()
            for side in range(2):
                a_copy(g, side, j, pos).start()

    def start_b(g):
        for j in others:
            for side in range(2):
                a_copy(g, side, j, near_pos[side]).wait_recv()
                b_copy(g, 1 - side, j, near_pos[side]).start()

    def start_s(g):
        for j in others:
            for side in range(2):
                b_copy(g, side, j, far).wait_recv()
            s_copy(g, j, core).start()

    def ready(g):
        for j in others:
            s_copy(g, j, 1 - core).wait_recv()

    def tick(t):
        for g, stage_of in ((t - 5, ready), (t - 4, start_s), (t - 3, start_b), (t - 1, start_a), (t + 1, start_z)):
            if 0 <= g < len(chunks):
                stage_of(g)

    own = pltpu.make_async_copy(
        w_ref,
        full_ref.at[:, pl.ds(pl.multiple_of(row * rows_dev, rows_dev), rows_dev)],
        own_sem,
    )
    start_z(0)
    start_z(1)
    own.start()

    def table_of(e):
        return table_ref if (layers - e) % 2 == 0 else table

    def items(e):
        par = e % 2
        found = [(0, border_buf.at[par], lambda k, c: table_of(e).at[k, c])]
        if e == 0:
            found.append((1, count_buf, lambda k, c: count_ref.at[k, c]))
        return found

    def out(e, item, src, dst, j):
        return remote(
            src,
            dst(core, chip),
            x_send.at[e + item * 4, j - 1],
            x_recv.at[e + item * 4, j - 1],
            ((chip + j) % chips * 2 + core, row),
        )

    def across(e, item, src, dst, j, of_core):
        origin = (chip - j + chips) % chips
        return remote(
            src if j == 0 else dst(of_core, origin),
            dst(of_core, origin),
            p_send.at[e + item * 4, j],
            p_recv.at[e + item * 4, j],
            sibling,
        )

    def share(e, value):
        par = e % 2
        choice = hot(iota((border, nodes), 1) == index_t[pl.ds(0, border), BORDER_ROW : BORDER_ROW + 1])
        rows_out = picked(choice, value)
        border_buf[par] = rows_out
        table_of(e)[core, chip] = rows_out
        for item, src, dst in items(e):
            for j in range(1, chips):
                out(e, item, src, dst, j).start()
            across(e, item, src, dst, 0, core).start()

    def relay(e):
        for item, src, dst in items(e):
            for j in range(1, chips):
                out(e, item, src, dst, j).wait_recv()
                across(e, item, src, dst, j, core).start()

    def gathered(e):
        for item, src, dst in items(e):
            for j in range(chips):
                across(e, item, src, dst, j, 1 - core).wait_recv()
            for j in range(chips):
                across(e, item, src, dst, j, core).wait_send()
            for j in range(1, chips):
                out(e, item, src, dst, j).wait_send()

    def put_src(at, value):
        value_high, value_low = pieces(value)
        size = value.shape[0]
        src_high[pl.ds(at, size)] = value_high
        src_low[pl.ds(at, size)] = value_low

    def save(kind, layer, src):
        dst = (before_ref, message_ref, edges_ref, embed_ref)[kind]
        return pltpu.make_async_copy(src, dst if layer is None else dst.at[layer], save_sem.at[kind])

    def table_place(index):
        far = (index - nodes).astype(jnp.float32)
        owner = jnp.floor((far + 0.5) * (1.0 / border))
        at_chip = jnp.floor(owner * 0.5)
        moved = ((owner - 2.0 * at_chip) * chips + at_chip) * border + far - owner * border
        return jnp.where(index < nodes, index, moved.astype(jnp.int32) + nodes)

    index_ref[...] = jnp.zeros_like(index_ref)
    index_ref[SEND_ROW : SEND_ROW + 1] = table_place(ends_ref[0:1])
    index_ref[RECV_ROW : RECV_ROW + 1] = ends_ref[1:2]
    index_ref[BORDER_ROW : BORDER_ROW + 1, pl.ds(0, border)] = border_ref[...]
    index_ref[FEED_ROW : FEED_ROW + 1, pl.ds(0, grids)] = feed_ref[...]
    index_ref[MASK_ROW : MASK_ROW + 1, pl.ds(0, grids)] = mask_ref[...]
    index_ref[READ_ROW:, pl.ds(0, grids)] = table_place(read_ref[...])
    index_t[...] = index_ref[...].T
    embed_buf = before_buf.at[pl.ds(0, grids)]
    channels = grid_ref.shape[0]
    embed_buf[...] = product(grid_ref[...], enc_ref[pl.ds(0, channels)], TN)
    save(3, None, embed_buf).start()
    tick(1)
    feed = hot(iota((nodes, grids), 0) == index_ref[FEED_ROW : FEED_ROW + 1, pl.ds(0, grids)])
    fed = picked(feed, silu(embed_buf[...]))
    fed_ref[...] = fed
    nodes_ref[0] = normed(fed)[0]
    mask = index_ref[MASK_ROW : MASK_ROW + 1, pl.ds(0, grids)].astype(jnp.float32)
    counts = jnp.broadcast_to(jnp.sum(mask, axis=1, keepdims=True), count_buf.shape)
    count_buf[...] = counts
    count_ref[core, chip] = counts
    tick(2)
    edge_t[...] = edge_rows(edge_ref, edge_t.shape[1]).T

    def embed_edges(at, size):
        return silu(embedded_edges(edge_t, enc_ref, channels, edge_ref.shape[0], at, size))

    fill_rows(edge_buf.at[0], embed_edges)
    inputs = src_high.shape[0]
    near_inputs = 2 * nodes

    def choose(at, size):
        columns = iota((size, inputs), 1)
        sent = index_t[pl.ds(at, size), SEND_ROW : SEND_ROW + 1]
        received = index_t[pl.ds(at, size), RECV_ROW : RECV_ROW + 1] + nodes
        sent = jnp.where(sent < nodes, sent, sent + nodes)
        return hot(jnp.logical_or(columns == sent, columns == received))

    fill_rows(pick, choose)
    tick(3)

    def choose_receiver(at, size):
        return hot(iota((size, edges), 0) + at == index_ref[RECV_ROW : RECV_ROW + 1])

    fill_rows(gather_t, choose_receiver, 64)
    own.wait()
    tick(4)
    tick(5)
    for layer in range(layers):
        first = layer * blocks
        now, later = layer % 2, (layer + 1) % 2
        weights.load(first, (1, 2))
        node = nodes_ref[layer]
        node_high, node_low = pieces(node)
        sender = weights.times(node_high, node_low, 1)
        share(layer, sender)
        put_src(0, sender)
        put_src(nodes, weights.times(node_high, node_low, 2))
        if layer > 0:
            save(0, layer - 1, before_buf).wait()
            save(1, layer - 1, message_buf).wait()
            save(2, layer - 1, edge_buf.at[later]).wait()
        else:
            save(3, None, embed_buf).wait()
        save(2, layer, edge_buf.at[now]).start()
        tick(6 + 4 * layer)
        weights.load(first, (0,))

        def near_part(t):
            at = pl.ds(t * tile, tile)
            before_buf[at] = (
                weights.apply(edge_buf[now, at], 0)
                + chosen(
                    pick[at, pl.ds(0, near_inputs)],
                    src_high[pl.ds(0, near_inputs)],
                    src_low[pl.ds(0, near_inputs)],
                )
                + param_ref[layer, pl.ds(0, 1)]
            )

        near_part(0)
        tick(7 + 4 * layer)
        relay(layer)
        near_part(1)
        weights.load(first, (3, 4))
        inner = weights.times(node_high, node_low, 4) + param_ref[layer, pl.ds(4, 1)]
        gathered(layer)
        table_now = table_of(layer)
        for side in range(2):
            put_src(
                near_inputs + side * chips * border,
                table_now[side].reshape(chips * border, width),
            )
        agg_ref[layer] = jnp.zeros((nodes, width), jnp.float32)

        def edge_tile(t):
            at = pl.ds(t * tile, tile)
            far_inputs = pl.ds(near_inputs, inputs - near_inputs)
            before = before_buf[at] + chosen(
                pick[at, far_inputs], src_high[far_inputs], src_low[far_inputs]
            )
            before_buf[at] = before
            message = weights.apply(silu(before), 3) + param_ref[layer, pl.ds(1, 1)]
            message_buf[at] = message
            edge = (
                edge_buf[now, at]
                + normed(message)[0] * (1.0 + param_ref[layer, pl.ds(2, 1)])
                + param_ref[layer, pl.ds(3, 1)]
            )
            if layer < layers - 1:
                edge_buf[later, at] = edge
            agg_ref[layer] += picked(gather_t[:, at], edge)

        edge_tile(0)
        tick(8 + 4 * layer)
        edge_tile(1)
        save(0, layer, before_buf).start()
        save(1, layer, message_buf).start()
        weights.load(first, (5, 6))
        inner = inner + weights.apply(agg_ref[layer], 5)
        inner_ref[layer] = inner
        update = weights.apply(silu(inner), 6) + param_ref[layer, pl.ds(5, 1)]
        update_ref[layer] = update
        nodes_ref[layer + 1] = (
            node
            + normed(update)[0] * (1.0 + param_ref[layer, pl.ds(6, 1)])
            + param_ref[layer, pl.ds(7, 1)]
        )
        tick(9 + 4 * layer)
    share(layers, nodes_ref[layers])
    relay(layers)
    gathered(layers)
    save(0, layers - 1, before_buf).wait()
    save(1, layers - 1, message_buf).wait()
    save(2, layers - 1, edge_buf.at[(layers - 1) % 2]).wait()
    for g in range(len(chunks)):
        for j in others:
            z_copy(g, j, row).wait_send()
            for side in range(2):
                a_copy(g, side, j, pos).wait_send()
                b_copy(g, 1 - side, j, near_pos[side]).wait_send()
            s_copy(g, j, core).wait_send()


def forward(bands, rows, grid, edge, indices, blocks, enc, params):
    f32, bf16 = jnp.float32, jnp.bfloat16
    dma = pltpu.SemaphoreType.DMA
    width = blocks.shape[2]
    edges, grids = edge.shape[1], grid.shape[1]
    layers = params.shape[0]
    rim = indices[1].shape[1]
    index_rows = READ_ROW + indices[4].shape[0]
    nodes = NODE_DEV
    chips = bands // 2
    inputs = 2 * nodes + bands * rim
    each = blocks.shape[0] // layers
    chunks = []
    for layer in range(layers):
        chunks += [(layer * each + first, size) for first, size in ((1, 2), (0, 1), (3, 2), (5, 2))]
    groups = len(chunks)
    tile = edges // 2

    def array(*shape):
        return jax.ShapeDtypeStruct(shape, f32)

    return pl.pallas_call(
        functools.partial(forward_kernel, bands, rows, tuple(chunks), tile),
        out_shape=(
            array(blocks.shape[0], width, width),
            array(layers, edges, width),
            array(layers, edges, width),
            array(layers, edges, width),
            array(grids, width),
            array(layers + 1, nodes, width),
            array(nodes, width),
            array(layers, nodes, width),
            array(layers, nodes, width),
            array(layers, nodes, width),
            array(2, chips, rim, width),
            array(2, chips, 8, 128),
            jax.ShapeDtypeStruct((index_rows, edges), jnp.int32),
        ),
        in_specs=[VMEM] * 10,
        out_specs=[ANY] * 5 + [VMEM] * 8,
        scratch_shapes=[
            pltpu.VMEM((2, edges, width), f32),
            pltpu.VMEM((edges, width), f32),
            pltpu.VMEM((edges, width), f32),
            pltpu.VMEM((edges, index_rows), jnp.int32),
            pltpu.VMEM((edges, 8), f32),
            pltpu.VMEM((edges, inputs), bf16),
            pltpu.VMEM((nodes, edges), bf16),
            pltpu.VMEM((inputs, width), bf16),
            pltpu.VMEM((inputs, width), bf16),
            pltpu.VMEM((each, width, width), bf16),
            pltpu.VMEM((each, width, width), bf16),
            pltpu.VMEM((2, width, width), f32),
            pltpu.VMEM((2, chips, rim, width), f32),
            pltpu.VMEM((2, rim, width), f32),
            pltpu.VMEM((8, 128), f32),
            dma((2,)),
            dma((4,)),
            dma,
            dma((groups, rows - 1)),
            dma((groups, rows - 1)),
            dma((groups, 2, rows - 1)),
            dma((groups, 2, rows - 1)),
            dma((groups, 2, rows - 1)),
            dma((groups, 2, rows - 1)),
            dma((groups, rows - 1)),
            dma((groups, rows - 1)),
            dma((5, chips - 1)),
            dma((5, chips - 1)),
            dma((5, chips)),
            dma((5, chips)),
        ],
        compiler_params=pltpu.CompilerParams(
            collective_id=1, has_side_effects=True, vmem_limit_bytes=VMEM_BYTES
        ),
        name="forward",
    )(
        grid,
        edge,
        *indices,
        blocks,
        enc,
        params,
    )


def groups(layer):
    return (
        (layer, 0, 0, 3),
        (3 + layer, 0, 4, 3),
        (6 + layer // 2, layer % 2, 3, 1),
    )


class Reducer:
    def __init__(self, bands, layer, at, grads, sib, land, total, sems):
        band, row, self.chip, self.core = place(bands, 1)
        self.row = row
        self.chips = bands // 2
        self.sibling = (self.chip * 2 + 1 - self.core, row)
        self.layer, self.at = layer, at
        self.grads, self.sib, self.land, self.total = grads, sib, land, total
        (self.c_send, self.c_recv, self.r_send, self.r_recv) = sems[:4]
        (self.o_send, self.o_recv, self.p_send, self.p_recv, self.k_sem) = sems[4:]

    def each(self):
        for q, (owner, slot, block, count) in enumerate(groups(self.layer)):
            yield q, owner // 2, owner % 2, slot, pl.ds(block, count), count

    def to_sibling(self, q, rows):
        return remote(
            self.grads.at[rows],
            self.sib.at[rows],
            self.c_send.at[self.at, q],
            self.c_recv.at[self.at, q],
            self.sibling,
        )

    def to_owner(self, q, at_chip, at_core, rows, count):
        step = (at_chip - self.chip + self.chips) % self.chips
        return remote(
            self.grads.at[rows],
            self.land.at[self.at, step - 1, pl.ds(0, count)],
            self.r_send.at[self.at, q],
            self.r_recv.at[self.at, step - 1],
            (at_chip * 2 + at_core, self.row),
        )

    def to_chip(self, q, rows, j):
        return remote(
            self.grads.at[rows],
            self.total.at[rows],
            self.o_send.at[self.at, j - 1],
            self.o_recv.at[self.at, q],
            ((self.chip + j) % self.chips * 2 + self.core, self.row),
        )

    def across(self, q, rows, src):
        return remote(
            src.at[rows],
            self.total.at[rows],
            self.p_send.at[self.at, q],
            self.p_recv.at[self.at, q],
            self.sibling,
        )

    def keep(self, rows):
        return pltpu.make_async_copy(self.grads.at[rows], self.total.at[rows], self.k_sem.at[self.at])

    def start(self):
        for q, at_chip, at_core, slot, rows, count in self.each():
            @pl.when(self.core != at_core)
            def _():
                self.to_sibling(q, rows).start()

    def pair(self):
        for q, at_chip, at_core, slot, rows, count in self.each():
            @pl.when(self.core == at_core)
            def _():
                self.to_sibling(q, rows).wait_recv()
                self.grads[rows] += self.sib[rows]

                @pl.when(self.chip != at_chip)
                def _():
                    self.to_owner(q, at_chip, at_core, rows, count).start()

    def reduce(self, take, load):
        for q, at_chip, at_core, slot, rows, count in self.each():
            @pl.when(jnp.logical_and(self.core == at_core, self.chip == at_chip))
            def _():
                value = self.grads[rows]
                for j in range(1, self.chips):
                    landed = self.land.at[self.at, j - 1, pl.ds(0, count)]
                    remote(
                        landed,
                        landed,
                        self.r_send.at[self.at, q],
                        self.r_recv.at[self.at, j - 1],
                        self.sibling,
                    ).wait_recv()
                    value = value + load(landed, count)
                self.grads[rows] = value
                take(slot, count, value)
                for j in range(1, self.chips):
                    self.to_chip(q, rows, j).start()
                self.across(q, rows, self.grads).start()
                self.keep(rows).start()

    def relay(self):
        for q, at_chip, at_core, slot, rows, count in self.each():
            @pl.when(jnp.logical_and(self.core == at_core, self.chip != at_chip))
            def _():
                self.to_chip(q, rows, 1).wait_recv()
                self.across(q, rows, self.total).start()

    def finish(self):
        for q, at_chip, at_core, slot, rows, count in self.each():
            @pl.when(self.core != at_core)
            def _():
                self.to_sibling(q, rows).wait_send()
                self.across(q, rows, self.total).wait_recv()

            @pl.when(self.core == at_core)
            def _():
                self.across(q, rows, self.total).wait_send()

                @pl.when(self.chip != at_chip)
                def _():
                    self.to_owner(q, at_chip, at_core, rows, count).wait_send()

                @pl.when(self.chip == at_chip)
                def _():
                    for j in range(1, self.chips):
                        self.to_chip(q, rows, j).wait_send()
                    self.keep(rows).wait()


def reducer_sems(count, chips):
    dma = pltpu.SemaphoreType.DMA
    return [
        dma((count, 3)),
        dma((count, 3)),
        dma((count, 3)),
        dma((count, chips - 1)),
        dma((count, chips - 1)),
        dma((count, 3)),
        dma((count, 3)),
        dma((count, 3)),
        dma((count,)),
    ]


class Spreader:
    def __init__(self, bands, at, grads, sib, land, landed, total, sems):
        band, self.row, self.chip, self.core = place(bands, 1)
        self.chips = bands // 2
        self.sibling = (self.chip * 2 + 1 - self.core, self.row)
        self.at = at
        self.grads, self.sib, self.land, self.landed, self.total = grads, sib, land, landed, total
        self.half = grads.shape[1] // 2
        self.piece = self.half // OWNER_CHIPS
        (self.c_sem, self.r_send, self.r_recv, self.o_send, self.o_recv, self.p_sem, self.k_sem) = sems

    def rows(self, core):
        return pl.ds(pl.multiple_of(core * self.half, 8), self.half)

    def part(self, core, chip):
        return pl.ds(pl.multiple_of(core * self.half + chip * self.piece, 8), self.piece)

    def to_sibling(self):
        return remote(
            self.grads.at[:, self.rows(1 - self.core)],
            self.sib,
            self.c_sem.at[self.at, 0],
            self.c_sem.at[self.at, 1],
            self.sibling,
        )

    def to_owner(self, chip):
        step = (chip - self.chip + self.chips) % self.chips
        return remote(
            self.grads.at[:, self.part(self.core, chip)],
            self.land.at[step - 1],
            self.r_send.at[self.at, chip],
            self.r_recv.at[self.at, step - 1],
            (chip * 2 + self.core, self.row),
        )

    def to_chip(self, j, chip):
        part = self.part(self.core, chip)
        return remote(
            self.grads.at[:, part],
            self.total.at[:, part],
            self.o_send.at[self.at, j - 1],
            self.o_recv.at[self.at, chip],
            ((self.chip + j) % self.chips * 2 + self.core, self.row),
        )

    def keep(self):
        part = self.part(self.core, self.chip)
        return pltpu.make_async_copy(
            self.grads.at[:, part], self.total.at[:, part], self.k_sem.at[self.at, 0]
        )

    def across(self, core):
        region = self.total.at[:, self.rows(core)]
        return remote(region, region, self.p_sem.at[self.at, 0], self.p_sem.at[self.at, 1], self.sibling)

    def owned(self, body):
        if self.chips == OWNER_CHIPS:
            body()
        else:
            pl.when(self.chip < OWNER_CHIPS)(body)

    def start(self):
        self.to_sibling().start()

    def pair(self):
        self.to_sibling().wait()
        self.grads[:, self.rows(self.core)] += self.sib[...]
        for chip in range(OWNER_CHIPS):
            pl.when(self.chip != chip)(self.to_owner(chip).start)

    def reduce(self):
        def body():
            part = self.part(self.core, self.chip)
            for j in range(1, self.chips):
                remote(
                    self.landed,
                    self.land.at[j - 1],
                    self.r_send.at[self.at, 0],
                    self.r_recv.at[self.at, j - 1],
                    self.sibling,
                ).wait_recv()
                copy = pltpu.make_async_copy(self.land.at[j - 1], self.landed, self.k_sem.at[self.at, 1])
                copy.start()
                copy.wait()
                self.grads[:, part] += self.landed[...]
            for j in range(1, self.chips):
                self.to_chip(j, self.chip).start()
            self.keep().start()

        self.owned(body)

    def relay(self):
        for chip in range(OWNER_CHIPS):
            pl.when(self.chip != chip)(self.to_chip(1, chip).wait_recv)
        self.owned(lambda: self.keep().wait())
        self.across(self.core).start()

    def finish(self):
        self.across(self.core).wait_send()
        self.across(1 - self.core).wait_recv()
        for chip in range(OWNER_CHIPS):
            pl.when(self.chip != chip)(self.to_owner(chip).wait_send)

        def body():
            for j in range(1, self.chips):
                self.to_chip(j, self.chip).wait_send()

        self.owned(body)


def spreader_sems(count, chips):
    dma = pltpu.SemaphoreType.DMA
    return [
        dma((count, 2)),
        dma((count, OWNER_CHIPS)),
        dma((count, chips - 1)),
        dma((count, chips - 1)),
        dma((count, OWNER_CHIPS)),
        dma((count, 2)),
        dma((count, 2)),
    ]


def backward_kernel(
    bands,
    rows,
    each,
    tile,
    grid_ref,
    target_ref,
    edge_ref,
    index_ref,
    enc_ref,
    dec_ref,
    param_ref,
    full_ref,
    before_ref,
    message_ref,
    edges_ref,
    embed_ref,
    nodes_ref,
    fed_ref,
    agg_ref,
    inner_ref,
    update_ref,
    table_ref,
    count_ref,
    grads_ref,
    small_ref,
    total_ref,
    land_grads,
    edge_buf,
    before_buf,
    message_buf,
    node_buf,
    agg_buf,
    inner_buf,
    update_buf,
    index_t,
    edge_t,
    features,
    edge_grad,
    node_grad,
    part_high,
    part_low,
    pick_t,
    gather,
    high,
    low,
    stage,
    table,
    sib,
    land,
    grads_buf,
    sib_grads,
    landed_buf,
    stage_sem,
    load_sem,
    d_send,
    d_recv,
    r_send,
    r_recv,
    *sems,
):
    band, row, chip, core = place(bands, rows)
    chips = bands // 2
    layers = param_ref.shape[0]
    nodes, width = node_buf.shape
    edges = edge_buf.shape[0]
    grids = grid_ref.shape[1]
    border = table.shape[2]
    table_rows = bands * border
    rows_dev = grads_ref.shape[1]
    weights = Weights(full_ref, stage, high, low, stage_sem)
    sibling = (chip * 2 + 1 - core, row)
    partners = [((chip + j) % chips * 2 + core, row) for j in range(1, chips)] + [sibling]
    own_rows = pl.ds(pl.multiple_of(row * rows_dev, rows_dev), rows_dev)

    def load(kind, layer):
        src = (before_ref, message_ref, edges_ref, agg_ref, inner_ref, update_ref, nodes_ref)[kind]
        dst = (before_buf, message_buf, edge_buf, agg_buf, inner_buf, update_buf, node_buf)[kind]
        return pltpu.make_async_copy(src.at[layer], dst, load_sem.at[kind])

    table_load = pltpu.make_async_copy(table_ref, table, load_sem.at[7])
    embed_buf = before_buf.at[pl.ds(0, grids)]
    fed_buf = agg_buf
    embed_load = pltpu.make_async_copy(embed_ref, embed_buf, load_sem.at[8])
    fed_load = pltpu.make_async_copy(fed_ref, fed_buf, load_sem.at[9])
    load(6, layers).start()
    table_load.start()
    for kind in range(6):
        load(kind, layers - 1).start()
    meet(partners)

    def to_sibling(e):
        return remote(table.at[1 - core], sib.at[e % 2], d_send.at[e], d_recv.at[e], sibling)

    def to_band(e, j):
        to = (chip + j) % chips
        return remote(
            table.at[core, to], land.at[e % 2, j - 1], r_send.at[e, j - 1], r_recv.at[e, j - 1], (to * 2 + core, row)
        )

    def give(e):
        to_sibling(e).wait()
        table[core] += sib[e % 2]
        for j in range(1, chips):
            to_band(e, j).start()

    def returned(e):
        total = table[core, chip]
        for j in range(1, chips):
            to_band(e, j).wait_recv()
            total = total + land[e % 2, j - 1]
        for j in range(1, chips):
            to_band(e, j).wait_send()
        return picked(hot(iota((nodes, border), 0) == index_ref[BORDER_ROW : BORDER_ROW + 1, pl.ds(0, border)]), total)

    def put_table(value_high, value_low, count):
        side_rows = chips * border
        for side in range(2):
            choice = pick_t[pl.ds(nodes + side * side_rows, side_rows), pl.ds(0, count)]
            table[side] = chosen(choice, value_high, value_low).reshape(chips, border, width)

    def grads_of(layer):
        return grads_buf.at[layer - 1] if layer > 0 else grads_ref

    reducers = [None] + [
        Spreader(
            bands,
            layer - 1,
            grads_of(layer),
            sib_grads,
            land_grads.at[layer - 1],
            landed_buf,
            total_ref.at[pl.ds(layer * each, each)],
            sems,
        )
        for layer in range(1, layers)
    ]

    def put_grad(layer, block, value):
        grads_of(layer)[block] = value

    def add_grad(layer, block, value):
        grads_of(layer)[block] += value

    index_t[...] = index_ref[...].T

    def choose_reads(at, size):
        line = iota((size, grids), 0) + at
        counts = jnp.zeros((size, grids), jnp.float32)
        for way in range(READ_ROW, index_ref.shape[0]):
            counts = counts + jnp.where(line == index_ref[way : way + 1, pl.ds(0, grids)], 1.0, 0.0)
        return counts.astype(jnp.bfloat16)

    def fill_reads(t, carry):
        at = pl.multiple_of(t * 64, 64)
        pick_t[pl.ds(at, 64), pl.ds(0, grids)] = choose_reads(at, 64)
        return carry

    lax.fori_loop(0, (nodes + table_rows) // 64, fill_reads, 0)

    def choose_gather(at, size):
        return hot(iota((size, nodes), 1) == index_t[pl.ds(at, size), RECV_ROW : RECV_ROW + 1])

    fill_rows(gather, choose_gather)
    load(6, layers).wait()
    table_load.wait()
    reads = edge_grad.at[pl.ds(0, grids)]
    own_high, own_low = pieces(node_buf[...])
    reads[...] = chosen(pick_t[pl.ds(0, nodes), pl.ds(0, grids)], own_high, own_low, TN)
    side_rows = chips * border
    for side in range(2):
        side_high, side_low = pieces(table[side].reshape(side_rows, width))
        choice = pick_t[pl.ds(nodes + side * side_rows, side_rows), pl.ds(0, grids)]
        reads[...] += chosen(choice, side_high, side_low, TN)
    load(6, layers - 1).start()
    weights.load((layers - 1) * each, (6, 4, 5, 3, 0, 1, 2))
    active = silu(reads[...])
    mask = index_ref[MASK_ROW : MASK_ROW + 1, pl.ds(0, grids)].astype(jnp.float32)
    missed = grid_ref[...] + product(dec_ref[...], active, NT) - target_ref[...]
    total = jnp.sum(jnp.sum(count_ref[:, :, 0:1, 0:1], axis=0), axis=0)
    masked = mask * missed
    loss = jnp.sum(column(masked * missed), axis=1, keepdims=True)
    grad = (2.0 / total) * masked
    channels = grid_ref.shape[0]
    encs = -(-channels // 8) * 8
    decs = encs
    decoder_at = encs + 8 + layers * 8
    small_ref[pl.ds(decoder_at, channels)] = product(grad, active)
    tail_rows = small_ref.shape[0] - decoder_at - decs
    small_ref[pl.ds(decoder_at + decs, tail_rows)] = jnp.broadcast_to(loss, (tail_rows, width))
    read_high, read_low = pieces(product(grad, dec_ref[...], TN) * silu_back(reads[...]))
    put_table(read_high, read_low, grids)
    to_sibling(0).start()
    node_grad[...] = chosen(pick_t[pl.ds(0, nodes), pl.ds(0, grids)], read_high, read_low)

    def choose(at, size):
        line = iota((size, edges), 0) + at
        sent = line == index_ref[SEND_ROW : SEND_ROW + 1]
        received = line == index_ref[RECV_ROW : RECV_ROW + 1] + (nodes + table_rows)
        return hot(jnp.logical_or(sent, received))

    fill_rows(pick_t, choose, 64)
    give(0)
    edge_grad[...] = jnp.zeros_like(edge_grad)
    node_grad[...] += returned(0)

    for depth in range(layers):
        layer = layers - 1 - depth
        e = depth + 1
        base = encs + 8 + layer * 8

        def put_param(index, value, base=base):
            small_ref[pl.ds(base + index, 1)] = value

        def add_param(index, value, base=base):
            small_ref[pl.ds(base + index, 1)] += value

        for kind in (3, 4, 5, 6):
            load(kind, layer).wait()
        if layer + 1 < layers:
            reducers[layer + 1].pair()
        if layer + 2 < layers:
            reducers[layer + 2].reduce()
        grad = node_grad[...]
        norm, scale = normed(update_buf[...])
        put_param(7, column(grad))
        put_param(6, column(grad * norm))
        grad = normed_back(grad * (1.0 + param_ref[layer, pl.ds(6, 1)]), norm, scale)
        put_param(5, column(grad))
        grad_high, grad_low = pieces(grad)
        put_grad(layer, 6, product(silu(inner_buf[:, own_rows]), grad, TN))
        grad = weights.times(grad_high, grad_low, 6, NT) * silu_back(inner_buf[...])
        put_param(4, column(grad))
        grad_high, grad_low = pieces(grad)
        put_grad(layer, 4, product(node_buf[:, own_rows], grad, TN))
        put_grad(layer, 5, product(agg_buf[:, own_rows], grad, TN))
        node_grad[...] += weights.times(grad_high, grad_low, 4, NT)
        agg_high, agg_low = pieces(weights.times(grad_high, grad_low, 5, NT))
        for kind in (0, 1, 2):
            load(kind, layer).wait()
        for index in range(4):
            put_param(index, jnp.zeros((1, width), jnp.float32))
        for block in (0, 3):
            put_grad(layer, block, jnp.zeros((rows_dev, width), jnp.float32))

        def edge_tile(t, carry):
            at = pl.ds(pl.multiple_of(t * tile, tile), tile)
            grad = edge_grad[at] + chosen(gather[at], agg_high, agg_low)
            edge_grad[at] = grad
            norm, scale = normed(message_buf[at])
            add_param(3, column(grad))
            add_param(2, column(grad * norm))
            grad = normed_back(grad * (1.0 + param_ref[layer, pl.ds(2, 1)]), norm, scale)
            add_param(1, column(grad))
            grad_high, grad_low = pieces(grad)
            add_grad(layer, 3, product(silu(before_buf[at, own_rows]), grad, TN))
            grad = weights.times(grad_high, grad_low, 3, NT) * silu_back(before_buf[at])
            add_param(0, column(grad))
            add_grad(layer, 0, product(edge_buf[at, own_rows], grad, TN))
            grad_high, grad_low = pieces(grad)
            part_high[at] = grad_high
            part_low[at] = grad_low
            return carry

        lax.fori_loop(0, edges // tile, edge_tile, 0)
        if layer > 0:
            for kind in range(6):
                load(kind, layer - 1).start()
        else:
            embed_load.start()
            fed_load.start()
        put_table(part_high[...], part_low[...], edges)
        to_sibling(e).start()
        sender = chosen(pick_t[pl.ds(0, nodes)], part_high[...], part_low[...])
        give(e)
        received = chosen(pick_t[pl.ds(nodes + table_rows, nodes)], part_high[...], part_low[...])

        def edge_back(t, carry):
            at = pl.ds(pl.multiple_of(t * tile, tile), tile)
            edge_grad[at] += weights.times(part_high[at], part_low[at], 0, NT)
            return carry

        lax.fori_loop(0, edges // tile, edge_back, 0)
        put_grad(layer, 2, product(node_buf[:, own_rows], received, TN))
        node_grad[...] += weights.apply(received, 2, NT)
        if layer > 0:
            weights.load((layer - 1) * each, (6, 4, 5, 3, 0))
        sender = sender + returned(e)
        put_grad(layer, 1, product(node_buf[:, own_rows], sender, TN))
        node_grad[...] += weights.apply(sender, 1, NT)
        if layer > 0:
            load(6, layer - 1).start()
            weights.load((layer - 1) * each, (1, 2))
            reducers[layer].start()

    reducers[1].reduce()
    embed_load.wait()
    fed_load.wait()
    norm, scale = normed(fed_buf[...])
    fed_grad = normed_back(node_grad[...], norm, scale)
    feed = hot(iota((grids, nodes), 1) == index_t[pl.ds(0, grids), FEED_ROW : FEED_ROW + 1])
    grad = picked(feed, fed_grad) * silu_back(embed_buf[...])
    small_ref[pl.ds(0, channels)] = product(grid_ref[...], grad)
    small_ref[pl.ds(encs, 8)] = jnp.zeros((8, width), jnp.float32)
    features[...] = edge_rows(edge_ref, 8)
    edge_t[...] = features[...].T

    def embed_back(t, carry):
        first = pl.multiple_of(t * 128, 128)
        at = pl.ds(first, 128)
        embed = embedded_edges(edge_t, enc_ref, channels, edge_ref.shape[0], first, 128)
        grad = edge_grad[at] * silu_back(embed)
        small_ref[pl.ds(encs, 8)] += product(features[:, at], grad)
        return carry

    lax.fori_loop(0, edges // 128, embed_back, 0)
    for layer in range(layers - 1, 0, -1):
        reducers[layer].relay()
    for layer in range(1, layers):
        reducers[layer].finish()


def backward(bands, rows, rim, rows_dev, inputs, saved):
    f32, bf16 = jnp.float32, jnp.bfloat16
    dma = pltpu.SemaphoreType.DMA
    grid, edge, index, decoder, params = inputs[0], inputs[2], inputs[3], inputs[5], inputs[6]
    layers = params.shape[0]
    full = saved[0]
    width = full.shape[2]
    each = full.shape[0] // layers
    edges, grids = edge.shape[1], grid.shape[1]
    nodes = NODE_DEV
    chips = bands // 2
    padded = -(-grid.shape[0] // 8) * 8
    small = padded + 8 + layers * 8 + padded + 8
    small = -(-small // (16 * OWNER_CHIPS)) * 16 * OWNER_CHIPS
    tile = edges // 2
    node = pltpu.VMEM((nodes, width), f32)
    return pl.pallas_call(
        functools.partial(backward_kernel, bands, rows, each, tile),
        out_shape=(
            jax.ShapeDtypeStruct((each, rows_dev, width), f32),
            jax.ShapeDtypeStruct((small, width), f32),
            jax.ShapeDtypeStruct((full.shape[0], rows_dev, width), f32),
            jax.ShapeDtypeStruct((layers - 1, chips - 1, each, rows_dev // 8, width), f32),
        ),
        in_specs=[VMEM] * 7 + [ANY] * 11 + [VMEM],
        out_specs=[VMEM, VMEM, ANY, ANY],
        scratch_shapes=[
            pltpu.VMEM((edges, width), f32),
            pltpu.VMEM((edges, width), f32),
            pltpu.VMEM((edges, width), f32),
            node,
            node,
            node,
            node,
            pltpu.VMEM((edges, index.shape[0]), jnp.int32),
            pltpu.VMEM((edges, 8), f32),
            pltpu.VMEM((8, edges), f32),
            pltpu.VMEM((edges, width), f32),
            node,
            pltpu.VMEM((edges, width), bf16),
            pltpu.VMEM((edges, width), bf16),
            pltpu.VMEM((2 * nodes + bands * rim, edges), bf16),
            pltpu.VMEM((edges, nodes), bf16),
            pltpu.VMEM((each, width, width), bf16),
            pltpu.VMEM((each, width, width), bf16),
            pltpu.VMEM((2, width, width), f32),
            pltpu.VMEM((2, chips, rim, width), f32),
            pltpu.VMEM((2, chips, rim, width), f32),
            pltpu.VMEM((2, chips - 1, rim, width), f32),
            pltpu.VMEM((layers - 1, each, rows_dev, width), f32),
            pltpu.VMEM((each, rows_dev // 2, width), f32),
            pltpu.VMEM((each, rows_dev // 8, width), f32),
            dma((2,)),
            dma((10,)),
            dma((layers + 1,)),
            dma((layers + 1,)),
            dma((layers + 1, chips - 1)),
            dma((layers + 1, chips - 1)),
            ]
        + spreader_sems(layers - 1, chips),
        compiler_params=pltpu.CompilerParams(
            collective_id=2, has_side_effects=True, vmem_limit_bytes=VMEM_BYTES
        ),
        name="backward",
    )(*inputs, *saved)


def newton(matrix, result, first, count, arrive, leave, gram, poly, temp, later):
    gram[...] = jnp.zeros_like(gram)

    def add_gram(i, carry):
        arrive(first + i)
        block = matrix[first + i]
        gram[...] += product(block, block, TN)
        return carry

    lax.fori_loop(0, count, add_gram, 0)
    diagonal = iota(gram.shape, 0) == iota(gram.shape, 1)
    squares = column(jnp.where(diagonal, gram[...], 0.0))
    scale = 1.0 / (jnp.sqrt(jnp.sum(squares, axis=1, keepdims=True)) + 1e-07)
    gram[...] = gram[...] * (scale * scale)
    poly[...] = coef_b * gram[...] + coef_c * product(gram[...], gram[...])
    temp[...] = coef_a * gram[...] + product(gram[...], poly[...])
    gram[...] = coef_a * temp[...] + product(temp[...], poly[...])
    later[...] = coef_b * gram[...] + coef_c * product(gram[...], gram[...])
    temp[...] = coef_a * (poly[...] + later[...]) + product(poly[...], later[...])

    def last(i, carry):
        block = matrix[first + i] * scale
        result[first + i] = (coef_a * coef_a) * block + product(block, temp[...])
        leave(first + i)
        return carry

    lax.fori_loop(0, count, last, 0)


def late_slot(owner, slot):
    return owner in (0, 3) or (owner == 6 and slot == 0)


def tail_kernel(
    bands,
    rows,
    grads_ref,
    small_ref,
    mom_ref,
    given_ref,
    total_ref,
    ortho_ref,
    shared_ref,
    land,
    grads,
    sib,
    landed_buf,
    sib_small,
    part_small,
    land_small,
    held,
    matrix,
    result,
    back,
    gram,
    poly,
    temp,
    later,
    load_sem,
    landed_sem,
    m_pair,
    m_red_send,
    m_red_recv,
    m_out_send,
    m_out_recv,
    m_pass,
    m_keep,
    up_send,
    up_recv,
    down_send,
    down_recv,
    o_send,
    o_recv,
    p_send,
    p_recv,
    keep_sem,
    *sems,
):
    band, row, chip, core = place(bands, rows)
    chips = bands // 2
    rows_dev = held.shape[1]
    sibling = (chip * 2 + 1 - core, row)
    partners = [((chip + j) % chips * 2 + core, row) for j in range(1, chips)] + [sibling]
    partners += [(band, (row + j) % rows) for j in range(1, rows)]
    reducer = Reducer(bands, 0, 0, grads, sib.at[0], land, total_ref.at[pl.ds(0, grads.shape[0])], sems)
    grads[...] = grads_ref[...]

    def load(slot):
        return pltpu.make_async_copy(
            mom_ref.at[slot_block(band, slot)], held.at[slot], load_sem.at[slot]
        )

    owned = [band < (8, 7, 6)[slot] for slot in range(SLOTS)]
    third = band // 3
    last = [jnp.logical_and(band < 7, band % 3 == 0)]
    last += [jnp.logical_and(band < 6, band % 3 == 0)] * 2
    for slot in range(SLOTS):
        pl.when(owned[slot])(load(slot).start)
    meet(partners)

    small_pair = remote(small_ref.at[1 - core], sib_small, m_pair.at[0], m_pair.at[1], sibling)

    def small_to(at):
        step = (at - chip + chips) % chips
        return remote(
            part_small.at[at],
            land_small.at[step - 1],
            m_red_send.at[at],
            m_red_recv.at[step - 1],
            (at * 2 + core, row),
        )

    def small_out(at, j):
        home = shared_ref.at[core * OWNER_CHIPS + at]
        return remote(
            part_small.at[at],
            home,
            m_out_send.at[j - 1],
            m_out_recv.at[at],
            ((chip + j) % chips * 2 + core, row),
        )

    def small_across(at, of_core, local):
        home = shared_ref.at[of_core * OWNER_CHIPS + at]
        return remote(
            part_small.at[at] if local else home, home, m_pass.at[0, at], m_pass.at[1, at], sibling
        )

    def small_keep(at):
        return pltpu.make_async_copy(
            part_small.at[at], shared_ref.at[core * OWNER_CHIPS + at], m_keep
        )

    row_a = rows // 2 - 1 + core
    row_b = rows // 2 - core
    split_at = 3 - third

    def home(slot):
        return row_a + (slot + third) // 3 * (row_b - row_a)

    def rows_of(at_row):
        return pl.ds(pl.multiple_of(at_row * rows_dev, rows_dev), rows_dev)

    def up(slot, from_row):
        step = (from_row - home(slot) + rows) % rows
        return remote(
            held.at[slot],
            matrix.at[slot, rows_of(from_row)],
            up_send.at[slot],
            up_recv.at[slot, step],
            (band, home(slot)),
        )

    def down(slot, to_row):
        step = (to_row - home(slot) + rows) % rows
        return remote(
            result.at[slot, rows_of(to_row)],
            back.at[slot],
            down_send.at[slot, step],
            down_recv.at[slot],
            (band, to_row),
        )

    def momentum(slot, value):
        load(slot).wait()
        held[slot] = momentum_decay * held[slot] + value

        @pl.when(row == home(slot))
        def _():
            matrix[slot, rows_of(row)] = held[slot]

        @pl.when(row != home(slot))
        def _():
            up(slot, row).start()

    def solve(when):
        own_b = jnp.logical_and(row == row_b, jnp.logical_and(band > 2, band < 7))
        own_b = jnp.logical_and(own_b, jnp.logical_not(band == 3) if when == 0 else band == 3)
        own_a = jnp.logical_and(row == row_a, band < 8)
        own_a = jnp.logical_and(own_a, jnp.logical_not(last[0]) if when == 0 else last[0])

        @pl.when(jnp.logical_or(own_a, own_b))
        def _():
            second = (row - row_a) * (row_b - row_a)
            first = second * split_at
            count = (1 - second) * split_at + second

            def arrive(slot):
                for step in range(1, rows):
                    up(slot, (row + step) % rows).wait_recv()

            def leave(slot):
                for step in range(1, rows):
                    down(slot, (row + step) % rows).start()
                back[slot] = result[slot, rows_of(row)]

            newton(matrix, result, first, count, arrive, leave, gram, poly, temp, later)

    units = [
        (owner, slot)
        for owner in range(2 * OWNER_CHIPS)
        for slot in range(SLOTS)
        if slot_used(owner, slot)
    ]

    def target(owner, slot):
        return ortho_ref.at[slot_block(owner, slot)]

    def out(owner, slot, j):
        return remote(
            back.at[slot],
            target(owner, slot),
            o_send.at[slot, j - 1],
            o_recv.at[owner // 2, slot],
            ((chip + j) % chips * 2 + core, row),
        )

    def across(owner, slot, local):
        return remote(
            back.at[slot] if local else target(owner, slot),
            target(owner, slot),
            p_send.at[owner // 2, slot],
            p_recv.at[owner // 2, slot],
            sibling,
        )

    def keep(owner, slot):
        return pltpu.make_async_copy(back.at[slot], target(owner, slot), keep_sem.at[slot])

    def publish(when):
        for owner, slot in units:
            if late_slot(owner, slot) != (when == 1):
                continue

            @pl.when(band == owner)
            def _():
                @pl.when(row != home(slot))
                def _():
                    down(slot, row).wait_recv()

                for j in range(1, chips):
                    out(owner, slot, j).start()
                across(owner, slot, True).start()
                keep(owner, slot).start()

    def relay(when):
        for owner, slot in units:
            if late_slot(owner, slot) != (when == 1):
                continue

            @pl.when(jnp.logical_and(core == owner % 2, chip != owner // 2))
            def _():
                out(owner, slot, 1).wait_recv()
                across(owner, slot, False).start()

    reducer.start()
    small_pair.start()
    for slot in range(SLOTS):
        @pl.when(jnp.logical_and(owned[slot], jnp.logical_not(last[slot])))
        def _():
            ready = pltpu.make_async_copy(
                total_ref.at[slot_block(band, slot)], back.at[slot], load_sem.at[SLOTS + slot]
            )
            ready.start()
            ready.wait()
            momentum(slot, back[slot])

    reducer.pair()
    small_pair.wait()
    part_small[...] = small_ref[core] + sib_small[...]
    for at in range(OWNER_CHIPS):
        pl.when(chip != at)(small_to(at).start)
    solve(0)

    def take(slot, count, value):
        for n in range(count):
            momentum(slot + n, value[n])

    def load_landed(src, count):
        dst = landed_buf.at[pl.ds(0, count)]
        copy = pltpu.make_async_copy(src, dst, landed_sem)
        copy.start()
        copy.wait()
        return dst[...]

    reducer.reduce(take, load_landed)
    for at in range(OWNER_CHIPS):
        @pl.when(chip == at)
        def _():
            for j in range(1, chips):
                remote(
                    land_small.at[j - 1],
                    land_small.at[j - 1],
                    m_red_send.at[at],
                    m_red_recv.at[j - 1],
                    sibling,
                ).wait_recv()
                part_small[at] += land_small[j - 1]
            for j in range(1, chips):
                small_out(at, j).start()
            small_across(at, core, True).start()
            small_keep(at).start()

    publish(0)
    solve(1)
    reducer.relay()
    for at in range(OWNER_CHIPS):
        @pl.when(chip != at)
        def _():
            small_out(at, 1).wait_recv()
            small_across(at, core, False).start()

    publish(1)
    relay(0)
    relay(1)
    reducer.finish()
    for at in range(OWNER_CHIPS):
        small_across(at, core, False).wait_send()
        small_across(at, 1 - core, False).wait_recv()

        @pl.when(chip != at)
        def _():
            small_to(at).wait_send()

        @pl.when(chip == at)
        def _():
            for j in range(1, chips):
                small_out(at, j).wait_send()
            small_keep(at).wait()

    for owner, slot in units:
        @pl.when(core == owner % 2)
        def _():
            across(owner, slot, False).wait_send()

        @pl.when(core != owner % 2)
        def _():
            across(owner, slot, False).wait_recv()

        @pl.when(band == owner)
        def _():
            for j in range(1, chips):
                out(owner, slot, j).wait_send()
            keep(owner, slot).wait()

            @pl.when(row != home(slot))
            def _():
                up(slot, row).wait_send()

            @pl.when(row == home(slot))
            def _():
                for step in range(1, rows):
                    down(slot, (row + step) % rows).wait_send()


def tail(bands, rows, grads, small, momentum, given):
    blocks, rows_dev, width = momentum.shape
    each = grads.shape[0]
    chips = bands // 2
    chunk = small.shape[2]
    f32 = jnp.float32
    dma = pltpu.SemaphoreType.DMA
    square = pltpu.VMEM((width, width), f32)
    slots = pltpu.VMEM((SLOTS, rows_dev, width), f32)
    return pl.pallas_call(
        functools.partial(tail_kernel, bands, rows),
        out_shape=(
            jax.ShapeDtypeStruct(given.shape, f32),
            jax.ShapeDtypeStruct((blocks, rows_dev, width), f32),
            jax.ShapeDtypeStruct((2 * OWNER_CHIPS, chunk, width), f32),
            jax.ShapeDtypeStruct((1, chips - 1, SLOTS, rows_dev, width), f32),
        ),
        in_specs=[VMEM, VMEM, ANY, ANY],
        out_specs=[ANY, ANY, ANY, ANY],
        input_output_aliases={3: 0},
        scratch_shapes=[
            pltpu.VMEM((each, rows_dev, width), f32),
            pltpu.VMEM((1, each, rows_dev, width), f32),
            slots,
            pltpu.VMEM((OWNER_CHIPS, chunk, width), f32),
            pltpu.VMEM((OWNER_CHIPS, chunk, width), f32),
            pltpu.VMEM((chips - 1, chunk, width), f32),
            slots,
            pltpu.VMEM((SLOTS, width, width), f32),
            pltpu.VMEM((SLOTS, width, width), f32),
            slots,
            square,
            square,
            square,
            square,
            dma((2 * SLOTS,)),
            dma,
            dma((2,)),
            dma((OWNER_CHIPS,)),
            dma((chips - 1,)),
            dma((chips - 1,)),
            dma((OWNER_CHIPS,)),
            dma((2, OWNER_CHIPS)),
            dma,
            dma((SLOTS,)),
            dma((SLOTS, rows)),
            dma((SLOTS, rows)),
            dma((SLOTS,)),
            dma((SLOTS, chips - 1)),
            dma((OWNER_CHIPS, SLOTS)),
            dma((OWNER_CHIPS, SLOTS)),
            dma((OWNER_CHIPS, SLOTS)),
            dma((SLOTS,)),
        ]
        + reducer_sems(1, chips),
        compiler_params=pltpu.CompilerParams(
            collective_id=0, has_side_effects=True, vmem_limit_bytes=VMEM_BYTES
        ),
        name="tail",
    )(grads, small, momentum, given)


def finish_kernel(
    shapes,
    channels,
    edge_channels,
    w_ref,
    average_ref,
    mom_ref,
    total_ref,
    ortho_ref,
    small_ref,
    count_ref,
    enc_ref,
    enc_first_ref,
    enc_second_ref,
    dec_ref,
    dec_first_ref,
    dec_second_ref,
    param_ref,
    param_first_ref,
    param_second_ref,
    loss_ref,
    total_count_ref,
    new_w_ref,
    new_mom_ref,
    new_average_ref,
    enc_outs,
    dec_outs,
    param_outs,
):
    wide, params_at, decoder_at, loss_at = shapes
    step = pl.program_id(0)
    for n in range(w_ref.shape[0]):
        block = lax.rem(step * w_ref.shape[0] + n, len(block_scale))
        scale = jnp.where(block < 3, block_scale[0], jnp.where(block == 4, block_scale[4], 1.0))
        scale = jnp.where(block == 5, block_scale[5], scale)
        fresh = w_ref[n] * (1.0 - muon_rate * weight_decay) - (muon_rate * scale) * ortho_ref[n]
        new_w_ref[n] = fresh
        new_average_ref[n] = average_decay * average_ref[n] + (1.0 - average_decay) * fresh
        new_mom_ref[n] = momentum_decay * mom_ref[n] + total_ref[n]

    def put(outs, at, values):
        for ref, value in zip(outs, values):
            ref[at] = value

    @pl.when(step == 0)
    def _():
        for at, grad in (
            (pl.ds(0, channels), small_ref[pl.ds(0, channels)]),
            (pl.ds(channels, edge_channels), small_ref[pl.ds(wide, edge_channels)]),
        ):
            put(enc_outs, at, adam_update(enc_ref[at], enc_first_ref[at], enc_second_ref[at], grad, adam_rate))
        grad = small_ref[pl.ds(decoder_at, channels)]
        put(dec_outs, ..., adam_update(dec_ref[...], dec_first_ref[...], dec_second_ref[...], grad, adam_rate))
        for layer in range(param_ref.shape[0]):
            grad = small_ref[pl.ds(params_at + layer * 8, 8)]
            put(
                param_outs,
                layer,
                adam_update(param_ref[layer], param_first_ref[layer], param_second_ref[layer], grad, param_rate),
            )
        loss_ref[...] = small_ref[pl.ds(loss_at, 1), 0:1]
        total_count_ref[...] = jnp.sum(jnp.sum(count_ref[:, :, 0:1, 0:1], axis=0), axis=0)


def finish(shapes, edge_channels, blocks, small, counts, encoder, decoder, params):
    f32 = jnp.float32
    channels = decoder[0].shape[0]
    big = blocks[0]
    tiled = pl.BlockSpec((SLOTS,) + big.shape[1:], lambda i: (i, 0, 0))

    def whole(value):
        return pl.BlockSpec(value.shape, lambda i: (0,) * value.ndim)

    def like(value):
        return jax.ShapeDtypeStruct(value.shape, f32)

    scalar = jax.ShapeDtypeStruct((1, 1), f32)
    return pl.pallas_call(
        functools.partial(finish_kernel, shapes, channels, edge_channels),
        grid=(big.shape[0] // SLOTS,),
        out_shape=(
            scalar,
            scalar,
            like(big),
            like(big),
            like(big),
            (like(encoder[0]),) * 3,
            (like(decoder[0]),) * 3,
            (like(params[0]),) * 3,
        ),
        in_specs=[tiled] * 5 + [whole(value) for value in (small, counts, *encoder, *decoder, *params)],
        out_specs=(
            whole(scalar),
            whole(scalar),
            tiled,
            tiled,
            tiled,
            (whole(encoder[0]),) * 3,
            (whole(decoder[0]),) * 3,
            (whole(params[0]),) * 3,
        ),
        compiler_params=pltpu.CompilerParams(vmem_limit_bytes=VMEM_BYTES),
        name="finish",
    )(*blocks, small, counts, *encoder, *decoder, *params)


def adam_update(values, first, second, gradient, rate):
    first = beta_one * first + (1.0 - beta_one) * gradient
    second = beta_two * second + (1.0 - beta_two) * gradient * gradient
    corrected = (
        first / (1.0 - beta_one**STEP) / (jnp.sqrt(second / (1.0 - beta_two**STEP)) + adam_eps)
    )
    return (first, second, values * (1.0 - rate * weight_decay) - rate * corrected)


def body(
    grid_input,
    grid_target,
    edge_input,
    senders,
    receivers,
    border_nodes,
    grid_to_mesh,
    mesh_to_grid,
    loss_mask,
    encoder_weights,
    encoder_first,
    encoder_second,
    processor_weights,
    processor_momentum,
    processor_average,
    norm_params,
    norm_first,
    norm_second,
    decoder_weights,
    decoder_first,
    decoder_second,
):
    bands, rows = lax.axis_size("band"), lax.axis_size("row")
    layers, blocks, rows_dev, width = processor_weights.shape
    channels = grid_input.shape[1]
    edge_channels = edge_input.shape[1]
    wide = -(-channels // 8) * 8
    grids, rim = grid_input.shape[0], border_nodes.shape[0]
    reads = mesh_to_grid.reshape(grids, -1).T
    indices = (jnp.stack([senders, receivers]),) + tuple(
        value[None, :] for value in (border_nodes, grid_to_mesh, loss_mask)
    ) + (reads,)
    flat_weights = processor_weights.reshape(layers * blocks, rows_dev, width)
    *saved, index = forward(
        bands,
        rows,
        grid_input.T,
        edge_input.T,
        indices,
        flat_weights,
        encoder_weights,
        norm_params,
    )
    inputs = (
        grid_input.T,
        grid_target.T,
        edge_input.T,
        index,
        encoder_weights,
        decoder_weights.T,
        norm_params,
    )
    grads, small, total, _ = backward(bands, rows, rim, rows_dev, inputs, saved)
    flat_momentum = processor_momentum.reshape(layers * blocks, rows_dev, width)
    total, ortho, small, _ = tail(
        bands,
        rows,
        grads,
        small.reshape(2, OWNER_CHIPS, -1, width),
        flat_momentum,
        total,
    )
    params_at = wide + 8
    decoder_at = params_at + layers * 8
    loss_total, mask_count, next_weights, next_momentum, next_average, encoder, decoder, params = finish(
        (wide, params_at, decoder_at, decoder_at + wide),
        edge_channels,
        (flat_weights, processor_average.reshape(flat_momentum.shape), flat_momentum, total, ortho),
        small.reshape(-1, width),
        saved[-1],
        (encoder_weights, encoder_first, encoder_second),
        (decoder_weights.T, decoder_first.T, decoder_second.T),
        (norm_params, norm_first, norm_second),
    )
    encoder_moment, encoder_square, encoder_values = encoder
    decoder_moment, decoder_square, decoder_values = (value.T for value in decoder)
    param_moment, param_square, param_values = params
    loss_total, mask_count = loss_total[0, 0], mask_count[0, 0]
    next_weights, next_momentum, next_average = (
        value.reshape(processor_weights.shape) for value in (next_weights, next_momentum, next_average)
    )
    return (
        loss_total,
        mask_count,
        next_weights,
        next_momentum,
        next_average,
        param_moment,
        param_square,
        param_values,
        encoder_moment,
        encoder_square,
        encoder_values,
        decoder_moment,
        decoder_square,
        decoder_values,
    )


def solution(mesh):
    return jax.shard_map(
        body,
        mesh=mesh,
        in_specs=(
            P("band", None),
            P("band", None),
            P("band", None),
            P("band"),
            P("band"),
            P("band"),
            P("band"),
            P("band"),
            P("band"),
            P(),
            P(),
            P(),
            P(None, None, "row", None),
            P(None, None, "row", None),
            P(None, None, "row", None),
            P(),
            P(),
            P(),
            P(),
            P(),
            P(),
        ),
        out_specs=(
            P(),
            P(),
            P(None, None, "row", None),
            P(None, None, "row", None),
            P(None, None, "row", None),
            P(),
            P(),
            P(),
            P(),
            P(),
            P(),
            P(),
            P(),
            P(),
        ),
        check_vma=False,
    )
```

```python
import functools

import jax
import jax.numpy as jnp
from jax import lax
from jax.experimental import pallas as pl
from jax.experimental.pallas import tpu as pltpu
from jax.sharding import PartitionSpec as P

STEP = 10
NODE_DEV = 320


coef_a = 3.4445
coef_b = -4.775
coef_c = 2.0315
momentum_decay = 0.95
muon_rate = 0.3
adam_rate = 0.02
param_rate = 0.1
beta_one = 0.9
beta_two = 0.95
adam_eps = 1e-08
weight_decay = 0.01
average_decay = 0.9
block_scale = (3.0**0.5, 3.0**0.5, 3.0**0.5, 1.0, 2.0**0.5, 2.0**0.5, 1.0)


MESH = pl.DeviceIdType.MESH
NN = (((1,), (0,)), ((), ()))
NT = (((1,), (1,)), ((), ()))
TN = (((0,), (0,)), ((), ()))
OWNER_CHIPS = 4
SLOTS = 3
VMEM_BYTES = 62 * 2**20
ANY = pl.BlockSpec(memory_space=pl.ANY)
VMEM = pl.BlockSpec(memory_space=pltpu.VMEM)


def pieces(value):
    high = value.astype(jnp.bfloat16)
    return high, (value - high.astype(jnp.float32)).astype(jnp.bfloat16)


def dot(left, right, dims=NN):
    return lax.dot_general(left, right, dims, preferred_element_type=jnp.float32)


def product(left, right, dims=NN):
    left_high, left_low = pieces(left)
    right_high, right_low = pieces(right)
    return (
        dot(left_high, right_high, dims)
        + dot(left_low, right_high, dims)
        + dot(left_high, right_low, dims)
    )


def slot_block(owner, slot):
    third = owner // 3
    last = third // 2
    return (1 - last) * (7 * (owner % 3) + 4 * third + slot) + last * (
        3 + 14 * (owner - 6) + 7 * slot
    )


def slot_used(owner, slot):
    return owner < (8, 7, 6)[slot]


def remote(src, dst, send_sem, recv_sem, device):
    return pltpu.make_async_remote_copy(
        src_ref=src,
        dst_ref=dst,
        send_sem=send_sem,
        recv_sem=recv_sem,
        device_id=device,
        device_id_type=MESH,
    )


def silu(value):
    return value / (1.0 + jnp.exp(-value))


def silu_back(value):
    gate = 1.0 / (1.0 + jnp.exp(-value))
    return gate * (1.0 + value * (1.0 - gate))


def normed(value):
    centered = value - jnp.mean(value, axis=-1, keepdims=True)
    scale = lax.rsqrt(jnp.mean(centered * centered, axis=-1, keepdims=True) + 1e-05)
    return centered * scale, scale


def normed_back(grad, norm, scale):
    inner = jnp.mean(grad * norm, axis=-1, keepdims=True)
    return (grad - jnp.mean(grad, axis=-1, keepdims=True) - norm * inner) * scale


def column(value):
    return jnp.sum(value, axis=0, keepdims=True)


def hot(mask):
    return jnp.where(mask, 1.0, 0.0).astype(jnp.bfloat16)


def chosen(choice, high, low, dims=NN):
    return dot(choice, high, dims) + dot(choice, low, dims)


def picked(choice, value):
    high, low = pieces(value)
    return chosen(choice, high, low)


def fill_rows(out_ref, make, tile=128):
    def step(t, carry):
        at = pl.multiple_of(t * tile, tile)
        out_ref[pl.ds(at, tile)] = make(at, tile)
        return carry

    lax.fori_loop(0, out_ref.shape[0] // tile, step, 0)


def iota(shape, axis):
    return lax.broadcasted_iota(jnp.int32, shape, axis)


SEND_ROW, RECV_ROW, BORDER_ROW, FEED_ROW, MASK_ROW, READ_ROW = range(6)


def edge_rows(edge_ref, size):
    empty = jnp.zeros((size - edge_ref.shape[0], edge_ref.shape[1]), jnp.float32)
    return jnp.concatenate([edge_ref[...], empty], axis=0)


def embedded_edges(edge_t, enc_ref, first, count, at, size):
    total = edge_t[pl.ds(at, size), 0:1] * enc_ref[pl.ds(first, 1)]
    for n in range(1, count):
        total = total + edge_t[pl.ds(at, size), n : n + 1] * enc_ref[pl.ds(first + n, 1)]
    return total


class Weights:
    def __init__(self, full_ref, stage, high, low, sem):
        self.full, self.stage, self.high, self.low, self.sem = full_ref, stage, high, low, sem

    def copy(self, block, slot):
        return pltpu.make_async_copy(self.full.at[block], self.stage.at[slot], self.sem.at[slot])

    def load(self, first, blocks):
        for n, block in enumerate(blocks[:2]):
            self.copy(first + block, n % 2).start()
        for n, block in enumerate(blocks):
            self.copy(first + block, n % 2).wait()
            high, low = pieces(self.stage[n % 2])
            self.high[block] = high
            self.low[block] = low
            if n + 2 < len(blocks):
                self.copy(first + blocks[n + 2], n % 2).start()

    def times(self, high, low, block, dims=NN):
        weight = self.high[block]
        return dot(high, weight, dims) + dot(low, weight, dims) + dot(high, self.low[block], dims)

    def apply(self, value, block, dims=NN):
        high, low = pieces(value)
        return self.times(high, low, block, dims)


def place(bands, rows):
    band = lax.axis_index("band")
    row = lax.axis_index("row")
    return band, row, band // 2, band % 2


def meet(partners):
    barrier = pltpu.get_barrier_semaphore()
    for partner in partners:
        pl.semaphore_signal(barrier, inc=1, device_id=partner, device_id_type=MESH)
    pl.semaphore_wait(barrier, len(partners))


def forward_kernel(
    bands,
    rows,
    chunks,
    tile,
    grid_ref,
    edge_ref,
    ends_ref,
    border_ref,
    feed_ref,
    mask_ref,
    read_ref,
    w_ref,
    enc_ref,
    param_ref,
    full_ref,
    before_ref,
    message_ref,
    edges_ref,
    embed_ref,
    nodes_ref,
    fed_ref,
    agg_ref,
    inner_ref,
    update_ref,
    table_ref,
    count_ref,
    index_ref,
    edge_buf,
    before_buf,
    message_buf,
    index_t,
    edge_t,
    pick,
    gather_t,
    src_high,
    src_low,
    high,
    low,
    stage,
    table,
    border_buf,
    count_buf,
    stage_sem,
    save_sem,
    own_sem,
    z_send,
    z_recv,
    a_send,
    a_recv,
    b_send,
    b_recv,
    s_send,
    s_recv,
    x_send,
    x_recv,
    p_send,
    p_recv,
):
    band, row, chip, core = place(bands, rows)
    chips = bands // 2
    layers, blocks = agg_ref.shape[0], w_ref.shape[0] // agg_ref.shape[0]
    rows_dev = w_ref.shape[1]
    nodes, width = fed_ref.shape
    edges = edge_buf.shape[1]
    border = border_buf.shape[1]
    grids = grid_ref.shape[1]
    weights = Weights(full_ref, stage, high, low, stage_sem)
    quad, pos = chip // 4, chip % 4
    pos_x, pos_y = pos + 1 - 2 * (pos % 2), pos + 2 - 4 * (pos // 2)
    sibling = (chip * 2 + 1 - core, row)
    near = (((quad * 4 + pos_x) * 2 + core, row), ((quad * 4 + pos_y) * 2 + core, row))
    near_pos = (pos_x, pos_y)
    partners = [((chip + j) % chips * 2 + core, row) for j in range(1, chips)] + [sibling]
    partners += [(band, (row + j) % rows) for j in range(1, rows)]
    meet(partners)

    piece = rows_dev // 8

    def part(g, from_row, of_core, of_pos, first=0, size=None):
        start, count = chunks[g]
        size = piece if size is None else size
        at = from_row * rows_dev + (of_core * 4 + of_pos) * piece + first
        return full_ref.at[pl.ds(start, count), pl.ds(pl.multiple_of(at, 8), size)]

    def z_copy(g, j, from_row):
        start, count = chunks[g]
        at = pl.multiple_of((core * 4 + pos) * piece, 8)
        return remote(
            w_ref.at[pl.ds(start, count), pl.ds(at, piece)],
            part(g, from_row, core, pos),
            z_send.at[g, j - 1],
            z_recv.at[g, j - 1],
            (band, (from_row + j) % rows),
        )

    def a_copy(g, side, j, of_pos):
        region = part(g, (row - j + rows) % rows, core, of_pos)
        return remote(region, region, a_send.at[g, side, j - 1], a_recv.at[g, side, j - 1], near[side])

    def b_copy(g, side, j, of_pos):
        half = piece // 2
        region = part(g, (row - j + rows) % rows, core, of_pos, side * half, half)
        return remote(region, region, b_send.at[g, side, j - 1], b_recv.at[g, side, j - 1], near[side])

    def s_copy(g, j, of_core):
        region = part(g, (row - j + rows) % rows, of_core, 0, 0, 4 * piece)
        return remote(region, region, s_send.at[g, j - 1], s_recv.at[g, j - 1], sibling)

    others = range(1, rows)
    far = 3 - pos

    def start_z(g):
        for j in others:
            z_copy(g, j, row).start()

    def start_a(g):
        for j in others:
            z_copy(g, j, (row - j + rows) % rows).wait_recv()
            for side in range(2):
                a_copy(g, side, j, pos).start()

    def start_b(g):
        for j in others:
            for side in range(2):
                a_copy(g, side, j, near_pos[side]).wait_recv()
                b_copy(g, 1 - side, j, near_pos[side]).start()

    def start_s(g):
        for j in others:
            for side in range(2):
                b_copy(g, side, j, far).wait_recv()
            s_copy(g, j, core).start()

    def ready(g):
        for j in others:
            s_copy(g, j, 1 - core).wait_recv()

    def tick(t):
        for g, stage_of in ((t - 5, ready), (t - 4, start_s), (t - 3, start_b), (t - 1, start_a), (t + 1, start_z)):
            if 0 <= g < len(chunks):
                stage_of(g)

    own = pltpu.make_async_copy(
        w_ref,
        full_ref.at[:, pl.ds(pl.multiple_of(row * rows_dev, rows_dev), rows_dev)],
        own_sem,
    )
    start_z(0)
    start_z(1)
    own.start()

    def table_of(e):
        return table_ref if (layers - e) % 2 == 0 else table

    def items(e):
        par = e % 2
        found = [(0, border_buf.at[par], lambda k, c: table_of(e).at[k, c])]
        if e == 0:
            found.append((1, count_buf, lambda k, c: count_ref.at[k, c]))
        return found

    def out(e, item, src, dst, j):
        return remote(
            src,
            dst(core, chip),
            x_send.at[e + item * 4, j - 1],
            x_recv.at[e + item * 4, j - 1],
            ((chip + j) % chips * 2 + core, row),
        )

    def across(e, item, src, dst, j, of_core):
        origin = (chip - j + chips) % chips
        return remote(
            src if j == 0 else dst(of_core, origin),
            dst(of_core, origin),
            p_send.at[e + item * 4, j],
            p_recv.at[e + item * 4, j],
            sibling,
        )

    def share(e, value):
        par = e % 2
        choice = hot(iota((border, nodes), 1) == index_t[pl.ds(0, border), BORDER_ROW : BORDER_ROW + 1])
        rows_out = picked(choice, value)
        border_buf[par] = rows_out
        table_of(e)[core, chip] = rows_out
        for item, src, dst in items(e):
            for j in range(1, chips):
                out(e, item, src, dst, j).start()
            across(e, item, src, dst, 0, core).start()

    def relay(e):
        for item, src, dst in items(e):
            for j in range(1, chips):
                out(e, item, src, dst, j).wait_recv()
                across(e, item, src, dst, j, core).start()

    def gathered(e):
        for item, src, dst in items(e):
            for j in range(chips):
                across(e, item, src, dst, j, 1 - core).wait_recv()
            for j in range(chips):
                across(e, item, src, dst, j, core).wait_send()
            for j in range(1, chips):
                out(e, item, src, dst, j).wait_send()

    def put_src(at, value):
        value_high, value_low = pieces(value)
        size = value.shape[0]
        src_high[pl.ds(at, size)] = value_high
        src_low[pl.ds(at, size)] = value_low

    def save(kind, layer, src):
        dst = (before_ref, message_ref, edges_ref, embed_ref)[kind]
        return pltpu.make_async_copy(src, dst if layer is None else dst.at[layer], save_sem.at[kind])

    def table_place(index):
        far = (index - nodes).astype(jnp.float32)
        owner = jnp.floor((far + 0.5) * (1.0 / border))
        at_chip = jnp.floor(owner * 0.5)
        moved = ((owner - 2.0 * at_chip) * chips + at_chip) * border + far - owner * border
        return jnp.where(index < nodes, index, moved.astype(jnp.int32) + nodes)

    index_ref[...] = jnp.zeros_like(index_ref)
    index_ref[SEND_ROW : SEND_ROW + 1] = table_place(ends_ref[0:1])
    index_ref[RECV_ROW : RECV_ROW + 1] = ends_ref[1:2]
    index_ref[BORDER_ROW : BORDER_ROW + 1, pl.ds(0, border)] = border_ref[...]
    index_ref[FEED_ROW : FEED_ROW + 1, pl.ds(0, grids)] = feed_ref[...]
    index_ref[MASK_ROW : MASK_ROW + 1, pl.ds(0, grids)] = mask_ref[...]
    index_ref[READ_ROW:, pl.ds(0, grids)] = table_place(read_ref[...])
    index_t[...] = index_ref[...].T
    embed_buf = before_buf.at[pl.ds(0, grids)]
    channels = grid_ref.shape[0]
    embed_buf[...] = product(grid_ref[...], enc_ref[pl.ds(0, channels)], TN)
    save(3, None, embed_buf).start()
    tick(1)
    feed = hot(iota((nodes, grids), 0) == index_ref[FEED_ROW : FEED_ROW + 1, pl.ds(0, grids)])
    fed = picked(feed, silu(embed_buf[...]))
    fed_ref[...] = fed
    nodes_ref[0] = normed(fed)[0]
    mask = index_ref[MASK_ROW : MASK_ROW + 1, pl.ds(0, grids)].astype(jnp.float32)
    counts = jnp.broadcast_to(jnp.sum(mask, axis=1, keepdims=True), count_buf.shape)
    count_buf[...] = counts
    count_ref[core, chip] = counts
    tick(2)
    edge_t[...] = edge_rows(edge_ref, edge_t.shape[1]).T

    def embed_edges(at, size):
        return silu(embedded_edges(edge_t, enc_ref, channels, edge_ref.shape[0], at, size))

    fill_rows(edge_buf.at[0], embed_edges)
    inputs = src_high.shape[0]
    near_inputs = 2 * nodes

    def choose(at, size):
        columns = iota((size, inputs), 1)
        sent = index_t[pl.ds(at, size), SEND_ROW : SEND_ROW + 1]
        received = index_t[pl.ds(at, size), RECV_ROW : RECV_ROW + 1] + nodes
        sent = jnp.where(sent < nodes, sent, sent + nodes)
        return hot(jnp.logical_or(columns == sent, columns == received))

    fill_rows(pick, choose)
    tick(3)

    def choose_receiver(at, size):
        return hot(iota((size, edges), 0) + at == index_ref[RECV_ROW : RECV_ROW + 1])

    fill_rows(gather_t, choose_receiver, 64)
    own.wait()
    tick(4)
    tick(5)
    for layer in range(layers):
        first = layer * blocks
        now, later = layer % 2, (layer + 1) % 2
        weights.load(first, (1, 2))
        node = nodes_ref[layer]
        node_high, node_low = pieces(node)
        sender = weights.times(node_high, node_low, 1)
        share(layer, sender)
        put_src(0, sender)
        put_src(nodes, weights.times(node_high, node_low, 2))
        if layer > 0:
            save(0, layer - 1, before_buf).wait()
            save(1, layer - 1, message_buf).wait()
            save(2, layer - 1, edge_buf.at[later]).wait()
        else:
            save(3, None, embed_buf).wait()
        save(2, layer, edge_buf.at[now]).start()
        tick(6 + 4 * layer)
        weights.load(first, (0,))

        def near_part(t):
            at = pl.ds(t * tile, tile)
            before_buf[at] = (
                weights.apply(edge_buf[now, at], 0)
                + chosen(
                    pick[at, pl.ds(0, near_inputs)],
                    src_high[pl.ds(0, near_inputs)],
                    src_low[pl.ds(0, near_inputs)],
                )
                + param_ref[layer, pl.ds(0, 1)]
            )

        near_part(0)
        tick(7 + 4 * layer)
        relay(layer)
        near_part(1)
        weights.load(first, (3, 4))
        inner = weights.times(node_high, node_low, 4) + param_ref[layer, pl.ds(4, 1)]
        gathered(layer)
        table_now = table_of(layer)
        for side in range(2):
            put_src(
                near_inputs + side * chips * border,
                table_now[side].reshape(chips * border, width),
            )
        agg_ref[layer] = jnp.zeros((nodes, width), jnp.float32)

        def edge_tile(t):
            at = pl.ds(t * tile, tile)
            far_inputs = pl.ds(near_inputs, inputs - near_inputs)
            before = before_buf[at] + chosen(
                pick[at, far_inputs], src_high[far_inputs], src_low[far_inputs]
            )
            before_buf[at] = before
            message = weights.apply(silu(before), 3) + param_ref[layer, pl.ds(1, 1)]
            message_buf[at] = message
            edge = (
                edge_buf[now, at]
                + normed(message)[0] * (1.0 + param_ref[layer, pl.ds(2, 1)])
                + param_ref[layer, pl.ds(3, 1)]
            )
            if layer < layers - 1:
                edge_buf[later, at] = edge
            agg_ref[layer] += picked(gather_t[:, at], edge)

        edge_tile(0)
        tick(8 + 4 * layer)
        edge_tile(1)
        save(0, layer, before_buf).start()
        save(1, layer, message_buf).start()
        weights.load(first, (5, 6))
        inner = inner + weights.apply(agg_ref[layer], 5)
        inner_ref[layer] = inner
        update = weights.apply(silu(inner), 6) + param_ref[layer, pl.ds(5, 1)]
        update_ref[layer] = update
        nodes_ref[layer + 1] = (
            node
            + normed(update)[0] * (1.0 + param_ref[layer, pl.ds(6, 1)])
            + param_ref[layer, pl.ds(7, 1)]
        )
        tick(9 + 4 * layer)
    share(layers, nodes_ref[layers])
    relay(layers)
    gathered(layers)
    save(0, layers - 1, before_buf).wait()
    save(1, layers - 1, message_buf).wait()
    save(2, layers - 1, edge_buf.at[(layers - 1) % 2]).wait()
    for g in range(len(chunks)):
        for j in others:
            z_copy(g, j, row).wait_send()
            for side in range(2):
                a_copy(g, side, j, pos).wait_send()
                b_copy(g, 1 - side, j, near_pos[side]).wait_send()
            s_copy(g, j, core).wait_send()


def forward(bands, rows, grid, edge, indices, blocks, enc, params):
    f32, bf16 = jnp.float32, jnp.bfloat16
    dma = pltpu.SemaphoreType.DMA
    width = blocks.shape[2]
    edges, grids = edge.shape[1], grid.shape[1]
    layers = params.shape[0]
    rim = indices[1].shape[1]
    index_rows = READ_ROW + indices[4].shape[0]
    nodes = NODE_DEV
    chips = bands // 2
    inputs = 2 * nodes + bands * rim
    each = blocks.shape[0] // layers
    chunks = []
    for layer in range(layers):
        chunks += [(layer * each + first, size) for first, size in ((1, 2), (0, 1), (3, 2), (5, 2))]
    groups = len(chunks)
    tile = edges // 2

    def array(*shape):
        return jax.ShapeDtypeStruct(shape, f32)

    return pl.pallas_call(
        functools.partial(forward_kernel, bands, rows, tuple(chunks), tile),
        out_shape=(
            array(blocks.shape[0], width, width),
            array(layers, edges, width),
            array(layers, edges, width),
            array(layers, edges, width),
            array(grids, width),
            array(layers + 1, nodes, width),
            array(nodes, width),
            array(layers, nodes, width),
            array(layers, nodes, width),
            array(layers, nodes, width),
            array(2, chips, rim, width),
            array(2, chips, 8, 128),
            jax.ShapeDtypeStruct((index_rows, edges), jnp.int32),
        ),
        in_specs=[VMEM] * 10,
        out_specs=[ANY] * 5 + [VMEM] * 8,
        scratch_shapes=[
            pltpu.VMEM((2, edges, width), f32),
            pltpu.VMEM((edges, width), f32),
            pltpu.VMEM((edges, width), f32),
            pltpu.VMEM((edges, index_rows), jnp.int32),
            pltpu.VMEM((edges, 8), f32),
            pltpu.VMEM((edges, inputs), bf16),
            pltpu.VMEM((nodes, edges), bf16),
            pltpu.VMEM((inputs, width), bf16),
            pltpu.VMEM((inputs, width), bf16),
            pltpu.VMEM((each, width, width), bf16),
            pltpu.VMEM((each, width, width), bf16),
            pltpu.VMEM((2, width, width), f32),
            pltpu.VMEM((2, chips, rim, width), f32),
            pltpu.VMEM((2, rim, width), f32),
            pltpu.VMEM((8, 128), f32),
            dma((2,)),
            dma((4,)),
            dma,
            dma((groups, rows - 1)),
            dma((groups, rows - 1)),
            dma((groups, 2, rows - 1)),
            dma((groups, 2, rows - 1)),
            dma((groups, 2, rows - 1)),
            dma((groups, 2, rows - 1)),
            dma((groups, rows - 1)),
            dma((groups, rows - 1)),
            dma((5, chips - 1)),
            dma((5, chips - 1)),
            dma((5, chips)),
            dma((5, chips)),
        ],
        compiler_params=pltpu.CompilerParams(
            collective_id=1, has_side_effects=True, vmem_limit_bytes=VMEM_BYTES
        ),
        name="forward",
    )(
        grid,
        edge,
        *indices,
        blocks,
        enc,
        params,
    )


def groups(layer):
    return (
        (layer, 0, 0, 3),
        (3 + layer, 0, 4, 3),
        (6 + layer // 2, layer % 2, 3, 1),
    )


class Reducer:
    def __init__(self, bands, layer, at, grads, sib, land, total, sems):
        band, row, self.chip, self.core = place(bands, 1)
        self.row = row
        self.chips = bands // 2
        self.sibling = (self.chip * 2 + 1 - self.core, row)
        self.layer, self.at = layer, at
        self.grads, self.sib, self.land, self.total = grads, sib, land, total
        (self.c_send, self.c_recv, self.r_send, self.r_recv) = sems[:4]
        (self.o_send, self.o_recv, self.p_send, self.p_recv, self.k_sem) = sems[4:]

    def each(self):
        for q, (owner, slot, block, count) in enumerate(groups(self.layer)):
            yield q, owner // 2, owner % 2, slot, pl.ds(block, count), count

    def to_sibling(self, q, rows):
        return remote(
            self.grads.at[rows],
            self.sib.at[rows],
            self.c_send.at[self.at, q],
            self.c_recv.at[self.at, q],
            self.sibling,
        )

    def to_owner(self, q, at_chip, at_core, rows, count):
        step = (at_chip - self.chip + self.chips) % self.chips
        return remote(
            self.grads.at[rows],
            self.land.at[self.at, step - 1, pl.ds(0, count)],
            self.r_send.at[self.at, q],
            self.r_recv.at[self.at, step - 1],
            (at_chip * 2 + at_core, self.row),
        )

    def to_chip(self, q, rows, j):
        return remote(
            self.grads.at[rows],
            self.total.at[rows],
            self.o_send.at[self.at, j - 1],
            self.o_recv.at[self.at, q],
            ((self.chip + j) % self.chips * 2 + self.core, self.row),
        )

    def across(self, q, rows, src):
        return remote(
            src.at[rows],
            self.total.at[rows],
            self.p_send.at[self.at, q],
            self.p_recv.at[self.at, q],
            self.sibling,
        )

    def keep(self, rows):
        return pltpu.make_async_copy(self.grads.at[rows], self.total.at[rows], self.k_sem.at[self.at])

    def start(self):
        for q, at_chip, at_core, slot, rows, count in self.each():
            @pl.when(self.core != at_core)
            def _():
                self.to_sibling(q, rows).start()

    def pair(self):
        for q, at_chip, at_core, slot, rows, count in self.each():
            @pl.when(self.core == at_core)
            def _():
                self.to_sibling(q, rows).wait_recv()
                self.grads[rows] += self.sib[rows]

                @pl.when(self.chip != at_chip)
                def _():
                    self.to_owner(q, at_chip, at_core, rows, count).start()

    def reduce(self, take, load):
        for q, at_chip, at_core, slot, rows, count in self.each():
            @pl.when(jnp.logical_and(self.core == at_core, self.chip == at_chip))
            def _():
                value = self.grads[rows]
                for j in range(1, self.chips):
                    landed = self.land.at[self.at, j - 1, pl.ds(0, count)]
                    remote(
                        landed,
                        landed,
                        self.r_send.at[self.at, q],
                        self.r_recv.at[self.at, j - 1],
                        self.sibling,
                    ).wait_recv()
                    value = value + load(landed, count)
                self.grads[rows] = value
                take(slot, count, value)
                for j in range(1, self.chips):
                    self.to_chip(q, rows, j).start()
                self.across(q, rows, self.grads).start()
                self.keep(rows).start()

    def relay(self):
        for q, at_chip, at_core, slot, rows, count in self.each():
            @pl.when(jnp.logical_and(self.core == at_core, self.chip != at_chip))
            def _():
                self.to_chip(q, rows, 1).wait_recv()
                self.across(q, rows, self.total).start()

    def finish(self):
        for q, at_chip, at_core, slot, rows, count in self.each():
            @pl.when(self.core != at_core)
            def _():
                self.to_sibling(q, rows).wait_send()
                self.across(q, rows, self.total).wait_recv()

            @pl.when(self.core == at_core)
            def _():
                self.across(q, rows, self.total).wait_send()

                @pl.when(self.chip != at_chip)
                def _():
                    self.to_owner(q, at_chip, at_core, rows, count).wait_send()

                @pl.when(self.chip == at_chip)
                def _():
                    for j in range(1, self.chips):
                        self.to_chip(q, rows, j).wait_send()
                    self.keep(rows).wait()


def reducer_sems(count, chips):
    dma = pltpu.SemaphoreType.DMA
    return [
        dma((count, 3)),
        dma((count, 3)),
        dma((count, 3)),
        dma((count, chips - 1)),
        dma((count, chips - 1)),
        dma((count, 3)),
        dma((count, 3)),
        dma((count, 3)),
        dma((count,)),
    ]


class Spreader:
    def __init__(self, bands, at, grads, sib, land, landed, total, sems):
        band, self.row, self.chip, self.core = place(bands, 1)
        self.chips = bands // 2
        self.sibling = (self.chip * 2 + 1 - self.core, self.row)
        self.at = at
        self.grads, self.sib, self.land, self.landed, self.total = grads, sib, land, landed, total
        self.half = grads.shape[1] // 2
        self.piece = self.half // OWNER_CHIPS
        (self.c_sem, self.r_send, self.r_recv, self.o_send, self.o_recv, self.p_sem, self.k_sem) = sems

    def rows(self, core):
        return pl.ds(pl.multiple_of(core * self.half, 8), self.half)

    def part(self, core, chip):
        return pl.ds(pl.multiple_of(core * self.half + chip * self.piece, 8), self.piece)

    def to_sibling(self):
        return remote(
            self.grads.at[:, self.rows(1 - self.core)],
            self.sib,
            self.c_sem.at[self.at, 0],
            self.c_sem.at[self.at, 1],
            self.sibling,
        )

    def to_owner(self, chip):
        step = (chip - self.chip + self.chips) % self.chips
        return remote(
            self.grads.at[:, self.part(self.core, chip)],
            self.land.at[step - 1],
            self.r_send.at[self.at, chip],
            self.r_recv.at[self.at, step - 1],
            (chip * 2 + self.core, self.row),
        )

    def to_chip(self, j, chip):
        part = self.part(self.core, chip)
        return remote(
            self.grads.at[:, part],
            self.total.at[:, part],
            self.o_send.at[self.at, j - 1],
            self.o_recv.at[self.at, chip],
            ((self.chip + j) % self.chips * 2 + self.core, self.row),
        )

    def keep(self):
        part = self.part(self.core, self.chip)
        return pltpu.make_async_copy(
            self.grads.at[:, part], self.total.at[:, part], self.k_sem.at[self.at, 0]
        )

    def across(self, core):
        region = self.total.at[:, self.rows(core)]
        return remote(region, region, self.p_sem.at[self.at, 0], self.p_sem.at[self.at, 1], self.sibling)

    def owned(self, body):
        if self.chips == OWNER_CHIPS:
            body()
        else:
            pl.when(self.chip < OWNER_CHIPS)(body)

    def start(self):
        self.to_sibling().start()

    def pair(self):
        self.to_sibling().wait()
        self.grads[:, self.rows(self.core)] += self.sib[...]
        for chip in range(OWNER_CHIPS):
            pl.when(self.chip != chip)(self.to_owner(chip).start)

    def reduce(self):
        def body():
            part = self.part(self.core, self.chip)
            for j in range(1, self.chips):
                remote(
                    self.landed,
                    self.land.at[j - 1],
                    self.r_send.at[self.at, 0],
                    self.r_recv.at[self.at, j - 1],
                    self.sibling,
                ).wait_recv()
                copy = pltpu.make_async_copy(self.land.at[j - 1], self.landed, self.k_sem.at[self.at, 1])
                copy.start()
                copy.wait()
                self.grads[:, part] += self.landed[...]
            for j in range(1, self.chips):
                self.to_chip(j, self.chip).start()
            self.keep().start()

        self.owned(body)

    def relay(self):
        for chip in range(OWNER_CHIPS):
            pl.when(self.chip != chip)(self.to_chip(1, chip).wait_recv)
        self.owned(lambda: self.keep().wait())
        self.across(self.core).start()

    def finish(self):
        self.across(self.core).wait_send()
        self.across(1 - self.core).wait_recv()
        for chip in range(OWNER_CHIPS):
            pl.when(self.chip != chip)(self.to_owner(chip).wait_send)

        def body():
            for j in range(1, self.chips):
                self.to_chip(j, self.chip).wait_send()

        self.owned(body)


def spreader_sems(count, chips):
    dma = pltpu.SemaphoreType.DMA
    return [
        dma((count, 2)),
        dma((count, OWNER_CHIPS)),
        dma((count, chips - 1)),
        dma((count, chips - 1)),
        dma((count, OWNER_CHIPS)),
        dma((count, 2)),
        dma((count, 2)),
    ]


def backward_kernel(
    bands,
    rows,
    each,
    tile,
    grid_ref,
    target_ref,
    edge_ref,
    index_ref,
    enc_ref,
    dec_ref,
    param_ref,
    full_ref,
    before_ref,
    message_ref,
    edges_ref,
    embed_ref,
    nodes_ref,
    fed_ref,
    agg_ref,
    inner_ref,
    update_ref,
    table_ref,
    count_ref,
    grads_ref,
    small_ref,
    total_ref,
    land_grads,
    edge_buf,
    before_buf,
    message_buf,
    node_buf,
    agg_buf,
    inner_buf,
    update_buf,
    index_t,
    edge_t,
    features,
    edge_grad,
    node_grad,
    part_high,
    part_low,
    pick_t,
    gather,
    high,
    low,
    stage,
    table,
    sib,
    land,
    grads_buf,
    sib_grads,
    landed_buf,
    stage_sem,
    load_sem,
    d_send,
    d_recv,
    r_send,
    r_recv,
    *sems,
):
    band, row, chip, core = place(bands, rows)
    chips = bands // 2
    layers = param_ref.shape[0]
    nodes, width = node_buf.shape
    edges = edge_buf.shape[0]
    grids = grid_ref.shape[1]
    border = table.shape[2]
    table_rows = bands * border
    rows_dev = grads_ref.shape[1]
    weights = Weights(full_ref, stage, high, low, stage_sem)
    sibling = (chip * 2 + 1 - core, row)
    partners = [((chip + j) % chips * 2 + core, row) for j in range(1, chips)] + [sibling]
    own_rows = pl.ds(pl.multiple_of(row * rows_dev, rows_dev), rows_dev)

    def load(kind, layer):
        src = (before_ref, message_ref, edges_ref, agg_ref, inner_ref, update_ref, nodes_ref)[kind]
        dst = (before_buf, message_buf, edge_buf, agg_buf, inner_buf, update_buf, node_buf)[kind]
        return pltpu.make_async_copy(src.at[layer], dst, load_sem.at[kind])

    table_load = pltpu.make_async_copy(table_ref, table, load_sem.at[7])
    embed_buf = before_buf.at[pl.ds(0, grids)]
    fed_buf = agg_buf
    embed_load = pltpu.make_async_copy(embed_ref, embed_buf, load_sem.at[8])
    fed_load = pltpu.make_async_copy(fed_ref, fed_buf, load_sem.at[9])
    load(6, layers).start()
    table_load.start()
    for kind in range(6):
        load(kind, layers - 1).start()
    meet(partners)

    def to_sibling(e):
        return remote(table.at[1 - core], sib.at[e % 2], d_send.at[e], d_recv.at[e], sibling)

    def to_band(e, j):
        to = (chip + j) % chips
        return remote(
            table.at[core, to], land.at[e % 2, j - 1], r_send.at[e, j - 1], r_recv.at[e, j - 1], (to * 2 + core, row)
        )

    def give(e):
        to_sibling(e).wait()
        table[core] += sib[e % 2]
        for j in range(1, chips):
            to_band(e, j).start()

    def returned(e):
        total = table[core, chip]
        for j in range(1, chips):
            to_band(e, j).wait_recv()
            total = total + land[e % 2, j - 1]
        for j in range(1, chips):
            to_band(e, j).wait_send()
        return picked(hot(iota((nodes, border), 0) == index_ref[BORDER_ROW : BORDER_ROW + 1, pl.ds(0, border)]), total)

    def put_table(value_high, value_low, count):
        side_rows = chips * border
        for side in range(2):
            choice = pick_t[pl.ds(nodes + side * side_rows, side_rows), pl.ds(0, count)]
            table[side] = chosen(choice, value_high, value_low).reshape(chips, border, width)

    def grads_of(layer):
        return grads_buf.at[layer - 1] if layer > 0 else grads_ref

    reducers = [None] + [
        Spreader(
            bands,
            layer - 1,
            grads_of(layer),
            sib_grads,
            land_grads.at[layer - 1],
            landed_buf,
            total_ref.at[pl.ds(layer * each, each)],
            sems,
        )
        for layer in range(1, layers)
    ]

    def put_grad(layer, block, value):
        grads_of(layer)[block] = value

    def add_grad(layer, block, value):
        grads_of(layer)[block] += value

    index_t[...] = index_ref[...].T

    def choose_reads(at, size):
        line = iota((size, grids), 0) + at
        counts = jnp.zeros((size, grids), jnp.float32)
        for way in range(READ_ROW, index_ref.shape[0]):
            counts = counts + jnp.where(line == index_ref[way : way + 1, pl.ds(0, grids)], 1.0, 0.0)
        return counts.astype(jnp.bfloat16)

    def fill_reads(t, carry):
        at = pl.multiple_of(t * 64, 64)
        pick_t[pl.ds(at, 64), pl.ds(0, grids)] = choose_reads(at, 64)
        return carry

    lax.fori_loop(0, (nodes + table_rows) // 64, fill_reads, 0)

    def choose_gather(at, size):
        return hot(iota((size, nodes), 1) == index_t[pl.ds(at, size), RECV_ROW : RECV_ROW + 1])

    fill_rows(gather, choose_gather)
    load(6, layers).wait()
    table_load.wait()
    reads = edge_grad.at[pl.ds(0, grids)]
    own_high, own_low = pieces(node_buf[...])
    reads[...] = chosen(pick_t[pl.ds(0, nodes), pl.ds(0, grids)], own_high, own_low, TN)
    side_rows = chips * border
    for side in range(2):
        side_high, side_low = pieces(table[side].reshape(side_rows, width))
        choice = pick_t[pl.ds(nodes + side * side_rows, side_rows), pl.ds(0, grids)]
        reads[...] += chosen(choice, side_high, side_low, TN)
    load(6, layers - 1).start()
    weights.load((layers - 1) * each, (6, 4, 5, 3, 0, 1, 2))
    active = silu(reads[...])
    mask = index_ref[MASK_ROW : MASK_ROW + 1, pl.ds(0, grids)].astype(jnp.float32)
    missed = grid_ref[...] + product(dec_ref[...], active, NT) - target_ref[...]
    total = jnp.sum(jnp.sum(count_ref[:, :, 0:1, 0:1], axis=0), axis=0)
    masked = mask * missed
    loss = jnp.sum(column(masked * missed), axis=1, keepdims=True)
    grad = (2.0 / total) * masked
    channels = grid_ref.shape[0]
    encs = -(-channels // 8) * 8
    decs = encs
    decoder_at = encs + 8 + layers * 8
    small_ref[pl.ds(decoder_at, channels)] = product(grad, active)
    tail_rows = small_ref.shape[0] - decoder_at - decs
    small_ref[pl.ds(decoder_at + decs, tail_rows)] = jnp.broadcast_to(loss, (tail_rows, width))
    read_high, read_low = pieces(product(grad, dec_ref[...], TN) * silu_back(reads[...]))
    put_table(read_high, read_low, grids)
    to_sibling(0).start()
    node_grad[...] = chosen(pick_t[pl.ds(0, nodes), pl.ds(0, grids)], read_high, read_low)

    def choose(at, size):
        line = iota((size, edges), 0) + at
        sent = line == index_ref[SEND_ROW : SEND_ROW + 1]
        received = line == index_ref[RECV_ROW : RECV_ROW + 1] + (nodes + table_rows)
        return hot(jnp.logical_or(sent, received))

    fill_rows(pick_t, choose, 64)
    give(0)
    edge_grad[...] = jnp.zeros_like(edge_grad)
    node_grad[...] += returned(0)

    for depth in range(layers):
        layer = layers - 1 - depth
        e = depth + 1
        base = encs + 8 + layer * 8

        def put_param(index, value, base=base):
            small_ref[pl.ds(base + index, 1)] = value

        def add_param(index, value, base=base):
            small_ref[pl.ds(base + index, 1)] += value

        for kind in (3, 4, 5, 6):
            load(kind, layer).wait()
        if layer + 1 < layers:
            reducers[layer + 1].pair()
        if layer + 2 < layers:
            reducers[layer + 2].reduce()
        grad = node_grad[...]
        norm, scale = normed(update_buf[...])
        put_param(7, column(grad))
        put_param(6, column(grad * norm))
        grad = normed_back(grad * (1.0 + param_ref[layer, pl.ds(6, 1)]), norm, scale)
        put_param(5, column(grad))
        grad_high, grad_low = pieces(grad)
        put_grad(layer, 6, product(silu(inner_buf[:, own_rows]), grad, TN))
        grad = weights.times(grad_high, grad_low, 6, NT) * silu_back(inner_buf[...])
        put_param(4, column(grad))
        grad_high, grad_low = pieces(grad)
        put_grad(layer, 4, product(node_buf[:, own_rows], grad, TN))
        put_grad(layer, 5, product(agg_buf[:, own_rows], grad, TN))
        node_grad[...] += weights.times(grad_high, grad_low, 4, NT)
        agg_high, agg_low = pieces(weights.times(grad_high, grad_low, 5, NT))
        for kind in (0, 1, 2):
            load(kind, layer).wait()
        for index in range(4):
            put_param(index, jnp.zeros((1, width), jnp.float32))
        for block in (0, 3):
            put_grad(layer, block, jnp.zeros((rows_dev, width), jnp.float32))

        def edge_tile(t, carry):
            at = pl.ds(pl.multiple_of(t * tile, tile), tile)
            grad = edge_grad[at] + chosen(gather[at], agg_high, agg_low)
            edge_grad[at] = grad
            norm, scale = normed(message_buf[at])
            add_param(3, column(grad))
            add_param(2, column(grad * norm))
            grad = normed_back(grad * (1.0 + param_ref[layer, pl.ds(2, 1)]), norm, scale)
            add_param(1, column(grad))
            grad_high, grad_low = pieces(grad)
            add_grad(layer, 3, product(silu(before_buf[at, own_rows]), grad, TN))
            grad = weights.times(grad_high, grad_low, 3, NT) * silu_back(before_buf[at])
            add_param(0, column(grad))
            add_grad(layer, 0, product(edge_buf[at, own_rows], grad, TN))
            grad_high, grad_low = pieces(grad)
            part_high[at] = grad_high
            part_low[at] = grad_low
            return carry

        lax.fori_loop(0, edges // tile, edge_tile, 0)
        if layer > 0:
            for kind in range(6):
                load(kind, layer - 1).start()
        else:
            embed_load.start()
            fed_load.start()
        put_table(part_high[...], part_low[...], edges)
        to_sibling(e).start()
        sender = chosen(pick_t[pl.ds(0, nodes)], part_high[...], part_low[...])
        give(e)
        received = chosen(pick_t[pl.ds(nodes + table_rows, nodes)], part_high[...], part_low[...])

        def edge_back(t, carry):
            at = pl.ds(pl.multiple_of(t * tile, tile), tile)
            edge_grad[at] += weights.times(part_high[at], part_low[at], 0, NT)
            return carry

        lax.fori_loop(0, edges // tile, edge_back, 0)
        put_grad(layer, 2, product(node_buf[:, own_rows], received, TN))
        node_grad[...] += weights.apply(received, 2, NT)
        if layer > 0:
            weights.load((layer - 1) * each, (6, 4, 5, 3, 0))
        sender = sender + returned(e)
        put_grad(layer, 1, product(node_buf[:, own_rows], sender, TN))
        node_grad[...] += weights.apply(sender, 1, NT)
        if layer > 0:
            load(6, layer - 1).start()
            weights.load((layer - 1) * each, (1, 2))
            reducers[layer].start()

    reducers[1].reduce()
    embed_load.wait()
    fed_load.wait()
    norm, scale = normed(fed_buf[...])
    fed_grad = normed_back(node_grad[...], norm, scale)
    feed = hot(iota((grids, nodes), 1) == index_t[pl.ds(0, grids), FEED_ROW : FEED_ROW + 1])
    grad = picked(feed, fed_grad) * silu_back(embed_buf[...])
    small_ref[pl.ds(0, channels)] = product(grid_ref[...], grad)
    small_ref[pl.ds(encs, 8)] = jnp.zeros((8, width), jnp.float32)
    features[...] = edge_rows(edge_ref, 8)
    edge_t[...] = features[...].T

    def embed_back(t, carry):
        first = pl.multiple_of(t * 128, 128)
        at = pl.ds(first, 128)
        embed = embedded_edges(edge_t, enc_ref, channels, edge_ref.shape[0], first, 128)
        grad = edge_grad[at] * silu_back(embed)
        small_ref[pl.ds(encs, 8)] += product(features[:, at], grad)
        return carry

    lax.fori_loop(0, edges // 128, embed_back, 0)
    for layer in range(layers - 1, 0, -1):
        reducers[layer].relay()
    for layer in range(1, layers):
        reducers[layer].finish()


def backward(bands, rows, rim, rows_dev, inputs, saved):
    f32, bf16 = jnp.float32, jnp.bfloat16
    dma = pltpu.SemaphoreType.DMA
    grid, edge, index, decoder, params = inputs[0], inputs[2], inputs[3], inputs[5], inputs[6]
    layers = params.shape[0]
    full = saved[0]
    width = full.shape[2]
    each = full.shape[0] // layers
    edges, grids = edge.shape[1], grid.shape[1]
    nodes = NODE_DEV
    chips = bands // 2
    padded = -(-grid.shape[0] // 8) * 8
    small = padded + 8 + layers * 8 + padded + 8
    small = -(-small // (16 * OWNER_CHIPS)) * 16 * OWNER_CHIPS
    tile = edges
    node = pltpu.VMEM((nodes, width), f32)
    return pl.pallas_call(
        functools.partial(backward_kernel, bands, rows, each, tile),
        out_shape=(
            jax.ShapeDtypeStruct((each, rows_dev, width), f32),
            jax.ShapeDtypeStruct((small, width), f32),
            jax.ShapeDtypeStruct((full.shape[0], rows_dev, width), f32),
            jax.ShapeDtypeStruct((layers - 1, chips - 1, each, rows_dev // 8, width), f32),
        ),
        in_specs=[VMEM] * 7 + [ANY] * 11 + [VMEM],
        out_specs=[VMEM, VMEM, ANY, ANY],
        scratch_shapes=[
            pltpu.VMEM((edges, width), f32),
            pltpu.VMEM((edges, width), f32),
            pltpu.VMEM((edges, width), f32),
            node,
            node,
            node,
            node,
            pltpu.VMEM((edges, index.shape[0]), jnp.int32),
            pltpu.VMEM((edges, 8), f32),
            pltpu.VMEM((8, edges), f32),
            pltpu.VMEM((edges, width), f32),
            node,
            pltpu.VMEM((edges, width), bf16),
            pltpu.VMEM((edges, width), bf16),
            pltpu.VMEM((2 * nodes + bands * rim, edges), bf16),
            pltpu.VMEM((edges, nodes), bf16),
            pltpu.VMEM((each, width, width), bf16),
            pltpu.VMEM((each, width, width), bf16),
            pltpu.VMEM((2, width, width), f32),
            pltpu.VMEM((2, chips, rim, width), f32),
            pltpu.VMEM((2, chips, rim, width), f32),
            pltpu.VMEM((2, chips - 1, rim, width), f32),
            pltpu.VMEM((layers - 1, each, rows_dev, width), f32),
            pltpu.VMEM((each, rows_dev // 2, width), f32),
            pltpu.VMEM((each, rows_dev // 8, width), f32),
            dma((2,)),
            dma((10,)),
            dma((layers + 1,)),
            dma((layers + 1,)),
            dma((layers + 1, chips - 1)),
            dma((layers + 1, chips - 1)),
            ]
        + spreader_sems(layers - 1, chips),
        compiler_params=pltpu.CompilerParams(
            collective_id=2, has_side_effects=True, vmem_limit_bytes=VMEM_BYTES
        ),
        name="backward",
    )(*inputs, *saved)


def newton(matrix, result, first, count, arrive, leave, gram, poly, temp, later):
    gram[...] = jnp.zeros_like(gram)

    def add_gram(i, carry):
        arrive(first + i)
        block = matrix[first + i]
        gram[...] += product(block, block, TN)
        return carry

    lax.fori_loop(0, count, add_gram, 0)
    diagonal = iota(gram.shape, 0) == iota(gram.shape, 1)
    squares = column(jnp.where(diagonal, gram[...], 0.0))
    scale = 1.0 / (jnp.sqrt(jnp.sum(squares, axis=1, keepdims=True)) + 1e-07)
    gram[...] = gram[...] * (scale * scale)
    poly[...] = coef_b * gram[...] + coef_c * product(gram[...], gram[...])
    temp[...] = coef_a * gram[...] + product(gram[...], poly[...])
    gram[...] = coef_a * temp[...] + product(temp[...], poly[...])
    later[...] = coef_b * gram[...] + coef_c * product(gram[...], gram[...])
    temp[...] = coef_a * (poly[...] + later[...]) + product(poly[...], later[...])

    def last(i, carry):
        block = matrix[first + i] * scale
        result[first + i] = (coef_a * coef_a) * block + product(block, temp[...])
        leave(first + i)
        return carry

    lax.fori_loop(0, count, last, 0)


def late_slot(owner, slot):
    return owner in (0, 3) or (owner == 6 and slot == 0)


def tail_kernel(
    bands,
    rows,
    grads_ref,
    small_ref,
    mom_ref,
    given_ref,
    total_ref,
    ortho_ref,
    shared_ref,
    land,
    grads,
    sib,
    landed_buf,
    sib_small,
    part_small,
    land_small,
    held,
    matrix,
    result,
    back,
    gram,
    poly,
    temp,
    later,
    load_sem,
    landed_sem,
    m_pair,
    m_red_send,
    m_red_recv,
    m_out_send,
    m_out_recv,
    m_pass,
    m_keep,
    up_send,
    up_recv,
    down_send,
    down_recv,
    o_send,
    o_recv,
    p_send,
    p_recv,
    keep_sem,
    *sems,
):
    band, row, chip, core = place(bands, rows)
    chips = bands // 2
    rows_dev = held.shape[1]
    sibling = (chip * 2 + 1 - core, row)
    partners = [((chip + j) % chips * 2 + core, row) for j in range(1, chips)] + [sibling]
    partners += [(band, (row + j) % rows) for j in range(1, rows)]
    reducer = Reducer(bands, 0, 0, grads, sib.at[0], land, total_ref.at[pl.ds(0, grads.shape[0])], sems)
    grads[...] = grads_ref[...]

    def load(slot):
        return pltpu.make_async_copy(
            mom_ref.at[slot_block(band, slot)], held.at[slot], load_sem.at[slot]
        )

    owned = [band < (8, 7, 6)[slot] for slot in range(SLOTS)]
    third = band // 3
    last = [jnp.logical_and(band < 7, band % 3 == 0)]
    last += [jnp.logical_and(band < 6, band % 3 == 0)] * 2
    for slot in range(SLOTS):
        pl.when(owned[slot])(load(slot).start)
    meet(partners)

    small_pair = remote(small_ref.at[1 - core], sib_small, m_pair.at[0], m_pair.at[1], sibling)

    def small_to(at):
        step = (at - chip + chips) % chips
        return remote(
            part_small.at[at],
            land_small.at[step - 1],
            m_red_send.at[at],
            m_red_recv.at[step - 1],
            (at * 2 + core, row),
        )

    def small_out(at, j):
        home = shared_ref.at[core * OWNER_CHIPS + at]
        return remote(
            part_small.at[at],
            home,
            m_out_send.at[j - 1],
            m_out_recv.at[at],
            ((chip + j) % chips * 2 + core, row),
        )

    def small_across(at, of_core, local):
        home = shared_ref.at[of_core * OWNER_CHIPS + at]
        return remote(
            part_small.at[at] if local else home, home, m_pass.at[0, at], m_pass.at[1, at], sibling
        )

    def small_keep(at):
        return pltpu.make_async_copy(
            part_small.at[at], shared_ref.at[core * OWNER_CHIPS + at], m_keep
        )

    row_a = rows // 2 - 1 + core
    row_b = rows // 2 - core
    split_at = 3 - third

    def home(slot):
        return row_a + (slot + third) // 3 * (row_b - row_a)

    def rows_of(at_row):
        return pl.ds(pl.multiple_of(at_row * rows_dev, rows_dev), rows_dev)

    def up(slot, from_row):
        step = (from_row - home(slot) + rows) % rows
        return remote(
            held.at[slot],
            matrix.at[slot, rows_of(from_row)],
            up_send.at[slot],
            up_recv.at[slot, step],
            (band, home(slot)),
        )

    def down(slot, to_row):
        step = (to_row - home(slot) + rows) % rows
        return remote(
            result.at[slot, rows_of(to_row)],
            back.at[slot],
            down_send.at[slot, step],
            down_recv.at[slot],
            (band, to_row),
        )

    def momentum(slot, value):
        load(slot).wait()
        held[slot] = momentum_decay * held[slot] + value

        @pl.when(row == home(slot))
        def _():
            matrix[slot, rows_of(row)] = held[slot]

        @pl.when(row != home(slot))
        def _():
            up(slot, row).start()

    def solve(when):
        own_b = jnp.logical_and(row == row_b, jnp.logical_and(band > 2, band < 7))
        own_b = jnp.logical_and(own_b, jnp.logical_not(band == 3) if when == 0 else band == 3)
        own_a = jnp.logical_and(row == row_a, band < 8)
        own_a = jnp.logical_and(own_a, jnp.logical_not(last[0]) if when == 0 else last[0])

        @pl.when(jnp.logical_or(own_a, own_b))
        def _():
            second = (row - row_a) * (row_b - row_a)
            first = second * split_at
            count = (1 - second) * split_at + second

            def arrive(slot):
                for step in range(1, rows):
                    up(slot, (row + step) % rows).wait_recv()

            def leave(slot):
                for step in range(1, rows):
                    down(slot, (row + step) % rows).start()
                back[slot] = result[slot, rows_of(row)]

            newton(matrix, result, first, count, arrive, leave, gram, poly, temp, later)

    units = [
        (owner, slot)
        for owner in range(2 * OWNER_CHIPS)
        for slot in range(SLOTS)
        if slot_used(owner, slot)
    ]

    def target(owner, slot):
        return ortho_ref.at[slot_block(owner, slot)]

    def out(owner, slot, j):
        return remote(
            back.at[slot],
            target(owner, slot),
            o_send.at[slot, j - 1],
            o_recv.at[owner // 2, slot],
            ((chip + j) % chips * 2 + core, row),
        )

    def across(owner, slot, local):
        return remote(
            back.at[slot] if local else target(owner, slot),
            target(owner, slot),
            p_send.at[owner // 2, slot],
            p_recv.at[owner // 2, slot],
            sibling,
        )

    def keep(owner, slot):
        return pltpu.make_async_copy(back.at[slot], target(owner, slot), keep_sem.at[slot])

    def publish(when):
        for owner, slot in units:
            if late_slot(owner, slot) != (when == 1):
                continue

            @pl.when(band == owner)
            def _():
                @pl.when(row != home(slot))
                def _():
                    down(slot, row).wait_recv()

                for j in range(1, chips):
                    out(owner, slot, j).start()
                across(owner, slot, True).start()
                keep(owner, slot).start()

    def relay(when):
        for owner, slot in units:
            if late_slot(owner, slot) != (when == 1):
                continue

            @pl.when(jnp.logical_and(core == owner % 2, chip != owner // 2))
            def _():
                out(owner, slot, 1).wait_recv()
                across(owner, slot, False).start()

    reducer.start()
    small_pair.start()
    for slot in range(SLOTS):
        @pl.when(jnp.logical_and(owned[slot], jnp.logical_not(last[slot])))
        def _():
            ready = pltpu.make_async_copy(
                total_ref.at[slot_block(band, slot)], back.at[slot], load_sem.at[SLOTS + slot]
            )
            ready.start()
            ready.wait()
            momentum(slot, back[slot])

    reducer.pair()
    small_pair.wait()
    part_small[...] = small_ref[core] + sib_small[...]
    for at in range(OWNER_CHIPS):
        pl.when(chip != at)(small_to(at).start)
    solve(0)

    def take(slot, count, value):
        for n in range(count):
            momentum(slot + n, value[n])

    def load_landed(src, count):
        dst = landed_buf.at[pl.ds(0, count)]
        copy = pltpu.make_async_copy(src, dst, landed_sem)
        copy.start()
        copy.wait()
        return dst[...]

    reducer.reduce(take, load_landed)
    for at in range(OWNER_CHIPS):
        @pl.when(chip == at)
        def _():
            for j in range(1, chips):
                remote(
                    land_small.at[j - 1],
                    land_small.at[j - 1],
                    m_red_send.at[at],
                    m_red_recv.at[j - 1],
                    sibling,
                ).wait_recv()
                part_small[at] += land_small[j - 1]
            for j in range(1, chips):
                small_out(at, j).start()
            small_across(at, core, True).start()
            small_keep(at).start()

    publish(0)
    solve(1)
    reducer.relay()
    for at in range(OWNER_CHIPS):
        @pl.when(chip != at)
        def _():
            small_out(at, 1).wait_recv()
            small_across(at, core, False).start()

    publish(1)
    relay(0)
    relay(1)
    reducer.finish()
    for at in range(OWNER_CHIPS):
        small_across(at, core, False).wait_send()
        small_across(at, 1 - core, False).wait_recv()

        @pl.when(chip != at)
        def _():
            small_to(at).wait_send()

        @pl.when(chip == at)
        def _():
            for j in range(1, chips):
                small_out(at, j).wait_send()
            small_keep(at).wait()

    for owner, slot in units:
        @pl.when(core == owner % 2)
        def _():
            across(owner, slot, False).wait_send()

        @pl.when(core != owner % 2)
        def _():
            across(owner, slot, False).wait_recv()

        @pl.when(band == owner)
        def _():
            for j in range(1, chips):
                out(owner, slot, j).wait_send()
            keep(owner, slot).wait()

            @pl.when(row != home(slot))
            def _():
                up(slot, row).wait_send()

            @pl.when(row == home(slot))
            def _():
                for step in range(1, rows):
                    down(slot, (row + step) % rows).wait_send()


def tail(bands, rows, grads, small, momentum, given):
    blocks, rows_dev, width = momentum.shape
    each = grads.shape[0]
    chips = bands // 2
    chunk = small.shape[2]
    f32 = jnp.float32
    dma = pltpu.SemaphoreType.DMA
    square = pltpu.VMEM((width, width), f32)
    slots = pltpu.VMEM((SLOTS, rows_dev, width), f32)
    return pl.pallas_call(
        functools.partial(tail_kernel, bands, rows),
        out_shape=(
            jax.ShapeDtypeStruct(given.shape, f32),
            jax.ShapeDtypeStruct((blocks, rows_dev, width), f32),
            jax.ShapeDtypeStruct((2 * OWNER_CHIPS, chunk, width), f32),
            jax.ShapeDtypeStruct((1, chips - 1, SLOTS, rows_dev, width), f32),
        ),
        in_specs=[VMEM, VMEM, ANY, ANY],
        out_specs=[ANY, ANY, ANY, ANY],
        input_output_aliases={3: 0},
        scratch_shapes=[
            pltpu.VMEM((each, rows_dev, width), f32),
            pltpu.VMEM((1, each, rows_dev, width), f32),
            slots,
            pltpu.VMEM((OWNER_CHIPS, chunk, width), f32),
            pltpu.VMEM((OWNER_CHIPS, chunk, width), f32),
            pltpu.VMEM((chips - 1, chunk, width), f32),
            slots,
            pltpu.VMEM((SLOTS, width, width), f32),
            pltpu.VMEM((SLOTS, width, width), f32),
            slots,
            square,
            square,
            square,
            square,
            dma((2 * SLOTS,)),
            dma,
            dma((2,)),
            dma((OWNER_CHIPS,)),
            dma((chips - 1,)),
            dma((chips - 1,)),
            dma((OWNER_CHIPS,)),
            dma((2, OWNER_CHIPS)),
            dma,
            dma((SLOTS,)),
            dma((SLOTS, rows)),
            dma((SLOTS, rows)),
            dma((SLOTS,)),
            dma((SLOTS, chips - 1)),
            dma((OWNER_CHIPS, SLOTS)),
            dma((OWNER_CHIPS, SLOTS)),
            dma((OWNER_CHIPS, SLOTS)),
            dma((SLOTS,)),
        ]
        + reducer_sems(1, chips),
        compiler_params=pltpu.CompilerParams(
            collective_id=0, has_side_effects=True, vmem_limit_bytes=VMEM_BYTES
        ),
        name="tail",
    )(grads, small, momentum, given)


def finish_kernel(
    shapes,
    channels,
    edge_channels,
    w_ref,
    average_ref,
    mom_ref,
    total_ref,
    ortho_ref,
    small_ref,
    count_ref,
    enc_ref,
    enc_first_ref,
    enc_second_ref,
    dec_ref,
    dec_first_ref,
    dec_second_ref,
    param_ref,
    param_first_ref,
    param_second_ref,
    loss_ref,
    total_count_ref,
    new_w_ref,
    new_mom_ref,
    new_average_ref,
    enc_outs,
    dec_outs,
    param_outs,
):
    wide, params_at, decoder_at, loss_at = shapes
    step = pl.program_id(0)
    for n in range(w_ref.shape[0]):
        block = lax.rem(step * w_ref.shape[0] + n, len(block_scale))
        scale = jnp.where(block < 3, block_scale[0], jnp.where(block == 4, block_scale[4], 1.0))
        scale = jnp.where(block == 5, block_scale[5], scale)
        fresh = w_ref[n] * (1.0 - muon_rate * weight_decay) - (muon_rate * scale) * ortho_ref[n]
        new_w_ref[n] = fresh
        new_average_ref[n] = average_decay * average_ref[n] + (1.0 - average_decay) * fresh
        new_mom_ref[n] = momentum_decay * mom_ref[n] + total_ref[n]

    def put(outs, at, values):
        for ref, value in zip(outs, values):
            ref[at] = value

    @pl.when(step == 0)
    def _():
        for at, grad in (
            (pl.ds(0, channels), small_ref[pl.ds(0, channels)]),
            (pl.ds(channels, edge_channels), small_ref[pl.ds(wide, edge_channels)]),
        ):
            put(enc_outs, at, adam_update(enc_ref[at], enc_first_ref[at], enc_second_ref[at], grad, adam_rate))
        grad = small_ref[pl.ds(decoder_at, channels)]
        put(dec_outs, ..., adam_update(dec_ref[...], dec_first_ref[...], dec_second_ref[...], grad, adam_rate))
        for layer in range(param_ref.shape[0]):
            grad = small_ref[pl.ds(params_at + layer * 8, 8)]
            put(
                param_outs,
                layer,
                adam_update(param_ref[layer], param_first_ref[layer], param_second_ref[layer], grad, param_rate),
            )
        loss_ref[...] = small_ref[pl.ds(loss_at, 1), 0:1]
        total_count_ref[...] = jnp.sum(jnp.sum(count_ref[:, :, 0:1, 0:1], axis=0), axis=0)


def finish(shapes, edge_channels, blocks, small, counts, encoder, decoder, params):
    f32 = jnp.float32
    channels = decoder[0].shape[0]
    big = blocks[0]
    tiled = pl.BlockSpec((len(block_scale),) + big.shape[1:], lambda i: (i, 0, 0))

    def whole(value):
        return pl.BlockSpec(value.shape, lambda i: (0,) * value.ndim)

    def like(value):
        return jax.ShapeDtypeStruct(value.shape, f32)

    scalar = jax.ShapeDtypeStruct((1, 1), f32)
    return pl.pallas_call(
        functools.partial(finish_kernel, shapes, channels, edge_channels),
        grid=(big.shape[0] // len(block_scale),),
        out_shape=(
            scalar,
            scalar,
            like(big),
            like(big),
            like(big),
            (like(encoder[0]),) * 3,
            (like(decoder[0]),) * 3,
            (like(params[0]),) * 3,
        ),
        in_specs=[tiled] * 5 + [whole(value) for value in (small, counts, *encoder, *decoder, *params)],
        out_specs=(
            whole(scalar),
            whole(scalar),
            tiled,
            tiled,
            tiled,
            (whole(encoder[0]),) * 3,
            (whole(decoder[0]),) * 3,
            (whole(params[0]),) * 3,
        ),
        compiler_params=pltpu.CompilerParams(vmem_limit_bytes=VMEM_BYTES),
        name="finish",
    )(*blocks, small, counts, *encoder, *decoder, *params)


def adam_update(values, first, second, gradient, rate):
    first = beta_one * first + (1.0 - beta_one) * gradient
    second = beta_two * second + (1.0 - beta_two) * gradient * gradient
    corrected = (
        first / (1.0 - beta_one**STEP) / (jnp.sqrt(second / (1.0 - beta_two**STEP)) + adam_eps)
    )
    return (first, second, values * (1.0 - rate * weight_decay) - rate * corrected)


def body(
    grid_input,
    grid_target,
    edge_input,
    senders,
    receivers,
    border_nodes,
    grid_to_mesh,
    mesh_to_grid,
    loss_mask,
    encoder_weights,
    encoder_first,
    encoder_second,
    processor_weights,
    processor_momentum,
    processor_average,
    norm_params,
    norm_first,
    norm_second,
    decoder_weights,
    decoder_first,
    decoder_second,
):
    bands, rows = lax.axis_size("band"), lax.axis_size("row")
    layers, blocks, rows_dev, width = processor_weights.shape
    channels = grid_input.shape[1]
    edge_channels = edge_input.shape[1]
    wide = -(-channels // 8) * 8
    grids, rim = grid_input.shape[0], border_nodes.shape[0]
    reads = mesh_to_grid.reshape(grids, -1).T
    indices = (jnp.stack([senders, receivers]),) + tuple(
        value[None, :] for value in (border_nodes, grid_to_mesh, loss_mask)
    ) + (reads,)
    flat_weights = processor_weights.reshape(layers * blocks, rows_dev, width)
    *saved, index = forward(
        bands,
        rows,
        grid_input.T,
        edge_input.T,
        indices,
        flat_weights,
        encoder_weights,
        norm_params,
    )
    inputs = (
        grid_input.T,
        grid_target.T,
        edge_input.T,
        index,
        encoder_weights,
        decoder_weights.T,
        norm_params,
    )
    grads, small, total, _ = backward(bands, rows, rim, rows_dev, inputs, saved)
    flat_momentum = processor_momentum.reshape(layers * blocks, rows_dev, width)
    total, ortho, small, _ = tail(
        bands,
        rows,
        grads,
        small.reshape(2, OWNER_CHIPS, -1, width),
        flat_momentum,
        total,
    )
    params_at = wide + 8
    decoder_at = params_at + layers * 8
    loss_total, mask_count, next_weights, next_momentum, next_average, encoder, decoder, params = finish(
        (wide, params_at, decoder_at, decoder_at + wide),
        edge_channels,
        (flat_weights, processor_average.reshape(flat_momentum.shape), flat_momentum, total, ortho),
        small.reshape(-1, width),
        saved[-1],
        (encoder_weights, encoder_first, encoder_second),
        (decoder_weights.T, decoder_first.T, decoder_second.T),
        (norm_params, norm_first, norm_second),
    )
    encoder_moment, encoder_square, encoder_values = encoder
    decoder_moment, decoder_square, decoder_values = (value.T for value in decoder)
    param_moment, param_square, param_values = params
    loss_total, mask_count = loss_total[0, 0], mask_count[0, 0]
    next_weights, next_momentum, next_average = (
        value.reshape(processor_weights.shape) for value in (next_weights, next_momentum, next_average)
    )
    return (
        loss_total,
        mask_count,
        next_weights,
        next_momentum,
        next_average,
        param_moment,
        param_square,
        param_values,
        encoder_moment,
        encoder_square,
        encoder_values,
        decoder_moment,
        decoder_square,
        decoder_values,
    )


def solution(mesh):
    return jax.shard_map(
        body,
        mesh=mesh,
        in_specs=(
            P("band", None),
            P("band", None),
            P("band", None),
            P("band"),
            P("band"),
            P("band"),
            P("band"),
            P("band"),
            P("band"),
            P(),
            P(),
            P(),
            P(None, None, "row", None),
            P(None, None, "row", None),
            P(None, None, "row", None),
            P(),
            P(),
            P(),
            P(),
            P(),
            P(),
        ),
        out_specs=(
            P(),
            P(),
            P(None, None, "row", None),
            P(None, None, "row", None),
            P(None, None, "row", None),
            P(),
            P(),
            P(),
            P(),
            P(),
            P(),
            P(),
            P(),
            P(),
        ),
        check_vma=False,
    )
```

```python
import functools

import jax
import jax.numpy as jnp
from jax import lax
from jax.experimental import pallas as pl
from jax.experimental.pallas import tpu as pltpu
from jax.sharding import PartitionSpec as P

STEP = 10
NODE_DEV = 320


coef_a = 3.4445
coef_b = -4.775
coef_c = 2.0315
momentum_decay = 0.95
muon_rate = 0.3
adam_rate = 0.02
param_rate = 0.1
beta_one = 0.9
beta_two = 0.95
adam_eps = 1e-08
weight_decay = 0.01
average_decay = 0.9
block_scale = (3.0**0.5, 3.0**0.5, 3.0**0.5, 1.0, 2.0**0.5, 2.0**0.5, 1.0)


MESH = pl.DeviceIdType.MESH
NN = (((1,), (0,)), ((), ()))
NT = (((1,), (1,)), ((), ()))
TN = (((0,), (0,)), ((), ()))
OWNER_CHIPS = 4
SLOTS = 3
VMEM_BYTES = 62 * 2**20
ANY = pl.BlockSpec(memory_space=pl.ANY)
VMEM = pl.BlockSpec(memory_space=pltpu.VMEM)


def pieces(value):
    high = value.astype(jnp.bfloat16)
    return high, (value - high.astype(jnp.float32)).astype(jnp.bfloat16)


def dot(left, right, dims=NN):
    return lax.dot_general(left, right, dims, preferred_element_type=jnp.float32)


def product(left, right, dims=NN):
    left_high, left_low = pieces(left)
    right_high, right_low = pieces(right)
    return (
        dot(left_high, right_high, dims)
        + dot(left_low, right_high, dims)
        + dot(left_high, right_low, dims)
    )


def slot_block(owner, slot):
    third = owner // 3
    last = third // 2
    return (1 - last) * (7 * (owner % 3) + 4 * third + slot) + last * (
        3 + 14 * (owner - 6) + 7 * slot
    )


def slot_used(owner, slot):
    return owner < (8, 7, 6)[slot]


def remote(src, dst, send_sem, recv_sem, device):
    return pltpu.make_async_remote_copy(
        src_ref=src,
        dst_ref=dst,
        send_sem=send_sem,
        recv_sem=recv_sem,
        device_id=device,
        device_id_type=MESH,
    )


def silu(value):
    return value / (1.0 + jnp.exp(-value))


def silu_back(value):
    gate = 1.0 / (1.0 + jnp.exp(-value))
    return gate * (1.0 + value * (1.0 - gate))


def normed(value):
    centered = value - jnp.mean(value, axis=-1, keepdims=True)
    scale = lax.rsqrt(jnp.mean(centered * centered, axis=-1, keepdims=True) + 1e-05)
    return centered * scale, scale


def normed_back(grad, norm, scale):
    inner = jnp.mean(grad * norm, axis=-1, keepdims=True)
    return (grad - jnp.mean(grad, axis=-1, keepdims=True) - norm * inner) * scale


def column(value):
    return jnp.sum(value, axis=0, keepdims=True)


def hot(mask):
    return jnp.where(mask, 1.0, 0.0).astype(jnp.bfloat16)


def chosen(choice, high, low, dims=NN):
    return dot(choice, high, dims) + dot(choice, low, dims)


def picked(choice, value):
    high, low = pieces(value)
    return chosen(choice, high, low)


def fill_rows(out_ref, make, tile=128):
    def step(t, carry):
        at = pl.multiple_of(t * tile, tile)
        out_ref[pl.ds(at, tile)] = make(at, tile)
        return carry

    lax.fori_loop(0, out_ref.shape[0] // tile, step, 0)


def iota(shape, axis):
    return lax.broadcasted_iota(jnp.int32, shape, axis)


SEND_ROW, RECV_ROW, BORDER_ROW, FEED_ROW, MASK_ROW, READ_ROW = range(6)


def edge_rows(edge_ref, size):
    empty = jnp.zeros((size - edge_ref.shape[0], edge_ref.shape[1]), jnp.float32)
    return jnp.concatenate([edge_ref[...], empty], axis=0)


def embedded_edges(edge_t, enc_ref, first, count, at, size):
    total = edge_t[pl.ds(at, size), 0:1] * enc_ref[pl.ds(first, 1)]
    for n in range(1, count):
        total = total + edge_t[pl.ds(at, size), n : n + 1] * enc_ref[pl.ds(first + n, 1)]
    return total


class Weights:
    def __init__(self, full_ref, stage, high, low, sem):
        self.full, self.stage, self.high, self.low, self.sem = full_ref, stage, high, low, sem

    def copy(self, block, slot):
        return pltpu.make_async_copy(self.full.at[block], self.stage.at[slot], self.sem.at[slot])

    def load(self, first, blocks):
        for n, block in enumerate(blocks[:2]):
            self.copy(first + block, n % 2).start()
        for n, block in enumerate(blocks):
            self.copy(first + block, n % 2).wait()
            high, low = pieces(self.stage[n % 2])
            self.high[block] = high
            self.low[block] = low
            if n + 2 < len(blocks):
                self.copy(first + blocks[n + 2], n % 2).start()

    def times(self, high, low, block, dims=NN):
        weight = self.high[block]
        return dot(high, weight, dims) + dot(low, weight, dims) + dot(high, self.low[block], dims)

    def apply(self, value, block, dims=NN):
        high, low = pieces(value)
        return self.times(high, low, block, dims)


def place(bands, rows):
    band = lax.axis_index("band")
    row = lax.axis_index("row")
    return band, row, band // 2, band % 2


def meet(partners):
    barrier = pltpu.get_barrier_semaphore()
    for partner in partners:
        pl.semaphore_signal(barrier, inc=1, device_id=partner, device_id_type=MESH)
    pl.semaphore_wait(barrier, len(partners))


def forward_kernel(
    bands,
    rows,
    chunks,
    tile,
    grid_ref,
    edge_ref,
    ends_ref,
    border_ref,
    feed_ref,
    mask_ref,
    read_ref,
    w_ref,
    enc_ref,
    param_ref,
    full_ref,
    before_ref,
    message_ref,
    edges_ref,
    embed_ref,
    nodes_ref,
    fed_ref,
    agg_ref,
    inner_ref,
    update_ref,
    table_ref,
    count_ref,
    index_ref,
    edge_buf,
    before_buf,
    message_buf,
    index_t,
    edge_t,
    pick,
    gather_t,
    src_high,
    src_low,
    high,
    low,
    stage,
    table,
    border_buf,
    count_buf,
    stage_sem,
    save_sem,
    own_sem,
    z_send,
    z_recv,
    a_send,
    a_recv,
    b_send,
    b_recv,
    s_send,
    s_recv,
    x_send,
    x_recv,
    p_send,
    p_recv,
):
    band, row, chip, core = place(bands, rows)
    chips = bands // 2
    layers, blocks = agg_ref.shape[0], w_ref.shape[0] // agg_ref.shape[0]
    rows_dev = w_ref.shape[1]
    nodes, width = fed_ref.shape
    edges = edge_buf.shape[1]
    border = border_buf.shape[1]
    grids = grid_ref.shape[1]
    weights = Weights(full_ref, stage, high, low, stage_sem)
    quad, pos = chip // 4, chip % 4
    pos_x, pos_y = pos + 1 - 2 * (pos % 2), pos + 2 - 4 * (pos // 2)
    sibling = (chip * 2 + 1 - core, row)
    near = (((quad * 4 + pos_x) * 2 + core, row), ((quad * 4 + pos_y) * 2 + core, row))
    near_pos = (pos_x, pos_y)
    partners = [((chip + j) % chips * 2 + core, row) for j in range(1, chips)] + [sibling]
    partners += [(band, (row + j) % rows) for j in range(1, rows)]
    meet(partners)

    piece = rows_dev // 8

    def part(g, from_row, of_core, of_pos, first=0, size=None):
        start, count = chunks[g]
        size = piece if size is None else size
        at = from_row * rows_dev + (of_core * 4 + of_pos) * piece + first
        return full_ref.at[pl.ds(start, count), pl.ds(pl.multiple_of(at, 8), size)]

    def z_copy(g, j, from_row):
        start, count = chunks[g]
        at = pl.multiple_of((core * 4 + pos) * piece, 8)
        return remote(
            w_ref.at[pl.ds(start, count), pl.ds(at, piece)],
            part(g, from_row, core, pos),
            z_send.at[g, j - 1],
            z_recv.at[g, j - 1],
            (band, (from_row + j) % rows),
        )

    def a_copy(g, side, j, of_pos):
        region = part(g, (row - j + rows) % rows, core, of_pos)
        return remote(region, region, a_send.at[g, side, j - 1], a_recv.at[g, side, j - 1], near[side])

    def b_copy(g, side, j, of_pos):
        half = piece // 2
        region = part(g, (row - j + rows) % rows, core, of_pos, side * half, half)
        return remote(region, region, b_send.at[g, side, j - 1], b_recv.at[g, side, j - 1], near[side])

    def s_copy(g, j, of_core):
        region = part(g, (row - j + rows) % rows, of_core, 0, 0, 4 * piece)
        return remote(region, region, s_send.at[g, j - 1], s_recv.at[g, j - 1], sibling)

    others = range(1, rows)
    far = 3 - pos

    def start_z(g):
        for j in others:
            z_copy(g, j, row).start()

    def start_a(g):
        for j in others:
            z_copy(g, j, (row - j + rows) % rows).wait_recv()
            for side in range(2):
                a_copy(g, side, j, pos).start()

    def start_b(g):
        for j in others:
            for side in range(2):
                a_copy(g, side, j, near_pos[side]).wait_recv()
                b_copy(g, 1 - side, j, near_pos[side]).start()

    def start_s(g):
        for j in others:
            for side in range(2):
                b_copy(g, side, j, far).wait_recv()
            s_copy(g, j, core).start()

    def ready(g):
        for j in others:
            s_copy(g, j, 1 - core).wait_recv()

    def tick(t):
        for g, stage_of in ((t - 5, ready), (t - 4, start_s), (t - 3, start_b), (t - 1, start_a), (t + 1, start_z)):
            if 0 <= g < len(chunks):
                stage_of(g)

    own = pltpu.make_async_copy(
        w_ref,
        full_ref.at[:, pl.ds(pl.multiple_of(row * rows_dev, rows_dev), rows_dev)],
        own_sem,
    )
    start_z(0)
    start_z(1)
    own.start()

    def table_of(e):
        return table_ref if (layers - e) % 2 == 0 else table

    def items(e):
        par = e % 2
        found = [(0, border_buf.at[par], lambda k, c: table_of(e).at[k, c])]
        if e == 0:
            found.append((1, count_buf, lambda k, c: count_ref.at[k, c]))
        return found

    def out(e, item, src, dst, j):
        return remote(
            src,
            dst(core, chip),
            x_send.at[e + item * 4, j - 1],
            x_recv.at[e + item * 4, j - 1],
            ((chip + j) % chips * 2 + core, row),
        )

    def across(e, item, src, dst, j, of_core):
        origin = (chip - j + chips) % chips
        return remote(
            src if j == 0 else dst(of_core, origin),
            dst(of_core, origin),
            p_send.at[e + item * 4, j],
            p_recv.at[e + item * 4, j],
            sibling,
        )

    def share(e, value):
        par = e % 2
        choice = hot(iota((border, nodes), 1) == index_t[pl.ds(0, border), BORDER_ROW : BORDER_ROW + 1])
        rows_out = picked(choice, value)
        border_buf[par] = rows_out
        table_of(e)[core, chip] = rows_out
        for item, src, dst in items(e):
            for j in range(1, chips):
                out(e, item, src, dst, j).start()
            across(e, item, src, dst, 0, core).start()

    def relay(e):
        for item, src, dst in items(e):
            for j in range(1, chips):
                out(e, item, src, dst, j).wait_recv()
                across(e, item, src, dst, j, core).start()

    def gathered(e):
        for item, src, dst in items(e):
            for j in range(chips):
                across(e, item, src, dst, j, 1 - core).wait_recv()
            for j in range(chips):
                across(e, item, src, dst, j, core).wait_send()
            for j in range(1, chips):
                out(e, item, src, dst, j).wait_send()

    def put_src(at, value):
        value_high, value_low = pieces(value)
        size = value.shape[0]
        src_high[pl.ds(at, size)] = value_high
        src_low[pl.ds(at, size)] = value_low

    def save(kind, layer, src):
        dst = (before_ref, message_ref, edges_ref, embed_ref)[kind]
        return pltpu.make_async_copy(src, dst if layer is None else dst.at[layer], save_sem.at[kind])

    def table_place(index):
        far = (index - nodes).astype(jnp.float32)
        owner = jnp.floor((far + 0.5) * (1.0 / border))
        at_chip = jnp.floor(owner * 0.5)
        moved = ((owner - 2.0 * at_chip) * chips + at_chip) * border + far - owner * border
        return jnp.where(index < nodes, index, moved.astype(jnp.int32) + nodes)

    index_ref[...] = jnp.zeros_like(index_ref)
    index_ref[SEND_ROW : SEND_ROW + 1] = table_place(ends_ref[0:1])
    index_ref[RECV_ROW : RECV_ROW + 1] = ends_ref[1:2]
    index_ref[BORDER_ROW : BORDER_ROW + 1, pl.ds(0, border)] = border_ref[...]
    index_ref[FEED_ROW : FEED_ROW + 1, pl.ds(0, grids)] = feed_ref[...]
    index_ref[MASK_ROW : MASK_ROW + 1, pl.ds(0, grids)] = mask_ref[...]
    index_ref[READ_ROW:, pl.ds(0, grids)] = table_place(read_ref[...])
    index_t[...] = index_ref[...].T
    embed_buf = before_buf.at[pl.ds(0, grids)]
    channels = grid_ref.shape[0]
    embed_buf[...] = product(grid_ref[...], enc_ref[pl.ds(0, channels)], TN)
    save(3, None, embed_buf).start()
    tick(1)
    feed = hot(iota((nodes, grids), 0) == index_ref[FEED_ROW : FEED_ROW + 1, pl.ds(0, grids)])
    fed = picked(feed, silu(embed_buf[...]))
    fed_ref[...] = fed
    nodes_ref[0] = normed(fed)[0]
    mask = index_ref[MASK_ROW : MASK_ROW + 1, pl.ds(0, grids)].astype(jnp.float32)
    counts = jnp.broadcast_to(jnp.sum(mask, axis=1, keepdims=True), count_buf.shape)
    count_buf[...] = counts
    count_ref[core, chip] = counts
    tick(2)
    edge_t[...] = edge_rows(edge_ref, edge_t.shape[1]).T

    def embed_edges(at, size):
        return silu(embedded_edges(edge_t, enc_ref, channels, edge_ref.shape[0], at, size))

    fill_rows(edge_buf.at[0], embed_edges)
    inputs = src_high.shape[0]
    near_inputs = 2 * nodes

    def choose(at, size):
        columns = iota((size, inputs), 1)
        sent = index_t[pl.ds(at, size), SEND_ROW : SEND_ROW + 1]
        received = index_t[pl.ds(at, size), RECV_ROW : RECV_ROW + 1] + nodes
        sent = jnp.where(sent < nodes, sent, sent + nodes)
        return hot(jnp.logical_or(columns == sent, columns == received))

    fill_rows(pick, choose)
    tick(3)

    def choose_receiver(at, size):
        return hot(iota((size, edges), 0) + at == index_ref[RECV_ROW : RECV_ROW + 1])

    fill_rows(gather_t, choose_receiver, 64)
    own.wait()
    tick(4)
    tick(5)
    for layer in range(layers):
        first = layer * blocks
        now, later = layer % 2, (layer + 1) % 2
        weights.load(first, (1, 2))
        node = nodes_ref[layer]
        node_high, node_low = pieces(node)
        sender = weights.times(node_high, node_low, 1)
        share(layer, sender)
        put_src(0, sender)
        put_src(nodes, weights.times(node_high, node_low, 2))
        if layer > 0:
            save(0, layer - 1, before_buf).wait()
            save(1, layer - 1, message_buf).wait()
            save(2, layer - 1, edge_buf.at[later]).wait()
        else:
            save(3, None, embed_buf).wait()
        save(2, layer, edge_buf.at[now]).start()
        tick(6 + 4 * layer)
        weights.load(first, (0,))

        def near_part(t):
            at = pl.ds(t * tile, tile)
            before_buf[at] = (
                weights.apply(edge_buf[now, at], 0)
                + chosen(
                    pick[at, pl.ds(0, near_inputs)],
                    src_high[pl.ds(0, near_inputs)],
                    src_low[pl.ds(0, near_inputs)],
                )
                + param_ref[layer, pl.ds(0, 1)]
            )

        near_part(0)
        tick(7 + 4 * layer)
        relay(layer)
        near_part(1)
        weights.load(first, (3, 4))
        inner = weights.times(node_high, node_low, 4) + param_ref[layer, pl.ds(4, 1)]
        gathered(layer)
        table_now = table_of(layer)
        for side in range(2):
            put_src(
                near_inputs + side * chips * border,
                table_now[side].reshape(chips * border, width),
            )
        agg_ref[layer] = jnp.zeros((nodes, width), jnp.float32)

        def edge_tile(t):
            at = pl.ds(t * tile, tile)
            far_inputs = pl.ds(near_inputs, inputs - near_inputs)
            before = before_buf[at] + chosen(
                pick[at, far_inputs], src_high[far_inputs], src_low[far_inputs]
            )
            before_buf[at] = before
            message = weights.apply(silu(before), 3) + param_ref[layer, pl.ds(1, 1)]
            message_buf[at] = message
            edge = (
                edge_buf[now, at]
                + normed(message)[0] * (1.0 + param_ref[layer, pl.ds(2, 1)])
                + param_ref[layer, pl.ds(3, 1)]
            )
            if layer < layers - 1:
                edge_buf[later, at] = edge
            agg_ref[layer] += picked(gather_t[:, at], edge)

        edge_tile(0)
        tick(8 + 4 * layer)
        edge_tile(1)
        save(0, layer, before_buf).start()
        save(1, layer, message_buf).start()
        weights.load(first, (5, 6))
        inner = inner + weights.apply(agg_ref[layer], 5)
        inner_ref[layer] = inner
        update = weights.apply(silu(inner), 6) + param_ref[layer, pl.ds(5, 1)]
        update_ref[layer] = update
        nodes_ref[layer + 1] = (
            node
            + normed(update)[0] * (1.0 + param_ref[layer, pl.ds(6, 1)])
            + param_ref[layer, pl.ds(7, 1)]
        )
        tick(9 + 4 * layer)
    share(layers, nodes_ref[layers])
    relay(layers)
    gathered(layers)
    save(0, layers - 1, before_buf).wait()
    save(1, layers - 1, message_buf).wait()
    save(2, layers - 1, edge_buf.at[(layers - 1) % 2]).wait()
    for g in range(len(chunks)):
        for j in others:
            z_copy(g, j, row).wait_send()
            for side in range(2):
                a_copy(g, side, j, pos).wait_send()
                b_copy(g, 1 - side, j, near_pos[side]).wait_send()
            s_copy(g, j, core).wait_send()


def forward(bands, rows, grid, edge, indices, blocks, enc, params):
    f32, bf16 = jnp.float32, jnp.bfloat16
    dma = pltpu.SemaphoreType.DMA
    width = blocks.shape[2]
    edges, grids = edge.shape[1], grid.shape[1]
    layers = params.shape[0]
    rim = indices[1].shape[1]
    index_rows = READ_ROW + indices[4].shape[0]
    nodes = NODE_DEV
    chips = bands // 2
    inputs = 2 * nodes + bands * rim
    each = blocks.shape[0] // layers
    chunks = []
    for layer in range(layers):
        chunks += [(layer * each + first, size) for first, size in ((1, 2), (0, 1), (3, 2), (5, 2))]
    groups = len(chunks)
    tile = edges // 2

    def array(*shape):
        return jax.ShapeDtypeStruct(shape, f32)

    return pl.pallas_call(
        functools.partial(forward_kernel, bands, rows, tuple(chunks), tile),
        out_shape=(
            array(blocks.shape[0], width, width),
            array(layers, edges, width),
            array(layers, edges, width),
            array(layers, edges, width),
            array(grids, width),
            array(layers + 1, nodes, width),
            array(nodes, width),
            array(layers, nodes, width),
            array(layers, nodes, width),
            array(layers, nodes, width),
            array(2, chips, rim, width),
            array(2, chips, 8, 128),
            jax.ShapeDtypeStruct((index_rows, edges), jnp.int32),
        ),
        in_specs=[VMEM] * 10,
        out_specs=[ANY] * 5 + [VMEM] * 8,
        scratch_shapes=[
            pltpu.VMEM((2, edges, width), f32),
            pltpu.VMEM((edges, width), f32),
            pltpu.VMEM((edges, width), f32),
            pltpu.VMEM((edges, index_rows), jnp.int32),
            pltpu.VMEM((edges, 8), f32),
            pltpu.VMEM((edges, inputs), bf16),
            pltpu.VMEM((nodes, edges), bf16),
            pltpu.VMEM((inputs, width), bf16),
            pltpu.VMEM((inputs, width), bf16),
            pltpu.VMEM((each, width, width), bf16),
            pltpu.VMEM((each, width, width), bf16),
            pltpu.VMEM((2, width, width), f32),
            pltpu.VMEM((2, chips, rim, width), f32),
            pltpu.VMEM((2, rim, width), f32),
            pltpu.VMEM((8, 128), f32),
            dma((2,)),
            dma((4,)),
            dma,
            dma((groups, rows - 1)),
            dma((groups, rows - 1)),
            dma((groups, 2, rows - 1)),
            dma((groups, 2, rows - 1)),
            dma((groups, 2, rows - 1)),
            dma((groups, 2, rows - 1)),
            dma((groups, rows - 1)),
            dma((groups, rows - 1)),
            dma((5, chips - 1)),
            dma((5, chips - 1)),
            dma((5, chips)),
            dma((5, chips)),
        ],
        compiler_params=pltpu.CompilerParams(
            collective_id=1, has_side_effects=True, vmem_limit_bytes=VMEM_BYTES
        ),
        name="forward",
    )(
        grid,
        edge,
        *indices,
        blocks,
        enc,
        params,
    )


def groups(layer):
    return (
        (layer, 0, 0, 3),
        (3 + layer, 0, 4, 3),
        (6 + layer // 2, layer % 2, 3, 1),
    )


class Reducer:
    def __init__(self, bands, layer, at, grads, sib, land, total, sems):
        band, row, self.chip, self.core = place(bands, 1)
        self.row = row
        self.chips = bands // 2
        self.sibling = (self.chip * 2 + 1 - self.core, row)
        self.layer, self.at = layer, at
        self.grads, self.sib, self.land, self.total = grads, sib, land, total
        (self.c_send, self.c_recv, self.r_send, self.r_recv) = sems[:4]
        (self.o_send, self.o_recv, self.p_send, self.p_recv, self.k_sem) = sems[4:]

    def each(self):
        for q, (owner, slot, block, count) in enumerate(groups(self.layer)):
            yield q, owner // 2, owner % 2, slot, pl.ds(block, count), count

    def to_sibling(self, q, rows):
        return remote(
            self.grads.at[rows],
            self.sib.at[rows],
            self.c_send.at[self.at, q],
            self.c_recv.at[self.at, q],
            self.sibling,
        )

    def to_owner(self, q, at_chip, at_core, rows, count):
        step = (at_chip - self.chip + self.chips) % self.chips
        return remote(
            self.grads.at[rows],
            self.land.at[self.at, step - 1, pl.ds(0, count)],
            self.r_send.at[self.at, q],
            self.r_recv.at[self.at, step - 1],
            (at_chip * 2 + at_core, self.row),
        )

    def to_chip(self, q, rows, j):
        return remote(
            self.grads.at[rows],
            self.total.at[rows],
            self.o_send.at[self.at, j - 1],
            self.o_recv.at[self.at, q],
            ((self.chip + j) % self.chips * 2 + self.core, self.row),
        )

    def across(self, q, rows, src):
        return remote(
            src.at[rows],
            self.total.at[rows],
            self.p_send.at[self.at, q],
            self.p_recv.at[self.at, q],
            self.sibling,
        )

    def keep(self, rows):
        return pltpu.make_async_copy(self.grads.at[rows], self.total.at[rows], self.k_sem.at[self.at])

    def start(self):
        for q, at_chip, at_core, slot, rows, count in self.each():
            @pl.when(self.core != at_core)
            def _():
                self.to_sibling(q, rows).start()

    def pair(self):
        for q, at_chip, at_core, slot, rows, count in self.each():
            @pl.when(self.core == at_core)
            def _():
                self.to_sibling(q, rows).wait_recv()
                self.grads[rows] += self.sib[rows]

                @pl.when(self.chip != at_chip)
                def _():
                    self.to_owner(q, at_chip, at_core, rows, count).start()

    def reduce(self, take, load):
        for q, at_chip, at_core, slot, rows, count in self.each():
            @pl.when(jnp.logical_and(self.core == at_core, self.chip == at_chip))
            def _():
                value = self.grads[rows]
                for j in range(1, self.chips):
                    landed = self.land.at[self.at, j - 1, pl.ds(0, count)]
                    remote(
                        landed,
                        landed,
                        self.r_send.at[self.at, q],
                        self.r_recv.at[self.at, j - 1],
                        self.sibling,
                    ).wait_recv()
                    value = value + load(landed, count)
                self.grads[rows] = value
                take(slot, count, value)
                for j in range(1, self.chips):
                    self.to_chip(q, rows, j).start()
                self.across(q, rows, self.grads).start()
                self.keep(rows).start()

    def relay(self):
        for q, at_chip, at_core, slot, rows, count in self.each():
            @pl.when(jnp.logical_and(self.core == at_core, self.chip != at_chip))
            def _():
                self.to_chip(q, rows, 1).wait_recv()
                self.across(q, rows, self.total).start()

    def finish(self):
        for q, at_chip, at_core, slot, rows, count in self.each():
            @pl.when(self.core != at_core)
            def _():
                self.to_sibling(q, rows).wait_send()
                self.across(q, rows, self.total).wait_recv()

            @pl.when(self.core == at_core)
            def _():
                self.across(q, rows, self.total).wait_send()

                @pl.when(self.chip != at_chip)
                def _():
                    self.to_owner(q, at_chip, at_core, rows, count).wait_send()

                @pl.when(self.chip == at_chip)
                def _():
                    for j in range(1, self.chips):
                        self.to_chip(q, rows, j).wait_send()
                    self.keep(rows).wait()


def reducer_sems(count, chips):
    dma = pltpu.SemaphoreType.DMA
    return [
        dma((count, 3)),
        dma((count, 3)),
        dma((count, 3)),
        dma((count, chips - 1)),
        dma((count, chips - 1)),
        dma((count, 3)),
        dma((count, 3)),
        dma((count, 3)),
        dma((count,)),
    ]


class Spreader:
    def __init__(self, bands, at, grads, sib, land, landed, total, sems):
        band, self.row, self.chip, self.core = place(bands, 1)
        self.chips = bands // 2
        self.sibling = (self.chip * 2 + 1 - self.core, self.row)
        self.at = at
        self.grads, self.sib, self.land, self.landed, self.total = grads, sib, land, landed, total
        self.half = grads.shape[1] // 2
        self.piece = self.half // OWNER_CHIPS
        (self.c_sem, self.r_send, self.r_recv, self.o_send, self.o_recv, self.p_sem, self.k_sem) = sems

    def rows(self, core):
        return pl.ds(pl.multiple_of(core * self.half, 8), self.half)

    def part(self, core, chip):
        return pl.ds(pl.multiple_of(core * self.half + chip * self.piece, 8), self.piece)

    def to_sibling(self):
        return remote(
            self.grads.at[:, self.rows(1 - self.core)],
            self.sib,
            self.c_sem.at[self.at, 0],
            self.c_sem.at[self.at, 1],
            self.sibling,
        )

    def to_owner(self, chip):
        step = (chip - self.chip + self.chips) % self.chips
        return remote(
            self.grads.at[:, self.part(self.core, chip)],
            self.land.at[step - 1],
            self.r_send.at[self.at, chip],
            self.r_recv.at[self.at, step - 1],
            (chip * 2 + self.core, self.row),
        )

    def to_chip(self, j, chip):
        part = self.part(self.core, chip)
        return remote(
            self.grads.at[:, part],
            self.total.at[:, part],
            self.o_send.at[self.at, j - 1],
            self.o_recv.at[self.at, chip],
            ((self.chip + j) % self.chips * 2 + self.core, self.row),
        )

    def keep(self):
        part = self.part(self.core, self.chip)
        return pltpu.make_async_copy(
            self.grads.at[:, part], self.total.at[:, part], self.k_sem.at[self.at, 0]
        )

    def across(self, core):
        region = self.total.at[:, self.rows(core)]
        return remote(region, region, self.p_sem.at[self.at, 0], self.p_sem.at[self.at, 1], self.sibling)

    def owned(self, body):
        if self.chips == OWNER_CHIPS:
            body()
        else:
            pl.when(self.chip < OWNER_CHIPS)(body)

    def start(self):
        self.to_sibling().start()

    def pair(self):
        self.to_sibling().wait()
        self.grads[:, self.rows(self.core)] += self.sib[...]
        for chip in range(OWNER_CHIPS):
            pl.when(self.chip != chip)(self.to_owner(chip).start)

    def reduce(self):
        def body():
            part = self.part(self.core, self.chip)
            for j in range(1, self.chips):
                remote(
                    self.landed,
                    self.land.at[j - 1],
                    self.r_send.at[self.at, 0],
                    self.r_recv.at[self.at, j - 1],
                    self.sibling,
                ).wait_recv()
                copy = pltpu.make_async_copy(self.land.at[j - 1], self.landed, self.k_sem.at[self.at, 1])
                copy.start()
                copy.wait()
                self.grads[:, part] += self.landed[...]
            for j in range(1, self.chips):
                self.to_chip(j, self.chip).start()
            self.keep().start()

        self.owned(body)

    def relay(self):
        for chip in range(OWNER_CHIPS):
            pl.when(self.chip != chip)(self.to_chip(1, chip).wait_recv)
        self.owned(lambda: self.keep().wait())
        self.across(self.core).start()

    def finish(self):
        self.across(self.core).wait_send()
        self.across(1 - self.core).wait_recv()
        for chip in range(OWNER_CHIPS):
            pl.when(self.chip != chip)(self.to_owner(chip).wait_send)

        def body():
            for j in range(1, self.chips):
                self.to_chip(j, self.chip).wait_send()

        self.owned(body)


def spreader_sems(count, chips):
    dma = pltpu.SemaphoreType.DMA
    return [
        dma((count, 2)),
        dma((count, OWNER_CHIPS)),
        dma((count, chips - 1)),
        dma((count, chips - 1)),
        dma((count, OWNER_CHIPS)),
        dma((count, 2)),
        dma((count, 2)),
    ]


def backward_kernel(
    bands,
    rows,
    each,
    tile,
    grid_ref,
    target_ref,
    edge_ref,
    index_ref,
    enc_ref,
    dec_ref,
    param_ref,
    full_ref,
    before_ref,
    message_ref,
    edges_ref,
    embed_ref,
    nodes_ref,
    fed_ref,
    agg_ref,
    inner_ref,
    update_ref,
    table_ref,
    count_ref,
    grads_ref,
    small_ref,
    total_ref,
    land_grads,
    edge_buf,
    before_buf,
    message_buf,
    node_buf,
    agg_buf,
    inner_buf,
    update_buf,
    index_t,
    edge_t,
    features,
    edge_grad,
    node_grad,
    part_high,
    part_low,
    pick_t,
    gather,
    high,
    low,
    stage,
    table,
    sib,
    land,
    grads_buf,
    sib_grads,
    landed_buf,
    stage_sem,
    load_sem,
    d_send,
    d_recv,
    r_send,
    r_recv,
    *sems,
):
    band, row, chip, core = place(bands, rows)
    chips = bands // 2
    layers = param_ref.shape[0]
    nodes, width = node_buf.shape
    edges = edge_buf.shape[0]
    grids = grid_ref.shape[1]
    border = table.shape[2]
    table_rows = bands * border
    rows_dev = grads_ref.shape[1]
    weights = Weights(full_ref, stage, high, low, stage_sem)
    sibling = (chip * 2 + 1 - core, row)
    partners = [((chip + j) % chips * 2 + core, row) for j in range(1, chips)] + [sibling]
    own_rows = pl.ds(pl.multiple_of(row * rows_dev, rows_dev), rows_dev)

    def load(kind, layer):
        src = (before_ref, message_ref, edges_ref, agg_ref, inner_ref, update_ref, nodes_ref)[kind]
        dst = (before_buf, message_buf, edge_buf, agg_buf, inner_buf, update_buf, node_buf)[kind]
        return pltpu.make_async_copy(src.at[layer], dst, load_sem.at[kind])

    table_load = pltpu.make_async_copy(table_ref, table, load_sem.at[7])
    embed_buf = before_buf.at[pl.ds(0, grids)]
    fed_buf = agg_buf
    embed_load = pltpu.make_async_copy(embed_ref, embed_buf, load_sem.at[8])
    fed_load = pltpu.make_async_copy(fed_ref, fed_buf, load_sem.at[9])
    load(6, layers).start()
    table_load.start()
    for kind in range(6):
        load(kind, layers - 1).start()
    meet(partners)

    def to_sibling(e):
        return remote(table.at[1 - core], sib.at[e % 2], d_send.at[e], d_recv.at[e], sibling)

    def to_band(e, j):
        to = (chip + j) % chips
        return remote(
            table.at[core, to], land.at[e % 2, j - 1], r_send.at[e, j - 1], r_recv.at[e, j - 1], (to * 2 + core, row)
        )

    def give(e):
        to_sibling(e).wait()
        table[core] += sib[e % 2]
        for j in range(1, chips):
            to_band(e, j).start()

    def returned(e):
        total = table[core, chip]
        for j in range(1, chips):
            to_band(e, j).wait_recv()
            total = total + land[e % 2, j - 1]
        for j in range(1, chips):
            to_band(e, j).wait_send()
        return picked(hot(iota((nodes, border), 0) == index_ref[BORDER_ROW : BORDER_ROW + 1, pl.ds(0, border)]), total)

    def put_table(value_high, value_low, count):
        side_rows = chips * border
        for side in range(2):
            choice = pick_t[pl.ds(nodes + side * side_rows, side_rows), pl.ds(0, count)]
            table[side] = chosen(choice, value_high, value_low).reshape(chips, border, width)

    def grads_of(layer):
        return grads_buf.at[layer - 1] if layer > 0 else grads_ref

    reducers = [None] + [
        Spreader(
            bands,
            layer - 1,
            grads_of(layer),
            sib_grads,
            land_grads.at[layer - 1],
            landed_buf,
            total_ref.at[pl.ds(layer * each, each)],
            sems,
        )
        for layer in range(1, layers)
    ]

    def put_grad(layer, block, value):
        grads_of(layer)[block] = value

    def add_grad(layer, block, value):
        grads_of(layer)[block] += value

    index_t[...] = index_ref[...].T

    def choose_reads(at, size):
        line = iota((size, grids), 0) + at
        counts = jnp.zeros((size, grids), jnp.float32)
        for way in range(READ_ROW, index_ref.shape[0]):
            counts = counts + jnp.where(line == index_ref[way : way + 1, pl.ds(0, grids)], 1.0, 0.0)
        return counts.astype(jnp.bfloat16)

    def fill_reads(t, carry):
        at = pl.multiple_of(t * 64, 64)
        pick_t[pl.ds(at, 64), pl.ds(0, grids)] = choose_reads(at, 64)
        return carry

    lax.fori_loop(0, (nodes + table_rows) // 64, fill_reads, 0)

    def choose_gather(at, size):
        return hot(iota((size, nodes), 1) == index_t[pl.ds(at, size), RECV_ROW : RECV_ROW + 1])

    fill_rows(gather, choose_gather)
    load(6, layers).wait()
    table_load.wait()
    reads = edge_grad.at[pl.ds(0, grids)]
    own_high, own_low = pieces(node_buf[...])
    reads[...] = chosen(pick_t[pl.ds(0, nodes), pl.ds(0, grids)], own_high, own_low, TN)
    side_rows = chips * border
    for side in range(2):
        side_high, side_low = pieces(table[side].reshape(side_rows, width))
        choice = pick_t[pl.ds(nodes + side * side_rows, side_rows), pl.ds(0, grids)]
        reads[...] += chosen(choice, side_high, side_low, TN)
    load(6, layers - 1).start()
    weights.load((layers - 1) * each, (6, 4, 5, 3, 0, 1, 2))
    active = silu(reads[...])
    mask = index_ref[MASK_ROW : MASK_ROW + 1, pl.ds(0, grids)].astype(jnp.float32)
    missed = grid_ref[...] + product(dec_ref[...], active, NT) - target_ref[...]
    total = jnp.sum(jnp.sum(count_ref[:, :, 0:1, 0:1], axis=0), axis=0)
    masked = mask * missed
    loss = jnp.sum(column(masked * missed), axis=1, keepdims=True)
    grad = (2.0 / total) * masked
    channels = grid_ref.shape[0]
    encs = -(-channels // 8) * 8
    decs = encs
    decoder_at = encs + 8 + layers * 8
    small_ref[pl.ds(decoder_at, channels)] = product(grad, active)
    tail_rows = small_ref.shape[0] - decoder_at - decs
    small_ref[pl.ds(decoder_at + decs, tail_rows)] = jnp.broadcast_to(loss, (tail_rows, width))
    read_high, read_low = pieces(product(grad, dec_ref[...], TN) * silu_back(reads[...]))
    put_table(read_high, read_low, grids)
    to_sibling(0).start()
    node_grad[...] = chosen(pick_t[pl.ds(0, nodes), pl.ds(0, grids)], read_high, read_low)

    def choose(at, size):
        line = iota((size, edges), 0) + at
        sent = line == index_ref[SEND_ROW : SEND_ROW + 1]
        received = line == index_ref[RECV_ROW : RECV_ROW + 1] + (nodes + table_rows)
        return hot(jnp.logical_or(sent, received))

    fill_rows(pick_t, choose, 64)
    give(0)
    edge_grad[...] = jnp.zeros_like(edge_grad)
    node_grad[...] += returned(0)

    for depth in range(layers):
        layer = layers - 1 - depth
        e = depth + 1
        base = encs + 8 + layer * 8

        def put_param(index, value, base=base):
            small_ref[pl.ds(base + index, 1)] = value

        def add_param(index, value, base=base):
            small_ref[pl.ds(base + index, 1)] += value

        for kind in (3, 4, 5, 6):
            load(kind, layer).wait()
        if layer + 1 < layers:
            reducers[layer + 1].pair()
        if layer + 2 < layers:
            reducers[layer + 2].reduce()
        grad = node_grad[...]
        norm, scale = normed(update_buf[...])
        put_param(7, column(grad))
        put_param(6, column(grad * norm))
        grad = normed_back(grad * (1.0 + param_ref[layer, pl.ds(6, 1)]), norm, scale)
        put_param(5, column(grad))
        grad_high, grad_low = pieces(grad)
        put_grad(layer, 6, product(silu(inner_buf[:, own_rows]), grad, TN))
        grad = weights.times(grad_high, grad_low, 6, NT) * silu_back(inner_buf[...])
        put_param(4, column(grad))
        grad_high, grad_low = pieces(grad)
        put_grad(layer, 4, product(node_buf[:, own_rows], grad, TN))
        put_grad(layer, 5, product(agg_buf[:, own_rows], grad, TN))
        node_grad[...] += weights.times(grad_high, grad_low, 4, NT)
        agg_high, agg_low = pieces(weights.times(grad_high, grad_low, 5, NT))
        for kind in (0, 1, 2):
            load(kind, layer).wait()
        for index in range(4):
            put_param(index, jnp.zeros((1, width), jnp.float32))
        for block in (0, 3):
            put_grad(layer, block, jnp.zeros((rows_dev, width), jnp.float32))

        def edge_tile(t, carry):
            at = pl.ds(pl.multiple_of(t * tile, tile), tile)
            grad = edge_grad[at] + chosen(gather[at], agg_high, agg_low)
            edge_grad[at] = grad
            norm, scale = normed(message_buf[at])
            add_param(3, column(grad))
            add_param(2, column(grad * norm))
            grad = normed_back(grad * (1.0 + param_ref[layer, pl.ds(2, 1)]), norm, scale)
            add_param(1, column(grad))
            grad_high, grad_low = pieces(grad)
            add_grad(layer, 3, product(silu(before_buf[at, own_rows]), grad, TN))
            grad = weights.times(grad_high, grad_low, 3, NT) * silu_back(before_buf[at])
            add_param(0, column(grad))
            add_grad(layer, 0, product(edge_buf[at, own_rows], grad, TN))
            grad_high, grad_low = pieces(grad)
            part_high[at] = grad_high
            part_low[at] = grad_low
            return carry

        lax.fori_loop(0, edges // tile, edge_tile, 0)
        if layer > 0:
            for kind in range(6):
                load(kind, layer - 1).start()
        else:
            embed_load.start()
            fed_load.start()
        put_table(part_high[...], part_low[...], edges)
        to_sibling(e).start()
        sender = chosen(pick_t[pl.ds(0, nodes)], part_high[...], part_low[...])
        give(e)
        received = chosen(pick_t[pl.ds(nodes + table_rows, nodes)], part_high[...], part_low[...])

        def edge_back(t, carry):
            at = pl.ds(pl.multiple_of(t * tile, tile), tile)
            edge_grad[at] += weights.times(part_high[at], part_low[at], 0, NT)
            return carry

        lax.fori_loop(0, edges // tile, edge_back, 0)
        put_grad(layer, 2, product(node_buf[:, own_rows], received, TN))
        node_grad[...] += weights.apply(received, 2, NT)
        if layer > 0:
            weights.load((layer - 1) * each, (6, 4, 5, 3, 0))
        sender = sender + returned(e)
        put_grad(layer, 1, product(node_buf[:, own_rows], sender, TN))
        node_grad[...] += weights.apply(sender, 1, NT)
        if layer > 0:
            load(6, layer - 1).start()
            weights.load((layer - 1) * each, (1, 2))
            reducers[layer].start()

    reducers[1].reduce()
    embed_load.wait()
    fed_load.wait()
    norm, scale = normed(fed_buf[...])
    fed_grad = normed_back(node_grad[...], norm, scale)
    feed = hot(iota((grids, nodes), 1) == index_t[pl.ds(0, grids), FEED_ROW : FEED_ROW + 1])
    grad = picked(feed, fed_grad) * silu_back(embed_buf[...])
    small_ref[pl.ds(0, channels)] = product(grid_ref[...], grad)
    small_ref[pl.ds(encs, 8)] = jnp.zeros((8, width), jnp.float32)
    features[...] = edge_rows(edge_ref, 8)
    edge_t[...] = features[...].T

    def embed_back(t, carry):
        first = pl.multiple_of(t * 128, 128)
        at = pl.ds(first, 128)
        embed = embedded_edges(edge_t, enc_ref, channels, edge_ref.shape[0], first, 128)
        grad = edge_grad[at] * silu_back(embed)
        small_ref[pl.ds(encs, 8)] += product(features[:, at], grad)
        return carry

    lax.fori_loop(0, edges // 128, embed_back, 0)
    for layer in range(layers - 1, 0, -1):
        reducers[layer].relay()
    for layer in range(1, layers):
        reducers[layer].finish()


def backward(bands, rows, rim, rows_dev, inputs, saved):
    f32, bf16 = jnp.float32, jnp.bfloat16
    dma = pltpu.SemaphoreType.DMA
    grid, edge, index, decoder, params = inputs[0], inputs[2], inputs[3], inputs[5], inputs[6]
    layers = params.shape[0]
    full = saved[0]
    width = full.shape[2]
    each = full.shape[0] // layers
    edges, grids = edge.shape[1], grid.shape[1]
    nodes = NODE_DEV
    chips = bands // 2
    padded = -(-grid.shape[0] // 8) * 8
    small = padded + 8 + layers * 8 + padded + 8
    small = -(-small // (16 * OWNER_CHIPS)) * 16 * OWNER_CHIPS
    tile = edges
    node = pltpu.VMEM((nodes, width), f32)
    return pl.pallas_call(
        functools.partial(backward_kernel, bands, rows, each, tile),
        out_shape=(
            jax.ShapeDtypeStruct((each, rows_dev, width), f32),
            jax.ShapeDtypeStruct((small, width), f32),
            jax.ShapeDtypeStruct((full.shape[0], rows_dev, width), f32),
            jax.ShapeDtypeStruct((layers - 1, chips - 1, each, rows_dev // 8, width), f32),
        ),
        in_specs=[VMEM] * 7 + [ANY] * 11 + [VMEM],
        out_specs=[VMEM, VMEM, ANY, ANY],
        scratch_shapes=[
            pltpu.VMEM((edges, width), f32),
            pltpu.VMEM((edges, width), f32),
            pltpu.VMEM((edges, width), f32),
            node,
            node,
            node,
            node,
            pltpu.VMEM((edges, index.shape[0]), jnp.int32),
            pltpu.VMEM((edges, 8), f32),
            pltpu.VMEM((8, edges), f32),
            pltpu.VMEM((edges, width), f32),
            node,
            pltpu.VMEM((edges, width), bf16),
            pltpu.VMEM((edges, width), bf16),
            pltpu.VMEM((2 * nodes + bands * rim, edges), bf16),
            pltpu.VMEM((edges, nodes), bf16),
            pltpu.VMEM((each, width, width), bf16),
            pltpu.VMEM((each, width, width), bf16),
            pltpu.VMEM((2, width, width), f32),
            pltpu.VMEM((2, chips, rim, width), f32),
            pltpu.VMEM((2, chips, rim, width), f32),
            pltpu.VMEM((2, chips - 1, rim, width), f32),
            pltpu.VMEM((layers - 1, each, rows_dev, width), f32),
            pltpu.VMEM((each, rows_dev // 2, width), f32),
            pltpu.VMEM((each, rows_dev // 8, width), f32),
            dma((2,)),
            dma((10,)),
            dma((layers + 1,)),
            dma((layers + 1,)),
            dma((layers + 1, chips - 1)),
            dma((layers + 1, chips - 1)),
            ]
        + spreader_sems(layers - 1, chips),
        compiler_params=pltpu.CompilerParams(
            collective_id=2, has_side_effects=True, vmem_limit_bytes=VMEM_BYTES
        ),
        name="backward",
    )(*inputs, *saved)


def newton(matrix, result, first, count, arrive, leave, gram, poly, temp, later):
    gram[...] = jnp.zeros_like(gram)

    def add_gram(i, carry):
        arrive(first + i)
        block = matrix[first + i]
        gram[...] += product(block, block, TN)
        return carry

    lax.fori_loop(0, count, add_gram, 0)
    diagonal = iota(gram.shape, 0) == iota(gram.shape, 1)
    squares = column(jnp.where(diagonal, gram[...], 0.0))
    scale = 1.0 / (jnp.sqrt(jnp.sum(squares, axis=1, keepdims=True)) + 1e-07)
    gram[...] = gram[...] * (scale * scale)
    poly[...] = coef_b * gram[...] + coef_c * product(gram[...], gram[...])
    temp[...] = coef_a * gram[...] + product(gram[...], poly[...])
    gram[...] = coef_a * temp[...] + product(temp[...], poly[...])
    later[...] = coef_b * gram[...] + coef_c * product(gram[...], gram[...])
    temp[...] = coef_a * (poly[...] + later[...]) + product(poly[...], later[...])

    def last(i, carry):
        block = matrix[first + i] * scale
        result[first + i] = (coef_a * coef_a) * block + product(block, temp[...])
        leave(first + i)
        return carry

    lax.fori_loop(0, count, last, 0)


def late_slot(owner, slot):
    return owner in (0, 3) or (owner == 6 and slot == 0)


def tail_kernel(
    bands,
    rows,
    grads_ref,
    small_ref,
    mom_ref,
    given_ref,
    total_ref,
    ortho_ref,
    shared_ref,
    land,
    grads,
    sib,
    landed_buf,
    sib_small,
    part_small,
    land_small,
    held,
    matrix,
    result,
    back,
    gram,
    poly,
    temp,
    later,
    load_sem,
    landed_sem,
    m_pair,
    m_red_send,
    m_red_recv,
    m_out_send,
    m_out_recv,
    m_pass,
    m_keep,
    up_send,
    up_recv,
    down_send,
    down_recv,
    o_send,
    o_recv,
    p_send,
    p_recv,
    keep_sem,
    *sems,
):
    band, row, chip, core = place(bands, rows)
    chips = bands // 2
    rows_dev = held.shape[1]
    sibling = (chip * 2 + 1 - core, row)
    partners = [((chip + j) % chips * 2 + core, row) for j in range(1, chips)] + [sibling]
    partners += [(band, (row + j) % rows) for j in range(1, rows)]
    reducer = Reducer(bands, 0, 0, grads, sib.at[0], land, total_ref.at[pl.ds(0, grads.shape[0])], sems)
    grads[...] = grads_ref[...]

    def load(slot):
        return pltpu.make_async_copy(
            mom_ref.at[slot_block(band, slot)], held.at[slot], load_sem.at[slot]
        )

    owned = [band < (8, 7, 6)[slot] for slot in range(SLOTS)]
    third = band // 3
    last = [jnp.logical_and(band < 7, band % 3 == 0)]
    last += [jnp.logical_and(band < 6, band % 3 == 0)] * 2
    for slot in range(SLOTS):
        pl.when(owned[slot])(load(slot).start)
    meet(partners)

    small_pair = remote(small_ref.at[1 - core], sib_small, m_pair.at[0], m_pair.at[1], sibling)

    def small_to(at):
        step = (at - chip + chips) % chips
        return remote(
            part_small.at[at],
            land_small.at[step - 1],
            m_red_send.at[at],
            m_red_recv.at[step - 1],
            (at * 2 + core, row),
        )

    def small_out(at, j):
        home = shared_ref.at[core * OWNER_CHIPS + at]
        return remote(
            part_small.at[at],
            home,
            m_out_send.at[j - 1],
            m_out_recv.at[at],
            ((chip + j) % chips * 2 + core, row),
        )

    def small_across(at, of_core, local):
        home = shared_ref.at[of_core * OWNER_CHIPS + at]
        return remote(
            part_small.at[at] if local else home, home, m_pass.at[0, at], m_pass.at[1, at], sibling
        )

    def small_keep(at):
        return pltpu.make_async_copy(
            part_small.at[at], shared_ref.at[core * OWNER_CHIPS + at], m_keep
        )

    row_a = rows // 2 - 1 + core
    row_b = rows // 2 - core
    split_at = 3 - third

    def home(slot):
        return row_a + (slot + third) // 3 * (row_b - row_a)

    def rows_of(at_row):
        return pl.ds(pl.multiple_of(at_row * rows_dev, rows_dev), rows_dev)

    def up(slot, from_row):
        step = (from_row - home(slot) + rows) % rows
        return remote(
            held.at[slot],
            matrix.at[slot, rows_of(from_row)],
            up_send.at[slot],
            up_recv.at[slot, step],
            (band, home(slot)),
        )

    def down(slot, to_row):
        step = (to_row - home(slot) + rows) % rows
        return remote(
            result.at[slot, rows_of(to_row)],
            back.at[slot],
            down_send.at[slot, step],
            down_recv.at[slot],
            (band, to_row),
        )

    def momentum(slot, value):
        load(slot).wait()
        held[slot] = momentum_decay * held[slot] + value

        @pl.when(row == home(slot))
        def _():
            matrix[slot, rows_of(row)] = held[slot]

        @pl.when(row != home(slot))
        def _():
            up(slot, row).start()

    def solve(when):
        own_b = jnp.logical_and(row == row_b, jnp.logical_and(band > 2, band < 7))
        own_b = jnp.logical_and(own_b, jnp.logical_not(band == 3) if when == 0 else band == 3)
        own_a = jnp.logical_and(row == row_a, band < 8)
        own_a = jnp.logical_and(own_a, jnp.logical_not(last[0]) if when == 0 else last[0])

        @pl.when(jnp.logical_or(own_a, own_b))
        def _():
            second = (row - row_a) * (row_b - row_a)
            first = second * split_at
            count = (1 - second) * split_at + second

            def arrive(slot):
                for step in range(1, rows):
                    up(slot, (row + step) % rows).wait_recv()

            def leave(slot):
                for step in range(1, rows):
                    down(slot, (row + step) % rows).start()
                back[slot] = result[slot, rows_of(row)]

            newton(matrix, result, first, count, arrive, leave, gram, poly, temp, later)

    units = [
        (owner, slot)
        for owner in range(2 * OWNER_CHIPS)
        for slot in range(SLOTS)
        if slot_used(owner, slot)
    ]

    def target(owner, slot):
        return ortho_ref.at[slot_block(owner, slot)]

    def out(owner, slot, j):
        return remote(
            back.at[slot],
            target(owner, slot),
            o_send.at[slot, j - 1],
            o_recv.at[owner // 2, slot],
            ((chip + j) % chips * 2 + core, row),
        )

    def across(owner, slot, local):
        return remote(
            back.at[slot] if local else target(owner, slot),
            target(owner, slot),
            p_send.at[owner // 2, slot],
            p_recv.at[owner // 2, slot],
            sibling,
        )

    def keep(owner, slot):
        return pltpu.make_async_copy(back.at[slot], target(owner, slot), keep_sem.at[slot])

    def publish(when):
        for owner, slot in units:
            if late_slot(owner, slot) != (when == 1):
                continue

            @pl.when(band == owner)
            def _():
                @pl.when(row != home(slot))
                def _():
                    down(slot, row).wait_recv()

                for j in range(1, chips):
                    out(owner, slot, j).start()
                across(owner, slot, True).start()
                keep(owner, slot).start()

    def relay(when):
        for owner, slot in units:
            if late_slot(owner, slot) != (when == 1):
                continue

            @pl.when(jnp.logical_and(core == owner % 2, chip != owner // 2))
            def _():
                out(owner, slot, 1).wait_recv()
                across(owner, slot, False).start()

    reducer.start()
    small_pair.start()
    for slot in range(SLOTS):
        @pl.when(jnp.logical_and(owned[slot], jnp.logical_not(last[slot])))
        def _():
            ready = pltpu.make_async_copy(
                total_ref.at[slot_block(band, slot)], back.at[slot], load_sem.at[SLOTS + slot]
            )
            ready.start()
            ready.wait()
            momentum(slot, back[slot])

    reducer.pair()
    small_pair.wait()
    part_small[...] = small_ref[core] + sib_small[...]
    for at in range(OWNER_CHIPS):
        pl.when(chip != at)(small_to(at).start)
    solve(0)

    def take(slot, count, value):
        for n in range(count):
            momentum(slot + n, value[n])

    def load_landed(src, count):
        dst = landed_buf.at[pl.ds(0, count)]
        copy = pltpu.make_async_copy(src, dst, landed_sem)
        copy.start()
        copy.wait()
        return dst[...]

    reducer.reduce(take, load_landed)
    for at in range(OWNER_CHIPS):
        @pl.when(chip == at)
        def _():
            for j in range(1, chips):
                remote(
                    land_small.at[j - 1],
                    land_small.at[j - 1],
                    m_red_send.at[at],
                    m_red_recv.at[j - 1],
                    sibling,
                ).wait_recv()
                part_small[at] += land_small[j - 1]
            for j in range(1, chips):
                small_out(at, j).start()
            small_across(at, core, True).start()
            small_keep(at).start()

    def pass_on():
        reducer.relay()
        for at in range(OWNER_CHIPS):
            @pl.when(chip != at)
            def _():
                small_out(at, 1).wait_recv()
                small_across(at, core, False).start()

    pl.when(jnp.logical_not(last[0]))(pass_on)
    publish(0)
    solve(1)
    pl.when(last[0])(pass_on)
    publish(1)
    relay(0)
    relay(1)
    reducer.finish()
    for at in range(OWNER_CHIPS):
        small_across(at, core, False).wait_send()
        small_across(at, 1 - core, False).wait_recv()

        @pl.when(chip != at)
        def _():
            small_to(at).wait_send()

        @pl.when(chip == at)
        def _():
            for j in range(1, chips):
                small_out(at, j).wait_send()
            small_keep(at).wait()

    for owner, slot in units:
        @pl.when(core == owner % 2)
        def _():
            across(owner, slot, False).wait_send()

        @pl.when(core != owner % 2)
        def _():
            across(owner, slot, False).wait_recv()

        @pl.when(band == owner)
        def _():
            for j in range(1, chips):
                out(owner, slot, j).wait_send()
            keep(owner, slot).wait()

            @pl.when(row != home(slot))
            def _():
                up(slot, row).wait_send()

            @pl.when(row == home(slot))
            def _():
                for step in range(1, rows):
                    down(slot, (row + step) % rows).wait_send()


def tail(bands, rows, grads, small, momentum, given):
    blocks, rows_dev, width = momentum.shape
    each = grads.shape[0]
    chips = bands // 2
    chunk = small.shape[2]
    f32 = jnp.float32
    dma = pltpu.SemaphoreType.DMA
    square = pltpu.VMEM((width, width), f32)
    slots = pltpu.VMEM((SLOTS, rows_dev, width), f32)
    return pl.pallas_call(
        functools.partial(tail_kernel, bands, rows),
        out_shape=(
            jax.ShapeDtypeStruct(given.shape, f32),
            jax.ShapeDtypeStruct((blocks, rows_dev, width), f32),
            jax.ShapeDtypeStruct((2 * OWNER_CHIPS, chunk, width), f32),
            jax.ShapeDtypeStruct((1, chips - 1, SLOTS, rows_dev, width), f32),
        ),
        in_specs=[VMEM, VMEM, ANY, ANY],
        out_specs=[ANY, ANY, ANY, ANY],
        input_output_aliases={3: 0},
        scratch_shapes=[
            pltpu.VMEM((each, rows_dev, width), f32),
            pltpu.VMEM((1, each, rows_dev, width), f32),
            slots,
            pltpu.VMEM((OWNER_CHIPS, chunk, width), f32),
            pltpu.VMEM((OWNER_CHIPS, chunk, width), f32),
            pltpu.VMEM((chips - 1, chunk, width), f32),
            slots,
            pltpu.VMEM((SLOTS, width, width), f32),
            pltpu.VMEM((SLOTS, width, width), f32),
            slots,
            square,
            square,
            square,
            square,
            dma((2 * SLOTS,)),
            dma,
            dma((2,)),
            dma((OWNER_CHIPS,)),
            dma((chips - 1,)),
            dma((chips - 1,)),
            dma((OWNER_CHIPS,)),
            dma((2, OWNER_CHIPS)),
            dma,
            dma((SLOTS,)),
            dma((SLOTS, rows)),
            dma((SLOTS, rows)),
            dma((SLOTS,)),
            dma((SLOTS, chips - 1)),
            dma((OWNER_CHIPS, SLOTS)),
            dma((OWNER_CHIPS, SLOTS)),
            dma((OWNER_CHIPS, SLOTS)),
            dma((SLOTS,)),
        ]
        + reducer_sems(1, chips),
        compiler_params=pltpu.CompilerParams(
            collective_id=0, has_side_effects=True, vmem_limit_bytes=VMEM_BYTES
        ),
        name="tail",
    )(grads, small, momentum, given)


def finish_kernel(
    shapes,
    channels,
    edge_channels,
    w_ref,
    average_ref,
    mom_ref,
    total_ref,
    ortho_ref,
    small_ref,
    count_ref,
    enc_ref,
    enc_first_ref,
    enc_second_ref,
    dec_ref,
    dec_first_ref,
    dec_second_ref,
    param_ref,
    param_first_ref,
    param_second_ref,
    loss_ref,
    total_count_ref,
    new_w_ref,
    new_mom_ref,
    new_average_ref,
    enc_outs,
    dec_outs,
    param_outs,
):
    wide, params_at, decoder_at, loss_at = shapes
    step = pl.program_id(0)
    for n in range(w_ref.shape[0]):
        block = lax.rem(step * w_ref.shape[0] + n, len(block_scale))
        scale = jnp.where(block < 3, block_scale[0], jnp.where(block == 4, block_scale[4], 1.0))
        scale = jnp.where(block == 5, block_scale[5], scale)
        fresh = w_ref[n] * (1.0 - muon_rate * weight_decay) - (muon_rate * scale) * ortho_ref[n]
        new_w_ref[n] = fresh
        new_average_ref[n] = average_decay * average_ref[n] + (1.0 - average_decay) * fresh
        new_mom_ref[n] = momentum_decay * mom_ref[n] + total_ref[n]

    def put(outs, at, values):
        for ref, value in zip(outs, values):
            ref[at] = value

    @pl.when(step == 0)
    def _():
        for at, grad in (
            (pl.ds(0, channels), small_ref[pl.ds(0, channels)]),
            (pl.ds(channels, edge_channels), small_ref[pl.ds(wide, edge_channels)]),
        ):
            put(enc_outs, at, adam_update(enc_ref[at], enc_first_ref[at], enc_second_ref[at], grad, adam_rate))
        grad = small_ref[pl.ds(decoder_at, channels)]
        put(dec_outs, ..., adam_update(dec_ref[...], dec_first_ref[...], dec_second_ref[...], grad, adam_rate))
        for layer in range(param_ref.shape[0]):
            grad = small_ref[pl.ds(params_at + layer * 8, 8)]
            put(
                param_outs,
                layer,
                adam_update(param_ref[layer], param_first_ref[layer], param_second_ref[layer], grad, param_rate),
            )
        loss_ref[...] = small_ref[pl.ds(loss_at, 1), 0:1]
        total_count_ref[...] = jnp.sum(jnp.sum(count_ref[:, :, 0:1, 0:1], axis=0), axis=0)


def finish(shapes, edge_channels, blocks, small, counts, encoder, decoder, params):
    f32 = jnp.float32
    channels = decoder[0].shape[0]
    big = blocks[0]
    tiled = pl.BlockSpec((len(block_scale),) + big.shape[1:], lambda i: (i, 0, 0))

    def whole(value):
        return pl.BlockSpec(value.shape, lambda i: (0,) * value.ndim)

    def like(value):
        return jax.ShapeDtypeStruct(value.shape, f32)

    scalar = jax.ShapeDtypeStruct((1, 1), f32)
    return pl.pallas_call(
        functools.partial(finish_kernel, shapes, channels, edge_channels),
        grid=(big.shape[0] // len(block_scale),),
        out_shape=(
            scalar,
            scalar,
            like(big),
            like(big),
            like(big),
            (like(encoder[0]),) * 3,
            (like(decoder[0]),) * 3,
            (like(params[0]),) * 3,
        ),
        in_specs=[tiled] * 5 + [whole(value) for value in (small, counts, *encoder, *decoder, *params)],
        out_specs=(
            whole(scalar),
            whole(scalar),
            tiled,
            tiled,
            tiled,
            (whole(encoder[0]),) * 3,
            (whole(decoder[0]),) * 3,
            (whole(params[0]),) * 3,
        ),
        compiler_params=pltpu.CompilerParams(vmem_limit_bytes=VMEM_BYTES),
        name="finish",
    )(*blocks, small, counts, *encoder, *decoder, *params)


def adam_update(values, first, second, gradient, rate):
    first = beta_one * first + (1.0 - beta_one) * gradient
    second = beta_two * second + (1.0 - beta_two) * gradient * gradient
    corrected = (
        first / (1.0 - beta_one**STEP) / (jnp.sqrt(second / (1.0 - beta_two**STEP)) + adam_eps)
    )
    return (first, second, values * (1.0 - rate * weight_decay) - rate * corrected)


def body(
    grid_input,
    grid_target,
    edge_input,
    senders,
    receivers,
    border_nodes,
    grid_to_mesh,
    mesh_to_grid,
    loss_mask,
    encoder_weights,
    encoder_first,
    encoder_second,
    processor_weights,
    processor_momentum,
    processor_average,
    norm_params,
    norm_first,
    norm_second,
    decoder_weights,
    decoder_first,
    decoder_second,
):
    bands, rows = lax.axis_size("band"), lax.axis_size("row")
    layers, blocks, rows_dev, width = processor_weights.shape
    channels = grid_input.shape[1]
    edge_channels = edge_input.shape[1]
    wide = -(-channels // 8) * 8
    grids, rim = grid_input.shape[0], border_nodes.shape[0]
    reads = mesh_to_grid.reshape(grids, -1).T
    indices = (jnp.stack([senders, receivers]),) + tuple(
        value[None, :] for value in (border_nodes, grid_to_mesh, loss_mask)
    ) + (reads,)
    flat_weights = processor_weights.reshape(layers * blocks, rows_dev, width)
    *saved, index = forward(
        bands,
        rows,
        grid_input.T,
        edge_input.T,
        indices,
        flat_weights,
        encoder_weights,
        norm_params,
    )
    inputs = (
        grid_input.T,
        grid_target.T,
        edge_input.T,
        index,
        encoder_weights,
        decoder_weights.T,
        norm_params,
    )
    grads, small, total, _ = backward(bands, rows, rim, rows_dev, inputs, saved)
    flat_momentum = processor_momentum.reshape(layers * blocks, rows_dev, width)
    total, ortho, small, _ = tail(
        bands,
        rows,
        grads,
        small.reshape(2, OWNER_CHIPS, -1, width),
        flat_momentum,
        total,
    )
    params_at = wide + 8
    decoder_at = params_at + layers * 8
    loss_total, mask_count, next_weights, next_momentum, next_average, encoder, decoder, params = finish(
        (wide, params_at, decoder_at, decoder_at + wide),
        edge_channels,
        (flat_weights, processor_average.reshape(flat_momentum.shape), flat_momentum, total, ortho),
        small.reshape(-1, width),
        saved[-1],
        (encoder_weights, encoder_first, encoder_second),
        (decoder_weights.T, decoder_first.T, decoder_second.T),
        (norm_params, norm_first, norm_second),
    )
    encoder_moment, encoder_square, encoder_values = encoder
    decoder_moment, decoder_square, decoder_values = (value.T for value in decoder)
    param_moment, param_square, param_values = params
    loss_total, mask_count = loss_total[0, 0], mask_count[0, 0]
    next_weights, next_momentum, next_average = (
        value.reshape(processor_weights.shape) for value in (next_weights, next_momentum, next_average)
    )
    return (
        loss_total,
        mask_count,
        next_weights,
        next_momentum,
        next_average,
        param_moment,
        param_square,
        param_values,
        encoder_moment,
        encoder_square,
        encoder_values,
        decoder_moment,
        decoder_square,
        decoder_values,
    )


def solution(mesh):
    return jax.shard_map(
        body,
        mesh=mesh,
        in_specs=(
            P("band", None),
            P("band", None),
            P("band", None),
            P("band"),
            P("band"),
            P("band"),
            P("band"),
            P("band"),
            P("band"),
            P(),
            P(),
            P(),
            P(None, None, "row", None),
            P(None, None, "row", None),
            P(None, None, "row", None),
            P(),
            P(),
            P(),
            P(),
            P(),
            P(),
        ),
        out_specs=(
            P(),
            P(),
            P(None, None, "row", None),
            P(None, None, "row", None),
            P(None, None, "row", None),
            P(),
            P(),
            P(),
            P(),
            P(),
            P(),
            P(),
            P(),
            P(),
        ),
        check_vma=False,
    )
```
